256 devices in a mesh: node: 16 (over x, y), feat: 16 (over z, core).
Axes of the slice: x: 4, y: 4, z: 8, core: 2. Of those that a mesh axis runs over, the one named last changes fastest.
Arguments:
- features: bfloat16 [1024, 131072], P('feat', 'node'), may hold values from -6 to 6
- tile_values: bfloat16 [1024, 2, 128, 128], P('node'), may hold values from -0.375 to 0.375
- tile_cols: int32 [1024, 2], P('node'), may hold values from 0 to 1023, as said below
- tile_count: int32 [1024], P('node'), may hold values from 1 to 2, as said below
- w_self: bfloat16 [1024, 1024], replicated, may hold values from -0.1875 to 0.1875
- w_neigh: bfloat16 [1024, 1024], replicated, may hold values from -0.1875 to 0.1875
- cotangent: bfloat16 [1024, 131072], P(None, ('node', 'feat')), may hold values from -6 to 6
Outputs:
- hidden: bfloat16 [1024, 131072], P(None, ('node', 'feat'))
- grad_features: bfloat16 [1024, 131072], P('feat', 'node')
- grad_w_neigh: float32 [1024, 1024], P(('node', 'feat'))
The draws below stay inside these ranges and needn't reach their ends.
Inputs may be any that keep to these rules, and one draw needn't show every extreme that they name: `tile_cols`: slot 0 of row block r names block r itself; every other slot names a block of the row block's own partition of 64 blocks or of the partition just before or after it. `tile_count`: the first row block of every partition has all 2 slots live.
All inputs are finite; a program needn't handle non-finite values.
Results may differ from the reference program's by a relative error of at most 0.0059.
Values may be sent and summed in bfloat16 or wider, within the bound.
No kernel may reach another device: no remote copies, remote signals or barrier semaphores. Data moves between devices by JAX's collectives and lax.ppermute only.
A program may use at most 128 MiB of HBM per device.

```python
import jax
import jax.numpy as jnp
from jax import lax

D = 1024
TILE = 128
K = 2
BLOCK_DEV = 64
BLOCKS = 1024
NODES = 131072
N_NODE = 16


def draw_tile_cols(key, part):
    key = jax.random.fold_in(key, 11)
    rows = jnp.arange(BLOCKS, dtype=jnp.int32)
    home = rows // BLOCK_DEV
    low = jnp.maximum(home - 1, 0) * BLOCK_DEV
    high = jnp.minimum(home + 2, N_NODE) * BLOCK_DEV
    picks = jax.random.randint(key, (BLOCKS, K), 0, 1 << 20)
    cols = low[:, None] + picks % (high - low)[:, None]
    return cols.at[:, 0].set(rows).astype(jnp.int32)


def draw_tile_count(key, part):
    key = jax.random.fold_in(key, 12)
    first, second = jax.random.split(key)
    level = jax.random.randint(first, (N_NODE,), 1, K + 1)
    jitter = jax.random.randint(second, (BLOCKS,), -1, 2)
    rows = jnp.arange(BLOCKS, dtype=jnp.int32)
    count = jnp.clip(level[rows // BLOCK_DEV] + jitter, 1, K)
    return jnp.where(rows % BLOCK_DEV == 0, K, count).astype(jnp.int32)


def level_of(stream_key, extent, shards, smallest, top_value):
    def one(dim, parts):
        steps = jax.random.uniform(jax.random.fold_in(jax.random.fold_in(stream_key, 6), dim), (parts,), jnp.float32, smallest / len(shards), top_value / len(shards))
        return jnp.repeat(jnp.exp(steps), extent[dim] // parts).reshape((-1,) + (1,) * (len(extent) - dim - 1))

    loudness = one(*shards[0])
    for cut in shards[1:]:
        loudness = loudness * one(*cut)
    return loudness


def centred(key, shape, deviation, limit, cuts=(), kind=jnp.bfloat16):
    loudness = level_of(key, shape, cuts, -0.22, 0.18) if cuts else 1.0
    values = jax.random.normal(key, shape, jnp.float32) * deviation * loudness
    return jnp.minimum(jnp.maximum(values, -limit), limit).astype(kind)


def setup_inputs(seed: int = 0) -> dict:
    splits = jax.random.split(jax.random.key(seed), 8)
    features = centred(splits[0], (D, NODES), 1.0, 6.0, ((0, 16), (1, 16)))
    tile_values = centred(splits[1], (BLOCKS, K, TILE, TILE), (TILE * K) ** -0.5, 0.375, ((0, 16),))
    tile_cols = draw_tile_cols(jax.random.fold_in(splits[7], 71), 0)
    tile_count = draw_tile_count(jax.random.fold_in(splits[7], 71), 0)
    w_self = centred(splits[4], (D, D), D ** -0.5, 0.1875)
    w_neigh = centred(splits[5], (D, D), D ** -0.5, 0.1875)
    cotangent = centred(splits[6], (D, NODES), 1.0, 6.0, ((1, 256),))
    return {"features": features, "tile_values": tile_values, "tile_cols": tile_cols, "tile_count": tile_count, "w_self": w_self, "w_neigh": w_neigh, "cotangent": cotangent}


def reference(features, tile_values, tile_cols, tile_count, w_self, w_neigh, cotangent):
    blocks = features.reshape(D, BLOCKS, TILE)
    live = jnp.arange(K, dtype=jnp.int32)[None, :] < tile_count[:, None]
    masked = jnp.where(live[:, :, None, None], tile_values, jnp.zeros_like(tile_values))

    def forward_part(part):
        start = (part * BLOCK_DEV).astype(jnp.int32)
        cols = lax.dynamic_slice_in_dim(tile_cols, start, BLOCK_DEV, 0)
        tiles = lax.dynamic_slice_in_dim(masked, start, BLOCK_DEV, 0)
        picked = blocks[:, cols, :].astype(jnp.float32)
        return jnp.einsum('fbkj,bkji->fbi', picked, tiles.astype(jnp.float32))

    pieces = lax.map(forward_part, jnp.arange(N_NODE, dtype=jnp.int32))
    agg = jnp.transpose(pieces, (1, 0, 2, 3)).reshape(D, NODES).astype(jnp.bfloat16)
    pre = jnp.dot(w_self, features, preferred_element_type=jnp.float32) + jnp.dot(w_neigh, agg, preferred_element_type=jnp.float32)
    sig = jax.nn.sigmoid(pre)
    hidden = (pre * sig).astype(jnp.bfloat16)
    dpre = (cotangent.astype(jnp.float32) * sig * (1.0 + pre * (1.0 - sig))).astype(jnp.bfloat16)
    rows_dims = (((1,), (1,)), ((), ()))
    grad_w_neigh = lax.dot_general(dpre, agg, rows_dims, preferred_element_type=jnp.float32)
    out_dims = (((0,), (0,)), ((), ()))
    dself = lax.dot_general(w_self, dpre, out_dims, preferred_element_type=jnp.float32).astype(jnp.bfloat16)
    dagg = lax.dot_general(w_neigh, dpre, out_dims, preferred_element_type=jnp.float32).astype(jnp.bfloat16)
    dagg_blocks = dagg.reshape(D, BLOCKS, TILE)

    def backward_part(total, part):
        start = (part * BLOCK_DEV).astype(jnp.int32)
        cols = lax.dynamic_slice_in_dim(tile_cols, start, BLOCK_DEV, 0)
        tiles = lax.dynamic_slice_in_dim(masked, start, BLOCK_DEV, 0)
        own = lax.dynamic_slice_in_dim(dagg_blocks, start, BLOCK_DEV, 1).astype(jnp.float32)
        contrib = jnp.einsum('fbi,bkji->fbkj', own, tiles.astype(jnp.float32))
        return total.at[:, cols, :].add(contrib), None

    spread, unused = lax.scan(backward_part, jnp.zeros((D, BLOCKS, TILE), jnp.float32), jnp.arange(N_NODE, dtype=jnp.int32))
    grad_features = (dself.astype(jnp.float32) + spread.reshape(D, NODES)).astype(jnp.bfloat16)
    return hidden, grad_features, grad_w_neigh
```

```python
import functools

import jax
import jax.numpy as jnp
from jax import lax
from jax.experimental import pallas as pl
from jax.experimental.pallas import tpu as pltpu
from jax.sharding import PartitionSpec as P

F32 = jnp.float32
BF16 = jnp.bfloat16
NT = (((1,), (1,)), ((), ()))
NN = (((1,), (0,)), ((), ()))
MIB = 1 << 20


def dot(a, b, dims=NN):
    return lax.dot_general(a, b, dims, preferred_element_type=F32)


def params(mib):
    return pltpu.CompilerParams(
        dimension_semantics=("arbitrary",), vmem_limit_bytes=mib * MIB
    )


def split_kernel(x_ref, out_ref):
    out_ref[0] = x_ref[...]


def split_columns(x, groups):
    rows, columns = x.shape
    width = columns // groups
    return pl.pallas_call(
        split_kernel,
        grid=(groups,),
        in_specs=[pl.BlockSpec((rows, width), lambda g: (0, g))],
        out_specs=pl.BlockSpec((1, rows, width), lambda g: (g, 0, 0)),
        out_shape=jax.ShapeDtypeStruct((groups, rows, width), x.dtype),
        compiler_params=params(16),
    )(x)


def agg_kernel(col_ref, live_ref, before, own, after, tiles_ref, out_ref, window, sems):
    step = pl.program_id(0)
    span = own.shape[1]
    tile = tiles_ref.shape[-1]
    blocks = span // tile
    group = tiles_ref.shape[0]
    per = out_ref.shape[2] // tile

    @pl.when(step == 0)
    def _():
        copies = [
            pltpu.make_async_copy(part, window.at[:, i * span : (i + 1) * span], sems.at[i])
            for i, part in enumerate((before, own, after))
        ]
        for copy in copies:
            copy.start()
        for copy in copies:
            copy.wait()

    for b in range(group):
        r = step * group + b
        here = pl.multiple_of((blocks + r) * tile, tile)
        there = pl.multiple_of(col_ref[r] * tile, tile)
        first = dot(window[:, pl.ds(here, tile)], tiles_ref[b, 0])
        second = dot(window[:, pl.ds(there, tile)], tiles_ref[b, 1])
        total = first + jnp.where(live_ref[r] > 0, second, 0.0)
        out_ref[b // per, :, (b % per) * tile : (b % per + 1) * tile] = total.astype(BF16)


def aggregate(col, live, before, own, after, tiles, groups):
    rows, span = own.shape
    blocks, slots, tile, _ = tiles.shape
    width = span // groups
    per = width // tile
    group = 2 * per
    anywhere = pl.BlockSpec(memory_space=pl.ANY)
    smem = pl.BlockSpec(memory_space=pltpu.SMEM)
    return pl.pallas_call(
        agg_kernel,
        grid=(blocks // group,),
        in_specs=[smem, smem, anywhere, anywhere, anywhere]
        + [pl.BlockSpec((group, slots, tile, tile), lambda g: (g, 0, 0, 0))],
        out_specs=pl.BlockSpec((group // per, rows, width), lambda g: (g, 0, 0)),
        out_shape=jax.ShapeDtypeStruct((groups, rows, width), BF16),
        scratch_shapes=[pltpu.VMEM((rows, 3 * span), BF16), pltpu.SemaphoreType.DMA((3,))],
        compiler_params=params(24),
        cost_estimate=pl.CostEstimate(
            flops=4 * rows * span * tile, bytes_accessed=9 * MIB, transcendentals=0
        ),
    )(col, live, before, own, after, tiles)


def spread_kernel(col_ref, live_ref, dagg_ref, tiles_ref, before_ref, own_ref, after_ref, acc):
    step = pl.program_id(0)
    tile = tiles_ref.shape[-1]
    blocks = own_ref.shape[0]
    group = tiles_ref.shape[0]
    per = dagg_ref.shape[2] // tile

    @pl.when(step == 0)
    def _():
        def clear(i, carry):
            acc[i] = jnp.zeros(acc.shape[1:], F32)
            return carry

        lax.fori_loop(0, acc.shape[0], clear, 0, unroll=8)

    for b in range(group):
        r = step * group + b
        grad = dagg_ref[b // per, :, (b % per) * tile : (b % per + 1) * tile]
        first = dot(grad, tiles_ref[b, 0], NT)
        second = dot(grad, tiles_ref[b, 1], NT)
        acc[blocks + r] += first
        acc[col_ref[r]] += jnp.where(live_ref[r] > 0, second, 0.0)

    @pl.when(step == pl.num_programs(0) - 1)
    def _():
        def store(i, carry):
            before_ref[i] = acc[i].astype(BF16)
            own_ref[i] = acc[blocks + i]
            after_ref[i] = acc[2 * blocks + i].astype(BF16)
            return carry

        lax.fori_loop(0, blocks, store, 0, unroll=4)


def spread(col, live, dagg, tiles):
    groups, rows, width = dagg.shape
    blocks, slots, tile, _ = tiles.shape
    per = width // tile
    group = 2 * per
    smem = pl.BlockSpec(memory_space=pltpu.SMEM)
    whole = pl.BlockSpec((blocks, rows, tile), lambda g: (0, 0, 0))
    shape = (blocks, rows, tile)
    return pl.pallas_call(
        spread_kernel,
        grid=(blocks // group,),
        in_specs=[
            smem,
            smem,
            pl.BlockSpec((group // per, rows, width), lambda g: (g, 0, 0)),
            pl.BlockSpec((group, slots, tile, tile), lambda g: (g, 0, 0, 0)),
        ],
        out_specs=[whole, whole, whole],
        out_shape=[
            jax.ShapeDtypeStruct(shape, BF16),
            jax.ShapeDtypeStruct(shape, F32),
            jax.ShapeDtypeStruct(shape, BF16),
        ],
        scratch_shapes=[pltpu.VMEM((3 * blocks, rows, tile), F32)],
        compiler_params=params(32),
        cost_estimate=pl.CostEstimate(
            flops=4 * rows * blocks * tile * tile, bytes_accessed=9 * MIB, transcendentals=0
        ),
    )(col, live, dagg, tiles)


def dense_kernel(chunk, w_self, w_neigh, w_back, x_ref, agg_ref, cot_ref, hidden, dpre, dagg):
    size = w_self.shape[0]

    def forward(i, carry):
        rows = pl.ds(pl.multiple_of(i * chunk, chunk), chunk)
        pre = dot(w_self[rows, :], x_ref[...]) + dot(w_neigh[rows, :], agg_ref[...])
        sig = jax.nn.sigmoid(pre)
        hidden[rows, :] = (pre * sig).astype(BF16)
        slope = sig * (1.0 + pre * (1.0 - sig))
        dpre[rows, :] = (cot_ref[rows, :].astype(F32) * slope).astype(BF16)
        return carry

    lax.fori_loop(0, size // chunk, forward, 0)

    def backward(i, carry):
        rows = pl.ds(pl.multiple_of(i * chunk, chunk), chunk)
        dagg[rows, :] = dot(w_back[rows, :], dpre[...]).astype(BF16)
        return carry

    lax.fori_loop(0, size // chunk, backward, 0)


def dense(w_self, w_neigh, w_back, x_rows, agg_rows, cot):
    size, width = x_rows.shape
    vmem = pl.BlockSpec(memory_space=pltpu.VMEM)
    out = jax.ShapeDtypeStruct((size, width), BF16)
    return pl.pallas_call(
        functools.partial(dense_kernel, 256),
        in_specs=[vmem] * 6,
        out_specs=[vmem] * 3,
        out_shape=[out] * 3,
        compiler_params=pltpu.CompilerParams(vmem_limit_bytes=24 * MIB),
        cost_estimate=pl.CostEstimate(
            flops=6 * size * size * width, bytes_accessed=12 * MIB, transcendentals=size * width
        ),
    )(w_self, w_neigh, w_back, x_rows, agg_rows, cot)


def late_kernel(chunk, w_back, dpre, ordered, agg_ref, dself, grad):
    def step(i, carry):
        rows = pl.ds(pl.multiple_of(i * chunk, chunk), chunk)
        dself[rows, :] = dot(w_back[rows, :], dpre[...]).astype(BF16)
        return carry

    lax.fori_loop(0, dself.shape[0] // chunk, step, 0)

    def weight(i, carry):
        rows = pl.ds(pl.multiple_of(i * chunk, chunk), chunk)
        grad[rows, :] = dot(ordered[rows, :], agg_ref[...], NT).astype(BF16)
        return carry

    lax.fori_loop(0, grad.shape[0] // chunk, weight, 0)


def late(w_back, dpre, ordered, agg_rows):
    size, width = dpre.shape
    vmem = pl.BlockSpec(memory_space=pltpu.VMEM)
    return pl.pallas_call(
        functools.partial(late_kernel, 256),
        in_specs=[vmem] * 4,
        out_specs=[vmem] * 2,
        out_shape=[
            jax.ShapeDtypeStruct((size, width), BF16),
            jax.ShapeDtypeStruct((size, size), BF16),
        ],
        compiler_params=pltpu.CompilerParams(vmem_limit_bytes=24 * MIB),
        cost_estimate=pl.CostEstimate(
            flops=4 * size * size * width, bytes_accessed=7 * MIB, transcendentals=0
        ),
    )(w_back, dpre, ordered, agg_rows)


def final_kernel(own_ref, before_ref, after_ref, dself_ref, out_ref):
    tile = own_ref.shape[2]
    for b in range(own_ref.shape[0]):
        columns = slice(b * tile, (b + 1) * tile)
        total = own_ref[b] + before_ref[b].astype(F32) + after_ref[b].astype(F32)
        out_ref[:, columns] = (dself_ref[0, :, columns].astype(F32) + total).astype(BF16)


def finish(own, before, after, dself):
    groups, rows, width = dself.shape
    blocks, _, tile = own.shape
    per = width // tile
    part = pl.BlockSpec((per, rows, tile), lambda g: (g, 0, 0))
    return pl.pallas_call(
        final_kernel,
        grid=(groups,),
        in_specs=[part, part, part, pl.BlockSpec((1, rows, width), lambda g: (g, 0, 0))],
        out_specs=pl.BlockSpec((rows, width), lambda g: (0, g)),
        out_shape=jax.ShapeDtypeStruct((rows, groups * width), BF16),
        compiler_params=params(16),
    )(own, before, after, dself)


def shifted(value, axis, steps):
    count = lax.axis_size(axis)
    first, last = max(0, -steps), min(count, count - steps)
    return lax.ppermute(value, axis, [(source, source + steps) for source in range(first, last)])


def exchange(value, axis):
    return lax.all_to_all(value, axis, split_axis=0, concat_axis=0, tiled=True)


SIDE = 4
CORES = 2


def by_owner(rows):
    size, width = rows.shape
    rows = rows.reshape(SIDE, SIDE, -1, CORES, size // (256), width)
    return rows.transpose(3, 1, 0, 2, 4, 5).reshape(size, width)


def exchange_sum(value, axis, count, index, partner):
    pieces = value.reshape(count, -1, value.shape[-1])
    total = lax.dynamic_index_in_dim(pieces, index, 0, keepdims=False).astype(F32)
    for step in range(1, count):
        target = (index + step) % count
        piece = lax.dynamic_index_in_dim(pieces, target, 0, keepdims=False).astype(BF16)
        pairs = [(i, partner(i, step)) for i in range(lax.axis_size(axis))]
        total = total + lax.ppermute(piece, axis, pairs).astype(F32)
    return total


def summed_over_all(value):
    feat, node = lax.axis_index("feat"), lax.axis_index("node")
    value = exchange_sum(value, "feat", CORES, feat % CORES, lambda i, s: i ^ 1)
    y = lambda i, s: i // SIDE * SIDE + (i + s) % SIDE
    value = exchange_sum(value, "node", SIDE, node % SIDE, y)
    x = lambda i, s: (i + s * SIDE) % (SIDE * SIDE)
    value = exchange_sum(value, "node", SIDE, node // SIDE, x)
    groups = lax.axis_size("feat")
    same = [[z * CORES + c for z in range(groups // CORES)] for c in range(CORES)]
    return lax.psum_scatter(value, "feat", scatter_dimension=0, tiled=True, axis_index_groups=same)


def local(features, tile_values, tile_cols, tile_count, w_self, w_neigh, cotangent):
    feat_dev, node_dev = features.shape
    tile = tile_values.shape[-1]
    block_count = node_dev // tile
    groups = lax.axis_size("feat")
    size = w_self.shape[0]
    part = lax.axis_index("node")
    col = tile_cols[:, 1] - (part - 1) * block_count
    live = (tile_count > 1).astype(jnp.int32)

    before = shifted(features, "node", 1)
    after = shifted(features, "node", -1)
    x_rows = exchange(split_columns(features, groups), "feat").reshape(size, -1)
    agg = aggregate(col, live, before, features, after, tile_values, groups)
    agg_rows = exchange(agg, "feat").reshape(size, -1)
    hidden, dpre, dagg = dense(w_self, w_neigh, w_neigh.T, x_rows, agg_rows, cotangent)
    dagg_cols = exchange(dagg.reshape(groups, feat_dev, -1), "feat")
    dself, part_neigh = late(w_self.T, dpre, by_owner(dpre), agg_rows)
    dself_cols = exchange(dself.reshape(groups, feat_dev, -1), "feat")

    grad_w_neigh = summed_over_all(part_neigh)

    to_before, own, to_after = spread(col, live, dagg_cols, tile_values)
    from_after = shifted(to_before, "node", -1)
    from_before = shifted(to_after, "node", 1)
    grad_features = finish(own, from_before, from_after, dself_cols)
    return (hidden, grad_features, grad_w_neigh)


def solution(mesh):
    placed = (
        P("feat", "node"),
        P("node", None, None, None),
        P("node", None),
        P("node"),
        P(),
        P(),
        P(None, ("node", "feat")),
    )
    return jax.shard_map(
        local,
        mesh=mesh,
        in_specs=placed,
        out_specs=(P(None, ("node", "feat")), P("feat", "node"), P(("node", "feat"), None)),
        check_vma=False,
    )
```

```python
import functools

import jax
import jax.numpy as jnp
from jax import lax
from jax.experimental import pallas as pl
from jax.experimental.pallas import tpu as pltpu
from jax.sharding import PartitionSpec as P

F32 = jnp.float32
BF16 = jnp.bfloat16
NT = (((1,), (1,)), ((), ()))
NN = (((1,), (0,)), ((), ()))
MIB = 1 << 20


def dot(a, b, dims=NN):
    return lax.dot_general(a, b, dims, preferred_element_type=F32)


def params(mib):
    return pltpu.CompilerParams(
        dimension_semantics=("arbitrary",), vmem_limit_bytes=mib * MIB
    )


def split_kernel(x_ref, out_ref):
    width = out_ref.shape[2]
    for g in range(out_ref.shape[0]):
        out_ref[g] = x_ref[:, g * width : (g + 1) * width]


def split_columns(x, groups):
    rows, columns = x.shape
    width = columns // groups
    steps = 4
    return pl.pallas_call(
        split_kernel,
        grid=(steps,),
        in_specs=[pl.BlockSpec((rows, columns // steps), lambda g: (0, g))],
        out_specs=pl.BlockSpec((groups // steps, rows, width), lambda g: (g, 0, 0)),
        out_shape=jax.ShapeDtypeStruct((groups, rows, width), x.dtype),
        compiler_params=params(56),
    )(x)


def agg_kernel(col_ref, live_ref, before, own, after, tiles_ref, out_ref, window, sems):
    step = pl.program_id(0)
    span = own.shape[1]
    tile = tiles_ref.shape[-1]
    blocks = span // tile
    group = tiles_ref.shape[0]
    per = out_ref.shape[2] // tile

    @pl.when(step == 0)
    def _():
        copies = [
            pltpu.make_async_copy(part, window.at[:, i * span : (i + 1) * span], sems.at[i])
            for i, part in enumerate((before, own, after))
        ]
        for copy in copies:
            copy.start()
        for copy in copies:
            copy.wait()

    for b in range(group):
        r = step * group + b
        here = pl.multiple_of((blocks + r) * tile, tile)
        there = pl.multiple_of(col_ref[r] * tile, tile)
        first = dot(window[:, pl.ds(here, tile)], tiles_ref[b, 0])
        second = dot(window[:, pl.ds(there, tile)], tiles_ref[b, 1])
        total = first + jnp.where(live_ref[r] > 0, second, 0.0)
        out_ref[b // per, :, (b % per) * tile : (b % per + 1) * tile] = total.astype(BF16)


def aggregate(col, live, before, own, after, tiles, groups):
    rows, span = own.shape
    blocks, slots, tile, _ = tiles.shape
    width = span // groups
    per = width // tile
    group = 4 * per
    anywhere = pl.BlockSpec(memory_space=pl.ANY)
    smem = pl.BlockSpec(memory_space=pltpu.SMEM)
    return pl.pallas_call(
        agg_kernel,
        grid=(blocks // group,),
        in_specs=[smem, smem, anywhere, anywhere, anywhere]
        + [pl.BlockSpec((group, slots, tile, tile), lambda g: (g, 0, 0, 0))],
        out_specs=pl.BlockSpec((group // per, rows, width), lambda g: (g, 0, 0)),
        out_shape=jax.ShapeDtypeStruct((groups, rows, width), BF16),
        scratch_shapes=[pltpu.VMEM((rows, 3 * span), BF16), pltpu.SemaphoreType.DMA((3,))],
        compiler_params=params(56),
        cost_estimate=pl.CostEstimate(
            flops=4 * rows * span * tile, bytes_accessed=9 * MIB, transcendentals=0
        ),
    )(col, live, before, own, after, tiles)


def spread_kernel(col_ref, live_ref, dagg_ref, tiles_ref, before_ref, own_ref, after_ref, acc):
    step = pl.program_id(0)
    tile = tiles_ref.shape[-1]
    blocks = own_ref.shape[0]
    group = tiles_ref.shape[0]
    per = dagg_ref.shape[2] // tile

    @pl.when(step == 0)
    def _():
        def clear(i, carry):
            acc[i] = jnp.zeros(acc.shape[1:], F32)
            return carry

        lax.fori_loop(0, acc.shape[0], clear, 0, unroll=8)

    for b in range(group):
        r = step * group + b
        grad = dagg_ref[b // per, :, (b % per) * tile : (b % per + 1) * tile]
        first = dot(grad, tiles_ref[b, 0], NT)
        second = dot(grad, tiles_ref[b, 1], NT)
        acc[blocks + r] += first
        acc[col_ref[r]] += jnp.where(live_ref[r] > 0, second, 0.0)

    @pl.when(step == pl.num_programs(0) - 1)
    def _():
        def store(i, carry):
            before_ref[i] = acc[i].astype(BF16)
            own_ref[i] = acc[blocks + i]
            after_ref[i] = acc[2 * blocks + i].astype(BF16)
            return carry

        lax.fori_loop(0, blocks, store, 0, unroll=4)


def spread(col, live, dagg, tiles):
    groups, rows, width = dagg.shape
    blocks, slots, tile, _ = tiles.shape
    per = width // tile
    group = 4 * per
    smem = pl.BlockSpec(memory_space=pltpu.SMEM)
    whole = pl.BlockSpec((blocks, rows, tile), lambda g: (0, 0, 0))
    shape = (blocks, rows, tile)
    return pl.pallas_call(
        spread_kernel,
        grid=(blocks // group,),
        in_specs=[
            smem,
            smem,
            pl.BlockSpec((group // per, rows, width), lambda g: (g, 0, 0)),
            pl.BlockSpec((group, slots, tile, tile), lambda g: (g, 0, 0, 0)),
        ],
        out_specs=[whole, whole, whole],
        out_shape=[
            jax.ShapeDtypeStruct(shape, BF16),
            jax.ShapeDtypeStruct(shape, F32),
            jax.ShapeDtypeStruct(shape, BF16),
        ],
        scratch_shapes=[pltpu.VMEM((3 * blocks, rows, tile), F32)],
        compiler_params=params(56),
        cost_estimate=pl.CostEstimate(
            flops=4 * rows * blocks * tile * tile, bytes_accessed=9 * MIB, transcendentals=0
        ),
    )(col, live, dagg, tiles)


def self_kernel(chunk, w_self, x_ref, out):
    def step(i, carry):
        rows = pl.ds(pl.multiple_of(i * chunk, chunk), chunk)
        out[rows, :] = dot(w_self[rows, :], x_ref[...])
        return carry

    lax.fori_loop(0, out.shape[0] // chunk, step, 0)


def self_product(w_self, x_rows):
    size, width = x_rows.shape
    vmem = pl.BlockSpec(memory_space=pltpu.VMEM)
    return pl.pallas_call(
        functools.partial(self_kernel, 256),
        in_specs=[vmem] * 2,
        out_specs=vmem,
        out_shape=jax.ShapeDtypeStruct((size, width), F32),
        compiler_params=pltpu.CompilerParams(vmem_limit_bytes=56 * MIB),
        cost_estimate=pl.CostEstimate(
            flops=2 * size * size * width, bytes_accessed=5 * MIB, transcendentals=0
        ),
    )(w_self, x_rows)


def dense_kernel(
    chunk,
    w_neigh_hbm,
    w_back_hbm,
    pre_hbm,
    agg_hbm,
    cot_hbm,
    hidden_hbm,
    dpre_hbm,
    dagg_hbm,
    w_neigh,
    w_back,
    pre_ref,
    agg_ref,
    cot_ref,
    hidden,
    dpre,
    dagg,
    in_sems,
    out_sems,
):
    steps = w_neigh.shape[0] // chunk
    part = [slice(i * chunk, (i + 1) * chunk) for i in range(steps)]
    whole = pltpu.make_async_copy(agg_hbm, agg_ref, in_sems.at[4, 0])
    whole.start()
    sources = ((w_neigh_hbm, w_neigh), (pre_hbm, pre_ref), (cot_hbm, cot_ref), (w_back_hbm, w_back))
    loads = [
        [
            pltpu.make_async_copy(src.at[part[i]], dst.at[part[i]], in_sems.at[k, i])
            for i in range(steps)
        ]
        for k, (src, dst) in enumerate(sources)
    ]
    for i in range(steps):
        for k in range(3):
            loads[k][i].start()
    for i in range(steps):
        loads[3][i].start()
    whole.wait()
    stores = []

    def store(k, src, dst, i):
        copy = pltpu.make_async_copy(src.at[part[i]], dst.at[part[i]], out_sems.at[k, i])
        copy.start()
        stores.append(copy)

    for i in range(steps):
        for k in range(3):
            loads[k][i].wait()
        pre = pre_ref[part[i], :] + dot(w_neigh[part[i], :], agg_ref[...])
        sig = jax.nn.sigmoid(pre)
        hidden[part[i], :] = (pre * sig).astype(BF16)
        slope = sig * (1.0 + pre * (1.0 - sig))
        dpre[part[i], :] = (cot_ref[part[i], :].astype(F32) * slope).astype(BF16)
        store(0, hidden, hidden_hbm, i)
        store(1, dpre, dpre_hbm, i)
    for i in range(steps):
        loads[3][i].wait()
        dagg[part[i], :] = dot(w_back[part[i], :], dpre[...]).astype(BF16)
        store(2, dagg, dagg_hbm, i)
    for copy in stores:
        copy.wait()


def dense(w_neigh, w_back, pre_self, agg_rows, cot):
    size, width = agg_rows.shape
    chunk = 256
    steps = size // chunk
    anywhere = pl.BlockSpec(memory_space=pl.ANY)
    out = jax.ShapeDtypeStruct((size, width), BF16)
    return pl.pallas_call(
        functools.partial(dense_kernel, chunk),
        in_specs=[anywhere] * 5,
        out_specs=[anywhere] * 3,
        out_shape=[out] * 3,
        scratch_shapes=[
            pltpu.VMEM((size, size), BF16),
            pltpu.VMEM((size, size), BF16),
            pltpu.VMEM((size, width), F32),
        ]
        + [pltpu.VMEM((size, width), BF16)] * 5
        + [pltpu.SemaphoreType.DMA((5, steps)), pltpu.SemaphoreType.DMA((3, steps))],
        compiler_params=pltpu.CompilerParams(vmem_limit_bytes=56 * MIB),
        cost_estimate=pl.CostEstimate(
            flops=4 * size * size * width, bytes_accessed=12 * MIB, transcendentals=size * width
        ),
    )(w_neigh, w_back, pre_self, agg_rows, cot)


def late_kernel(chunk, w_back, dpre, ordered, agg_ref, dself, grad):
    def step(i, carry):
        rows = pl.ds(pl.multiple_of(i * chunk, chunk), chunk)
        dself[rows, :] = dot(w_back[rows, :], dpre[...]).astype(BF16)
        return carry

    lax.fori_loop(0, dself.shape[0] // chunk, step, 0)

    def weight(i, carry):
        rows = pl.ds(pl.multiple_of(i * chunk, chunk), chunk)
        grad[rows, :] = dot(ordered[rows, :], agg_ref[...], NT).astype(BF16)
        return carry

    lax.fori_loop(0, grad.shape[0] // chunk, weight, 0)


def late(w_back, dpre, ordered, agg_rows):
    size, width = dpre.shape
    vmem = pl.BlockSpec(memory_space=pltpu.VMEM)
    return pl.pallas_call(
        functools.partial(late_kernel, 256),
        in_specs=[vmem] * 4,
        out_specs=[vmem] * 2,
        out_shape=[
            jax.ShapeDtypeStruct((size, width), BF16),
            jax.ShapeDtypeStruct((size, size), BF16),
        ],
        compiler_params=pltpu.CompilerParams(vmem_limit_bytes=56 * MIB),
        cost_estimate=pl.CostEstimate(
            flops=4 * size * size * width, bytes_accessed=7 * MIB, transcendentals=0
        ),
    )(w_back, dpre, ordered, agg_rows)


def final_kernel(own_ref, before_ref, after_ref, dself_ref, out_ref):
    tile = own_ref.shape[2]
    per = dself_ref.shape[2] // tile
    for b in range(own_ref.shape[0]):
        grad = dself_ref[b // per, :, (b % per) * tile : (b % per + 1) * tile]
        total = own_ref[b] + before_ref[b].astype(F32) + after_ref[b].astype(F32)
        out_ref[:, b * tile : (b + 1) * tile] = (grad.astype(F32) + total).astype(BF16)


def finish(own, before, after, dself):
    groups, rows, width = dself.shape
    blocks, _, tile = own.shape
    steps = 4
    part = pl.BlockSpec((blocks // steps, rows, tile), lambda g: (g, 0, 0))
    return pl.pallas_call(
        final_kernel,
        grid=(steps,),
        in_specs=[part, part, part]
        + [pl.BlockSpec((groups // steps, rows, width), lambda g: (g, 0, 0))],
        out_specs=pl.BlockSpec((rows, groups * width // steps), lambda g: (0, g)),
        out_shape=jax.ShapeDtypeStruct((rows, groups * width), BF16),
        compiler_params=params(56),
    )(own, before, after, dself)


def shifted(value, axis, steps):
    count = lax.axis_size(axis)
    first, last = max(0, -steps), min(count, count - steps)
    return lax.ppermute(value, axis, [(source, source + steps) for source in range(first, last)])


def exchange(value, axis):
    return lax.all_to_all(value, axis, split_axis=0, concat_axis=0, tiled=True)


SIDE = 4
CORES = 2


def by_owner(rows):
    size, width = rows.shape
    owners = lax.axis_size("node") * lax.axis_size("feat")
    rows = rows.reshape(SIDE, SIDE, -1, CORES, size // owners, width)
    return rows.transpose(3, 1, 0, 2, 4, 5).reshape(size, width)


def piece_at(pieces, index):
    return lax.dynamic_index_in_dim(pieces, index, 0, keepdims=False)


def exchange_sum(value, axis, count, index, partner, sent):
    pieces = value.reshape(count, -1, value.shape[-1])
    total = piece_at(pieces, index).astype(F32)
    for step in range(1, count):
        piece = piece_at(pieces, lax.rem(index + step, count)).astype(sent)
        pairs = [(i, partner(i, step)) for i in range(lax.axis_size(axis))]
        total = total + lax.ppermute(piece, axis, pairs).astype(F32)
    return total


def summed_over_all(value):
    feat, node = lax.axis_index("feat"), lax.axis_index("node")
    value = exchange_sum(value, "feat", CORES, lax.rem(feat, CORES), lambda i, s: i ^ 1, BF16)
    y = lambda i, s: i // SIDE * SIDE + (i + s) % SIDE
    value = exchange_sum(value, "node", SIDE, lax.rem(node, SIDE), y, BF16)
    x = lambda i, s: (i + s * SIDE) % (SIDE * SIDE)
    value = exchange_sum(value, "node", SIDE, lax.div(node, SIDE), x, BF16)
    half = lax.axis_size("feat") // 2
    while half >= CORES:
        flip = lambda i, s, half=half: i ^ half
        value = exchange_sum(value, "feat", 2, lax.rem(lax.div(feat, half), 2), flip, F32)
        half //= 2
    return value


def local(features, tile_values, tile_cols, tile_count, w_self, w_neigh, cotangent):
    feat_dev, node_dev = features.shape
    tile = tile_values.shape[-1]
    block_count = node_dev // tile
    groups = lax.axis_size("feat")
    size = w_self.shape[0]
    part = lax.axis_index("node")
    col = tile_cols[:, 1] - (part - 1) * block_count
    live = (tile_count > 1).astype(jnp.int32)

    before = shifted(features, "node", 1)
    after = shifted(features, "node", -1)
    x_rows = exchange(split_columns(features, groups), "feat").reshape(size, -1)
    agg = aggregate(col, live, before, features, after, tile_values, groups)
    agg_rows = exchange(agg, "feat").reshape(size, -1)
    pre_self = self_product(w_self, x_rows)
    hidden, dpre, dagg = dense(w_neigh, w_neigh.T, pre_self, agg_rows, cotangent)
    dagg_cols = exchange(dagg.reshape(groups, feat_dev, -1), "feat")
    dself, part_neigh = late(w_self.T, dpre, by_owner(dpre), agg_rows)
    dself_cols = exchange(dself.reshape(groups, feat_dev, -1), "feat")

    grad_w_neigh = summed_over_all(part_neigh)

    to_before, own, to_after = spread(col, live, dagg_cols, tile_values)
    from_after = shifted(to_before, "node", -1)
    from_before = shifted(to_after, "node", 1)
    grad_features = finish(own, from_before, from_after, dself_cols)
    return (hidden, grad_features, grad_w_neigh)


def solution(mesh):
    placed = (
        P("feat", "node"),
        P("node", None, None, None),
        P("node", None),
        P("node"),
        P(),
        P(),
        P(None, ("node", "feat")),
    )
    return jax.shard_map(
        local,
        mesh=mesh,
        in_specs=placed,
        out_specs=(P(None, ("node", "feat")), P("feat", "node"), P(("node", "feat"), None)),
        check_vma=False,
    )
```

```python
import functools

import jax
import jax.numpy as jnp
from jax import lax
from jax.experimental import pallas as pl
from jax.experimental.pallas import tpu as pltpu
from jax.sharding import PartitionSpec as P

F32 = jnp.float32
BF16 = jnp.bfloat16
NT = (((1,), (1,)), ((), ()))
NN = (((1,), (0,)), ((), ()))
MIB = 1 << 20


def dot(a, b, dims=NN):
    return lax.dot_general(a, b, dims, preferred_element_type=F32)


def whole_params(mib):
    return pltpu.CompilerParams(vmem_limit_bytes=mib * MIB)


def params(mib):
    return pltpu.CompilerParams(
        dimension_semantics=("arbitrary",), vmem_limit_bytes=mib * MIB
    )


def split_kernel(x_hbm, out_hbm, sems):
    width = out_hbm.shape[2]
    copies = [
        pltpu.make_async_copy(x_hbm.at[:, g * width : (g + 1) * width], out_hbm.at[g], sems.at[g])
        for g in range(out_hbm.shape[0])
    ]
    for copy in copies:
        copy.start()
    for copy in copies:
        copy.wait()


ANYWHERE = pl.BlockSpec(memory_space=pl.ANY)
SMEM = pl.BlockSpec(memory_space=pltpu.SMEM)
VMEM = pl.BlockSpec(memory_space=pltpu.VMEM)


def split_columns(x, groups):
    rows, columns = x.shape
    return pl.pallas_call(
        split_kernel,
        in_specs=[ANYWHERE],
        out_specs=ANYWHERE,
        out_shape=jax.ShapeDtypeStruct((groups, rows, columns // groups), x.dtype),
        scratch_shapes=[pltpu.SemaphoreType.DMA((groups,))],
        compiler_params=whole_params(60),
    )(x)


def gather_kernel(col_ref, before, own, after, out_hbm, sems):
    tile = 128
    blocks = own.shape[1] // tile
    per = out_hbm.shape[2] // tile

    def target(r):
        place = pl.ds(pl.multiple_of(lax.rem(r, per) * tile, tile), tile)
        return out_hbm.at[lax.div(r, per), :, place]

    def start(r, carry):
        col = col_ref[r]
        for i, part in enumerate((before, own, after)):

            @pl.when((col >= i * blocks) & (col < (i + 1) * blocks))
            def _(i=i, part=part):
                place = pl.ds(pl.multiple_of((col - i * blocks) * tile, tile), tile)
                pltpu.make_async_copy(part.at[:, place], target(r), sems.at[r]).start()

        return carry

    def wait(r, carry):
        pltpu.make_async_copy(own.at[:, :tile], target(r), sems.at[r]).wait()
        return carry

    lax.fori_loop(0, blocks, start, 0)
    lax.fori_loop(0, blocks, wait, 0)


def gather(col, before, own, after, groups):
    rows, span = own.shape
    return pl.pallas_call(
        gather_kernel,
        in_specs=[SMEM] + [ANYWHERE] * 3,
        out_specs=ANYWHERE,
        out_shape=jax.ShapeDtypeStruct((groups, rows, span // groups), BF16),
        scratch_shapes=[pltpu.SemaphoreType.DMA((col.shape[0],))],
        compiler_params=whole_params(2),
        cost_estimate=pl.CostEstimate(flops=0, bytes_accessed=8 * MIB, transcendentals=0),
    )(col, before, own, after)


def scatter_kernel(col_ref, parts_ref, before_hbm, own_hbm, after_hbm, acc, before, after, sems):
    tile = acc.shape[2]
    blocks = own_hbm.shape[0]
    per = parts_ref.shape[2] // tile

    def clear(i, carry):
        acc[i] = jnp.zeros(acc.shape[1:], F32)
        return carry

    lax.fori_loop(0, acc.shape[0], clear, 0, unroll=8)

    def add(g, carry):
        for b in range(per):
            acc[col_ref[g * per + b]] += parts_ref[g, :, b * tile : (b + 1) * tile].astype(F32)
        return carry

    lax.fori_loop(0, parts_ref.shape[0], add, 0)

    def cast(i, carry):
        before[i] = acc[i].astype(BF16)
        after[i] = acc[2 * blocks + i].astype(BF16)
        return carry

    lax.fori_loop(0, blocks, cast, 0, unroll=4)
    copies = [
        pltpu.make_async_copy(before, before_hbm, sems.at[0]),
        pltpu.make_async_copy(after, after_hbm, sems.at[1]),
        pltpu.make_async_copy(acc.at[blocks : 2 * blocks], own_hbm, sems.at[2]),
    ]
    for copy in copies:
        copy.start()
    for copy in copies:
        copy.wait()


def scatter(col, parts):
    groups, rows, width = parts.shape
    blocks = col.shape[0]
    tile = groups * width // blocks
    shape = (blocks, rows, tile)
    return pl.pallas_call(
        scatter_kernel,
        in_specs=[SMEM, VMEM],
        out_specs=[ANYWHERE] * 3,
        out_shape=[
            jax.ShapeDtypeStruct(shape, BF16),
            jax.ShapeDtypeStruct(shape, F32),
            jax.ShapeDtypeStruct(shape, BF16),
        ],
        scratch_shapes=[
            pltpu.VMEM((3 * blocks, rows, tile), F32),
            pltpu.VMEM(shape, BF16),
            pltpu.VMEM(shape, BF16),
            pltpu.SemaphoreType.DMA((3,)),
        ],
        compiler_params=whole_params(60),
        cost_estimate=pl.CostEstimate(flops=0, bytes_accessed=8 * MIB, transcendentals=0),
    )(col, parts)


def self_kernel(chunk, w_self, x_ref, tiles, pre, agg):
    tile = tiles.shape[-1]
    for i in range(pre.shape[0] // chunk):
        rows = slice(i * chunk, (i + 1) * chunk)
        pre[rows, :] = dot(w_self[rows, :], x_ref[...])
        for b in range(tiles.shape[0]):
            here = slice(b * tile, (b + 1) * tile)
            agg[rows, here] = dot(x_ref[rows, here], tiles[b, 0])


def self_products(w_self, x_rows, tiles):
    size, width = x_rows.shape
    out = jax.ShapeDtypeStruct((size, width), F32)
    return pl.pallas_call(
        functools.partial(self_kernel, 256),
        in_specs=[VMEM] * 3,
        out_specs=[VMEM] * 2,
        out_shape=[out, out],
        compiler_params=whole_params(60),
        cost_estimate=pl.CostEstimate(
            flops=2 * size * size * width, bytes_accessed=7 * MIB, transcendentals=0
        ),
    )(w_self, x_rows, tiles)


def dense_kernel(
    chunk,
    live_ref,
    tiles_hbm,
    picked_hbm,
    agg_self_hbm,
    w_neigh_hbm,
    pre_hbm,
    cot_hbm,
    w_back_hbm,
    agg_hbm,
    hidden_hbm,
    dpre_hbm,
    dagg_hbm,
    second_hbm,
    tiles,
    picked,
    agg_self,
    w_neigh,
    pre_ref,
    cot_ref,
    w_back,
    agg,
    hidden,
    dpre,
    dagg,
    second,
    in_sems,
    out_sems,
    tile_sem,
):
    steps = w_neigh.shape[0] // chunk
    tile = tiles.shape[-1]
    count = tiles.shape[0]
    part = [slice(i * chunk, (i + 1) * chunk) for i in range(steps)]
    here = [slice(b * tile, (b + 1) * tile) for b in range(count)]
    first = pltpu.make_async_copy(tiles_hbm, tiles, tile_sem)
    first.start()
    loads = {}
    order = (
        (picked_hbm, picked),
        (agg_self_hbm, agg_self),
        (w_neigh_hbm, w_neigh),
        (pre_hbm, pre_ref),
        (cot_hbm, cot_ref),
        (w_back_hbm, w_back),
    )
    for stage in ((0, 1), (2, 3, 4), (5,)):
        for i in range(steps):
            for k in stage:
                src, dst = order[k]
                copy = pltpu.make_async_copy(src.at[part[i]], dst.at[part[i]], in_sems.at[k, i])
                copy.start()
                loads[k, i] = copy
    stores = []

    def store(k, src, dst, i):
        copy = pltpu.make_async_copy(src.at[part[i]], dst.at[part[i]], out_sems.at[k, i])
        copy.start()
        stores.append(copy)

    first.wait()
    for i in range(steps):
        loads[0, i].wait()
        loads[1, i].wait()
        for b in range(count):
            other = dot(picked[part[i], here[b]], tiles[b, 1])
            total = agg_self[part[i], here[b]] + jnp.where(live_ref[b] > 0, other, 0.0)
            agg[part[i], here[b]] = total.astype(BF16)
        store(0, agg, agg_hbm, i)
    for i in range(steps):
        for k in (2, 3, 4):
            loads[k, i].wait()
        pre = pre_ref[part[i], :] + dot(w_neigh[part[i], :], agg[...])
        sig = jax.nn.sigmoid(pre)
        hidden[part[i], :] = (pre * sig).astype(BF16)
        slope = sig * (1.0 + pre * (1.0 - sig))
        dpre[part[i], :] = (cot_ref[part[i], :].astype(F32) * slope).astype(BF16)
        store(1, hidden, hidden_hbm, i)
        store(2, dpre, dpre_hbm, i)
    for i in range(steps):
        loads[5, i].wait()
        dagg[part[i], :] = dot(w_back[part[i], :], dpre[...]).astype(BF16)
        for b in range(count):
            other = dot(dagg[part[i], here[b]], tiles[b, 1], NT)
            second[part[i], here[b]] = jnp.where(live_ref[b] > 0, other, 0.0).astype(BF16)
        store(3, dagg, dagg_hbm, i)
        store(4, second, second_hbm, i)
    for copy in stores:
        copy.wait()


def dense(live, tiles, picked, agg_self, w_neigh, pre_self, cot, w_back):
    size, width = picked.shape
    chunk = 256
    steps = size // chunk
    out = jax.ShapeDtypeStruct((size, width), BF16)
    wide, narrow = pltpu.VMEM((size, width), F32), pltpu.VMEM((size, width), BF16)
    square = pltpu.VMEM((size, size), BF16)
    return pl.pallas_call(
        functools.partial(dense_kernel, chunk),
        in_specs=[SMEM] + [ANYWHERE] * 7,
        out_specs=[ANYWHERE] * 5,
        out_shape=[out] * 5,
        scratch_shapes=[pltpu.VMEM(tiles.shape, BF16), narrow, wide, square, wide, narrow, square]
        + [narrow] * 5
        + [
            pltpu.SemaphoreType.DMA((6, steps)),
            pltpu.SemaphoreType.DMA((5, steps)),
            pltpu.SemaphoreType.DMA(()),
        ],
        compiler_params=whole_params(60),
        cost_estimate=pl.CostEstimate(
            flops=4 * size * size * width, bytes_accessed=16 * MIB, transcendentals=size * width
        ),
    )(live, tiles, picked, agg_self, w_neigh, pre_self, cot, w_back)


def own_kernel(chunk, w_back, dpre, dagg_ref, tiles, own):
    tile = tiles.shape[-1]
    for i in range(own.shape[0] // chunk):
        rows = slice(i * chunk, (i + 1) * chunk)
        dself = dot(w_back[rows, :], dpre[...])
        for b in range(tiles.shape[0]):
            here = slice(b * tile, (b + 1) * tile)
            total = dself[:, here] + dot(dagg_ref[rows, here], tiles[b, 0], NT)
            own[rows, here] = total.astype(BF16)


def own_part(w_back, dpre, dagg, tiles):
    size, width = dpre.shape
    return pl.pallas_call(
        functools.partial(own_kernel, 256),
        in_specs=[VMEM] * 4,
        out_specs=VMEM,
        out_shape=jax.ShapeDtypeStruct((size, width), BF16),
        compiler_params=whole_params(12),
        cost_estimate=pl.CostEstimate(
            flops=2 * size * size * width, bytes_accessed=5 * MIB, transcendentals=0
        ),
    )(w_back, dpre, dagg, tiles)


def weight_kernel(chunk, half_ref, dpre, agg_ref, grad):
    rows = grad.shape[1]
    half = agg_ref.at[pl.ds(pl.multiple_of(half_ref[0] * rows, rows), rows)]
    for i in range(grad.shape[0] // chunk):
        here = slice(i * chunk, (i + 1) * chunk)
        grad[here, :] = dot(dpre[here, :], half[...], NT).astype(BF16)


def weight_sum_kernel(chunk, half_ref, dpre, agg_ref, other_ref, grad):
    rows = grad.shape[1]
    half = agg_ref.at[pl.ds(pl.multiple_of(half_ref[0] * rows, rows), rows)]
    for i in range(grad.shape[0] // chunk):
        here = slice(i * chunk, (i + 1) * chunk)
        total = dot(dpre[here, :], half[...], NT) + other_ref[here, :].astype(F32)
        grad[here, :] = total.astype(BF16)


def weight_part(half, dpre, agg_rows, other=None):
    size, width = dpre.shape
    body = weight_kernel if other is None else weight_sum_kernel
    more = () if other is None else (other,)
    return pl.pallas_call(
        functools.partial(body, 256),
        in_specs=[SMEM] + [VMEM] * (2 + len(more)),
        out_specs=VMEM,
        out_shape=jax.ShapeDtypeStruct((size, size // CORES), BF16),
        compiler_params=whole_params(12),
        cost_estimate=pl.CostEstimate(
            flops=size * size * width, bytes_accessed=3 * MIB, transcendentals=0
        ),
    )(half, dpre, agg_rows, *more)


def final_kernel(own_ref, before_ref, after_ref, dself_ref, out_ref):
    tile = own_ref.shape[2]
    per = dself_ref.shape[2] // tile
    for b in range(own_ref.shape[0]):
        grad = dself_ref[b // per, :, (b % per) * tile : (b % per + 1) * tile]
        total = own_ref[b] + before_ref[b].astype(F32) + after_ref[b].astype(F32)
        out_ref[:, b * tile : (b + 1) * tile] = (grad.astype(F32) + total).astype(BF16)


def finish(own, before, after, dself):
    groups, rows, width = dself.shape
    blocks, _, tile = own.shape
    steps = 4
    part = pl.BlockSpec((blocks // steps, rows, tile), lambda g: (g, 0, 0))
    return pl.pallas_call(
        final_kernel,
        grid=(steps,),
        in_specs=[part, part, part]
        + [pl.BlockSpec((groups // steps, rows, width), lambda g: (g, 0, 0))],
        out_specs=pl.BlockSpec((rows, groups * width // steps), lambda g: (0, g)),
        out_shape=jax.ShapeDtypeStruct((rows, groups * width), BF16),
        compiler_params=params(16),
    )(own, before, after, dself)


def shifted(value, axis, steps):
    count = lax.axis_size(axis)
    first, last = max(0, -steps), min(count, count - steps)
    return lax.ppermute(value, axis, [(source, source + steps) for source in range(first, last)])


def exchange(value, axis):
    return lax.all_to_all(value, axis, split_axis=0, concat_axis=0, tiled=True)


SIDE = 4
CORES = 2


def piece_at(pieces, index):
    return lax.dynamic_index_in_dim(pieces, index, 0, keepdims=False)


def exchange_sum(value, axis, count, index, partner, sent):
    pieces = value.reshape(count, -1, value.shape[-1])
    total = piece_at(pieces, index).astype(F32)
    for step in range(1, count):
        piece = piece_at(pieces, lax.rem(index + step, count)).astype(sent)
        pairs = [(i, partner(i, step)) for i in range(lax.axis_size(axis))]
        total = total + lax.ppermute(piece, axis, pairs).astype(F32)
    return total


def after(value, other):
    return lax.optimization_barrier((value, other))[0]


def weight_gradient(dpre, agg_rows, spread, halo):
    feat, node = lax.axis_index("feat"), lax.axis_index("node")
    core = lax.rem(feat, CORES)
    pairs = [(i, i ^ 1) for i in range(lax.axis_size("feat"))]
    sent = weight_part(1 - core[None], dpre, agg_rows)
    value = weight_part(core[None], dpre, agg_rows, lax.ppermute(sent, "feat", pairs))
    x = lambda i, s: (i + s * SIDE) % (SIDE * SIDE)
    value = exchange_sum(value, "node", SIDE, lax.div(node, SIDE), x, BF16)
    value = after(value, spread)
    y = lambda i, s: i // SIDE * SIDE + (i + s) % SIDE
    value = exchange_sum(value, "node", SIDE, lax.rem(node, SIDE), y, BF16)
    half = lax.axis_size("feat") // 2
    while half > 1:
        if half == CORES:
            value = after(value, halo)
        flip = lambda i, s, half=half: i ^ half
        value = exchange_sum(value, "feat", 2, lax.rem(lax.div(feat, half), 2), flip, F32)
        half //= 2
    pieces = value.reshape(CORES, -1, value.shape[-1])
    other = lax.ppermute(piece_at(pieces, 1 - core), "feat", pairs)
    kept = piece_at(pieces, core)
    first, second = jnp.where(core == 0, kept, other), jnp.where(core == 0, other, kept)
    return jnp.concatenate([first, second], axis=1)


def local(features, tile_values, tile_cols, tile_count, w_self, w_neigh, cotangent):
    feat_dev, node_dev = features.shape
    tile = tile_values.shape[-1]
    block_count = node_dev // tile
    groups = lax.axis_size("feat")
    size = w_self.shape[0]
    part, feat = lax.axis_index("node"), lax.axis_index("feat")
    col = tile_cols[:, 1] - (part - 1) * block_count
    mine = block_count // groups
    live = (lax.dynamic_slice_in_dim(tile_count, feat * mine, mine) > 1).astype(jnp.int32)
    tiles = lax.dynamic_slice_in_dim(tile_values, feat * mine, mine)

    before = shifted(features, "node", 1)
    after = shifted(features, "node", -1)
    x_rows = exchange(split_columns(features, groups), "feat").reshape(size, -1)
    picked = exchange(gather(col, before, features, after, groups), "feat").reshape(size, -1)
    pre_self, agg_self = self_products(w_self, x_rows, tiles)
    agg_rows, hidden, dpre, dagg, second = dense(
        live, tiles, picked, agg_self, w_neigh, pre_self, cotangent, w_neigh.T
    )
    second_cols = exchange(second.reshape(groups, feat_dev, -1), "feat")
    own_rows = own_part(w_self.T, dpre, dagg, tiles)
    second_cols, own_rows = lax.optimization_barrier((second_cols, own_rows))
    own_cols = exchange(own_rows.reshape(groups, feat_dev, -1), "feat")
    to_before, spread, to_after = scatter(col, second_cols)
    from_after = shifted(to_before, "node", -1)
    from_before = shifted(to_after, "node", 1)
    grad_w_neigh = weight_gradient(dpre, agg_rows, spread, (from_after, from_before))
    grad_features = finish(spread, from_before, from_after, own_cols)
    return (hidden, grad_features, grad_w_neigh)


def solution(mesh):
    placed = (
        P("feat", "node"),
        P("node", None, None, None),
        P("node", None),
        P("node"),
        P(),
        P(),
        P(None, ("node", "feat")),
    )
    return jax.shard_map(
        local,
        mesh=mesh,
        in_specs=placed,
        out_specs=(P(None, ("node", "feat")), P("feat", "node"), P(("node", "feat"), None)),
        check_vma=False,
    )
```

```python
import functools

import jax
import jax.numpy as jnp
from jax import lax
from jax.experimental import pallas as pl
from jax.experimental.pallas import tpu as pltpu
from jax.sharding import PartitionSpec as P

F32 = jnp.float32
BF16 = jnp.bfloat16
NT = (((1,), (1,)), ((), ()))
NN = (((1,), (0,)), ((), ()))
MIB = 1 << 20
DENSE_MIB = 60


def dot(a, b, dims=NN):
    return lax.dot_general(a, b, dims, preferred_element_type=F32)


def whole_params(mib):
    return pltpu.CompilerParams(vmem_limit_bytes=mib * MIB)


def params(mib):
    return pltpu.CompilerParams(
        dimension_semantics=("arbitrary",), vmem_limit_bytes=mib * MIB
    )


def split_kernel(x_hbm, out_hbm, held, in_sems, out_sems):
    width = out_hbm.shape[2]
    groups = range(out_hbm.shape[0])
    loads = [
        pltpu.make_async_copy(x_hbm.at[:, g * width : (g + 1) * width], held.at[g], in_sems.at[g])
        for g in groups
    ]
    stores = [pltpu.make_async_copy(held.at[g], out_hbm.at[g], out_sems.at[g]) for g in groups]
    for copy in loads:
        copy.start()
    for load, store in zip(loads, stores):
        load.wait()
        store.start()
    for copy in stores:
        copy.wait()


ANYWHERE = pl.BlockSpec(memory_space=pl.ANY)
SMEM = pl.BlockSpec(memory_space=pltpu.SMEM)
VMEM = pl.BlockSpec(memory_space=pltpu.VMEM)


def split_columns(x, groups):
    rows, columns = x.shape
    return pl.pallas_call(
        split_kernel,
        in_specs=[ANYWHERE],
        out_specs=ANYWHERE,
        out_shape=jax.ShapeDtypeStruct((groups, rows, columns // groups), x.dtype),
        scratch_shapes=[
            pltpu.VMEM((groups, rows, columns // groups), x.dtype),
            pltpu.SemaphoreType.DMA((groups,)),
            pltpu.SemaphoreType.DMA((groups,)),
        ],
        compiler_params=whole_params(60),
    )(x)


def gather_kernel(col_ref, before, own, after, out_hbm, sems):
    tile = 128
    blocks = own.shape[1] // tile
    per = out_hbm.shape[2] // tile

    def target(r):
        place = pl.ds(pl.multiple_of(lax.rem(r, per) * tile, tile), tile)
        return out_hbm.at[lax.div(r, per), :, place]

    def start(r, carry):
        col = col_ref[r]
        for i, part in enumerate((before, own, after)):

            @pl.when((col >= i * blocks) & (col < (i + 1) * blocks))
            def _(i=i, part=part):
                place = pl.ds(pl.multiple_of((col - i * blocks) * tile, tile), tile)
                pltpu.make_async_copy(part.at[:, place], target(r), sems.at[r]).start()

        return carry

    def wait(r, carry):
        pltpu.make_async_copy(own.at[:, :tile], target(r), sems.at[r]).wait()
        return carry

    lax.fori_loop(0, blocks, start, 0)
    lax.fori_loop(0, blocks, wait, 0)


def gather(col, before, own, after, groups):
    rows, span = own.shape
    return pl.pallas_call(
        gather_kernel,
        in_specs=[SMEM] + [ANYWHERE] * 3,
        out_specs=ANYWHERE,
        out_shape=jax.ShapeDtypeStruct((groups, rows, span // groups), BF16),
        scratch_shapes=[pltpu.SemaphoreType.DMA((col.shape[0],))],
        compiler_params=whole_params(2),
        cost_estimate=pl.CostEstimate(flops=0, bytes_accessed=8 * MIB, transcendentals=0),
    )(col, before, own, after)


def scatter_kernel(col_ref, parts_ref, before_hbm, own_hbm, after_hbm, acc, before, after, sems):
    tile = acc.shape[2]
    blocks = own_hbm.shape[0]
    per = parts_ref.shape[2] // tile

    def clear(i, carry):
        acc[i] = jnp.zeros(acc.shape[1:], F32)
        return carry

    lax.fori_loop(0, acc.shape[0], clear, 0, unroll=8)

    def add(g, carry):
        for b in range(per):
            acc[col_ref[g * per + b]] += parts_ref[g, :, b * tile : (b + 1) * tile].astype(F32)
        return carry

    lax.fori_loop(0, parts_ref.shape[0], add, 0)

    def cast(i, carry):
        before[i] = acc[i].astype(BF16)
        after[i] = acc[2 * blocks + i].astype(BF16)
        return carry

    lax.fori_loop(0, blocks, cast, 0, unroll=4)
    copies = [
        pltpu.make_async_copy(before, before_hbm, sems.at[0]),
        pltpu.make_async_copy(after, after_hbm, sems.at[1]),
        pltpu.make_async_copy(acc.at[blocks : 2 * blocks], own_hbm, sems.at[2]),
    ]
    for copy in copies:
        copy.start()
    for copy in copies:
        copy.wait()


def scatter(col, parts):
    groups, rows, width = parts.shape
    blocks = col.shape[0]
    tile = groups * width // blocks
    shape = (blocks, rows, tile)
    return pl.pallas_call(
        scatter_kernel,
        in_specs=[SMEM, VMEM],
        out_specs=[ANYWHERE] * 3,
        out_shape=[
            jax.ShapeDtypeStruct(shape, BF16),
            jax.ShapeDtypeStruct(shape, F32),
            jax.ShapeDtypeStruct(shape, BF16),
        ],
        scratch_shapes=[
            pltpu.VMEM((3 * blocks, rows, tile), F32),
            pltpu.VMEM(shape, BF16),
            pltpu.VMEM(shape, BF16),
            pltpu.SemaphoreType.DMA((3,)),
        ],
        compiler_params=whole_params(60),
        cost_estimate=pl.CostEstimate(flops=0, bytes_accessed=8 * MIB, transcendentals=0),
    )(col, parts)


def self_kernel(chunk, w_self, x_ref, pre):
    for i in range(pre.shape[0] // chunk):
        rows = slice(i * chunk, (i + 1) * chunk)
        pre[rows, :] = dot(w_self[rows, :], x_ref[...])


def self_product(w_self, x_rows):
    size, width = x_rows.shape
    return pl.pallas_call(
        functools.partial(self_kernel, 256),
        in_specs=[VMEM] * 2,
        out_specs=VMEM,
        out_shape=jax.ShapeDtypeStruct((size, width), F32),
        compiler_params=whole_params(60),
        cost_estimate=pl.CostEstimate(
            flops=2 * size * size * width, bytes_accessed=5 * MIB, transcendentals=0
        ),
    )(w_self, x_rows)


def dense_kernel(chunk, *refs):
    (tiles_hbm, turned_hbm, x_hbm, picked_hbm, w_neigh_hbm, pre_hbm, cot_hbm, w_back_hbm) = refs[:8]
    (agg_hbm, hidden_hbm, dpre_hbm, dagg_hbm, second_hbm) = refs[8:13]
    (tiles, turned, x_ref, picked, w_neigh, pre_ref, cot_ref, w_back) = refs[13:21]
    (agg, hidden, dpre, dagg, second, in_sems, out_sems) = refs[21:]
    size = w_neigh.shape[0]
    pair = tiles.shape[-1]
    part = [slice(i, i + chunk) for i in range(0, size, chunk)]
    here = [slice(i, i + pair) for i in range(0, agg.shape[1], pair)]
    loads = [
        pltpu.make_async_copy(refs[k], refs[13 + k], in_sems.at[k]) for k in (0, 2, 3, 4, 5, 6, 7, 1)
    ]
    for copy in loads:
        copy.start()
    stores = []

    def store(k, src, dst, i):
        copy = pltpu.make_async_copy(src.at[part[i]], dst.at[part[i]], out_sems.at[k, i])
        copy.start()
        stores.append(copy)

    for copy in loads[:3]:
        copy.wait()
    for i in range(len(part)):
        for p in range(len(here)):
            total = dot(x_ref[part[i], here[p]], tiles[0, p])
            total = total + dot(picked[part[i], here[p]], tiles[1, p])
            agg[part[i], here[p]] = total.astype(BF16)
    for copy in loads[3:6]:
        copy.wait()
    for i in range(len(part)):
        store(0, agg, agg_hbm, i)
        pre = pre_ref[part[i], :] + dot(w_neigh[part[i], :], agg[...])
        sig = 0.5 + 0.5 * jnp.tanh(0.5 * pre)
        hidden[part[i], :] = (pre * sig).astype(BF16)
        slope = sig * (1.0 + pre * (1.0 - sig))
        dpre[part[i], :] = (cot_ref[part[i], :].astype(F32) * slope).astype(BF16)
    for copy in loads[6:]:
        copy.wait()
    for i in range(len(part)):
        store(1, hidden, hidden_hbm, i)
        store(2, dpre, dpre_hbm, i)
        dagg[part[i], :] = dot(w_back[part[i], :], dpre[...]).astype(BF16)
        for p in range(len(here)):
            second[part[i], here[p]] = dot(dagg[part[i], here[p]], turned[1, p]).astype(BF16)
        store(3, dagg, dagg_hbm, i)
        store(4, second, second_hbm, i)
    for copy in stores:
        copy.wait()


def dense(tiles, turned, x_rows, picked, w_neigh, pre_self, cot, w_back):
    size, width = picked.shape
    chunk = 256
    out = jax.ShapeDtypeStruct((size, width), BF16)
    args = (tiles, turned, x_rows, picked, w_neigh, pre_self, cot, w_back)
    return pl.pallas_call(
        functools.partial(dense_kernel, chunk),
        in_specs=[ANYWHERE] * len(args),
        out_specs=[ANYWHERE] * 5,
        out_shape=[out] * 5,
        scratch_shapes=[pltpu.VMEM(arg.shape, arg.dtype) for arg in args]
        + [pltpu.VMEM((size, width), BF16)] * 5
        + [pltpu.SemaphoreType.DMA((len(args),)), pltpu.SemaphoreType.DMA((5, size // chunk))],
        compiler_params=whole_params(DENSE_MIB),
        cost_estimate=pl.CostEstimate(
            flops=4 * size * size * width, bytes_accessed=16 * MIB, transcendentals=size * width
        ),
    )(*args)


def own_kernel(chunk, w_back, dpre, dagg_ref, turned, own):
    pair = turned.shape[-1]
    for i in range(0, own.shape[0], chunk):
        rows = slice(i, i + chunk)
        dself = dot(w_back[rows, :], dpre[...])
        for p in range(own.shape[1] // pair):
            here = slice(p * pair, (p + 1) * pair)
            total = dself[:, here] + dot(dagg_ref[rows, here], turned[0, p])
            own[rows, here] = total.astype(BF16)


def own_part(w_back, dpre, dagg, turned):
    size, width = dpre.shape
    return pl.pallas_call(
        functools.partial(own_kernel, 256),
        in_specs=[VMEM] * 4,
        out_specs=VMEM,
        out_shape=jax.ShapeDtypeStruct((size, width), BF16),
        compiler_params=whole_params(12),
        cost_estimate=pl.CostEstimate(
            flops=2 * size * size * width, bytes_accessed=5 * MIB, transcendentals=0
        ),
    )(w_back, dpre, dagg, turned)


def weight_kernel(chunk, half_ref, dpre, agg_ref, grad):
    rows = grad.shape[1]
    half = agg_ref.at[pl.ds(pl.multiple_of(half_ref[0] * rows, rows), rows)]
    for i in range(grad.shape[0] // chunk):
        here = slice(i * chunk, (i + 1) * chunk)
        grad[here, :] = dot(dpre[here, :], half[...], NT).astype(BF16)


def weight_sum_kernel(chunk, half_ref, dpre, agg_ref, other_ref, grad):
    rows = grad.shape[1]
    half = agg_ref.at[pl.ds(pl.multiple_of(half_ref[0] * rows, rows), rows)]
    for i in range(grad.shape[0] // chunk):
        here = slice(i * chunk, (i + 1) * chunk)
        total = dot(dpre[here, :], half[...], NT) + other_ref[here, :].astype(F32)
        grad[here, :] = total.astype(BF16)


def weight_part(half, dpre, agg_rows, other=None):
    size, width = dpre.shape
    body = weight_kernel if other is None else weight_sum_kernel
    more = () if other is None else (other,)
    return pl.pallas_call(
        functools.partial(body, 256),
        in_specs=[SMEM] + [VMEM] * (2 + len(more)),
        out_specs=VMEM,
        out_shape=jax.ShapeDtypeStruct((size, size // CORES), BF16),
        compiler_params=whole_params(12),
        cost_estimate=pl.CostEstimate(
            flops=size * size * width, bytes_accessed=3 * MIB, transcendentals=0
        ),
    )(half, dpre, agg_rows, *more)


def final_kernel(own_ref, before_ref, after_ref, dself_ref, out_ref):
    tile = own_ref.shape[2]
    per = dself_ref.shape[2] // tile
    for b in range(own_ref.shape[0]):
        grad = dself_ref[b // per, :, (b % per) * tile : (b % per + 1) * tile]
        total = own_ref[b] + before_ref[b].astype(F32) + after_ref[b].astype(F32)
        out_ref[:, b * tile : (b + 1) * tile] = (grad.astype(F32) + total).astype(BF16)


def finish(own, before, after, dself):
    groups, rows, width = dself.shape
    blocks, _, tile = own.shape
    steps = 4
    part = pl.BlockSpec((blocks // steps, rows, tile), lambda g: (g, 0, 0))
    return pl.pallas_call(
        final_kernel,
        grid=(steps,),
        in_specs=[part, part, part]
        + [pl.BlockSpec((groups // steps, rows, width), lambda g: (g, 0, 0))],
        out_specs=pl.BlockSpec((rows, groups * width // steps), lambda g: (0, g)),
        out_shape=jax.ShapeDtypeStruct((rows, groups * width), BF16),
        compiler_params=params(16),
    )(own, before, after, dself)


def shifted(value, axis, steps):
    count = lax.axis_size(axis)
    first, last = max(0, -steps), min(count, count - steps)
    return lax.ppermute(value, axis, [(source, source + steps) for source in range(first, last)])


def exchange(value, axis):
    return lax.all_to_all(value, axis, split_axis=0, concat_axis=0, tiled=True)


SIDE = 4
CORES = 2


def piece_at(pieces, index):
    return lax.dynamic_index_in_dim(pieces, index, 0, keepdims=False)


def exchange_sum(value, axis, count, index, partner, sent):
    pieces = value.reshape(count, -1, value.shape[-1])
    total = piece_at(pieces, index).astype(F32)
    for step in range(1, count):
        piece = piece_at(pieces, lax.rem(index + step, count)).astype(sent)
        pairs = [(i, partner(i, step)) for i in range(lax.axis_size(axis))]
        total = total + lax.ppermute(piece, axis, pairs).astype(F32)
    return total


def after(value, other):
    return lax.optimization_barrier((value, other))[0]


def weight_first(dpre, agg_rows):
    feat, node = lax.axis_index("feat"), lax.axis_index("node")
    core = lax.rem(feat, CORES)
    pairs = [(i, i ^ 1) for i in range(lax.axis_size("feat"))]
    sent = weight_part(1 - core[None], dpre, agg_rows)
    value = weight_part(core[None], dpre, agg_rows, lax.ppermute(sent, "feat", pairs))
    x = lambda i, s: (i + s * SIDE) % (SIDE * SIDE)
    return exchange_sum(value, "node", SIDE, lax.div(node, SIDE), x, BF16)


def weight_rest(value, last):
    node, groups = lax.axis_index("node"), lax.axis_size("feat")
    y = lambda i, s: i // SIDE * SIDE + (i + s) % SIDE
    value = exchange_sum(value, "node", SIDE, lax.rem(node, SIDE), y, BF16)
    value = after(value, last)
    rows, half = value.shape
    pieces = exchange(value.reshape(groups, rows // groups, half), "feat")
    total = jnp.sum(pieces.reshape(groups // CORES, CORES, rows // groups, half), axis=0)
    return jnp.concatenate([total[i] for i in range(CORES)], axis=1)


def paired(tiles):
    blocks, tile, _ = tiles.shape
    tiles = tiles.reshape(blocks // 2, 2, tile, tile)
    empty = jnp.zeros_like(tiles[:, 0])
    upper = jnp.concatenate([tiles[:, 0], empty], axis=2)
    lower = jnp.concatenate([empty, tiles[:, 1]], axis=2)
    return jnp.concatenate([upper, lower], axis=1)


def local(features, tile_values, tile_cols, tile_count, w_self, w_neigh, cotangent):
    feat_dev, node_dev = features.shape
    tile = tile_values.shape[-1]
    block_count = node_dev // tile
    groups = lax.axis_size("feat")
    size = w_self.shape[0]
    part, feat = lax.axis_index("node"), lax.axis_index("feat")
    col = tile_cols[:, 1] - (part - 1) * block_count
    mine = block_count // groups
    live = lax.dynamic_slice_in_dim(tile_count, feat * mine, mine) > 1
    tiles = lax.dynamic_slice_in_dim(tile_values, feat * mine, mine)
    other = jnp.where(live[:, None, None], tiles[:, 1], jnp.zeros_like(tiles[:, 1]))
    straight = jnp.stack([paired(tiles[:, 0]), paired(other)])
    turned = straight.swapaxes(2, 3)

    before = shifted(features, "node", 1)
    behind = shifted(features, "node", -1)
    x_rows = exchange(split_columns(features, groups), "feat").reshape(size, -1)
    picked = exchange(gather(col, before, features, behind, groups), "feat").reshape(size, -1)
    x_rows, self_back, neigh_back, straight, turned = lax.optimization_barrier(
        (x_rows, w_self.T, w_neigh.T, straight, turned)
    )
    pre_self = self_product(w_self, x_rows)
    agg_rows, hidden, dpre, dagg, second = dense(
        straight, turned, x_rows, picked, w_neigh, pre_self, cotangent, neigh_back
    )
    second_cols = exchange(second.reshape(groups, feat_dev, -1), "feat")
    own_rows = own_part(self_back, dpre, dagg, turned)
    weight = weight_first(dpre, agg_rows)
    second_cols, own_rows, weight = lax.optimization_barrier((second_cols, own_rows, weight))
    own_cols = exchange(own_rows.reshape(groups, feat_dev, -1), "feat")
    to_before, spread, to_after = scatter(col, second_cols)
    from_after = shifted(to_before, "node", -1)
    from_before = shifted(to_after, "node", 1)
    grad_w_neigh = weight_rest(after(weight, spread), (from_after, from_before, own_cols))
    grad_features = finish(spread, from_before, from_after, own_cols)
    return (hidden, grad_features, grad_w_neigh)


def solution(mesh):
    placed = (
        P("feat", "node"),
        P("node", None, None, None),
        P("node", None),
        P("node"),
        P(),
        P(),
        P(None, ("node", "feat")),
    )
    return jax.shard_map(
        local,
        mesh=mesh,
        in_specs=placed,
        out_specs=(P(None, ("node", "feat")), P("feat", "node"), P(("node", "feat"), None)),
        check_vma=False,
    )
```

```python
import functools

import jax
import jax.numpy as jnp
from jax import lax
from jax.experimental import pallas as pl
from jax.experimental.pallas import tpu as pltpu
from jax.sharding import PartitionSpec as P

F32 = jnp.float32
BF16 = jnp.bfloat16
NT = (((1,), (1,)), ((), ()))
NN = (((1,), (0,)), ((), ()))
MIB = 1 << 20
DENSE_MIB = 60
OWN_MIB = 60
WEIGHT_MIB = 60
FINAL_MIB = 60


def dot(a, b, dims=NN):
    return lax.dot_general(a, b, dims, preferred_element_type=F32)


def whole_params(mib):
    return pltpu.CompilerParams(vmem_limit_bytes=mib * MIB)


def params(mib):
    return pltpu.CompilerParams(
        dimension_semantics=("arbitrary",), vmem_limit_bytes=mib * MIB
    )


def split_kernel(x_hbm, out_hbm, held, in_sems, out_sems):
    width = out_hbm.shape[2]
    groups = range(out_hbm.shape[0])
    loads = [
        pltpu.make_async_copy(x_hbm.at[:, g * width : (g + 1) * width], held.at[g], in_sems.at[g])
        for g in groups
    ]
    stores = [pltpu.make_async_copy(held.at[g], out_hbm.at[g], out_sems.at[g]) for g in groups]
    for copy in loads:
        copy.start()
    for load, store in zip(loads, stores):
        load.wait()
        store.start()
    for copy in stores:
        copy.wait()


ANYWHERE = pl.BlockSpec(memory_space=pl.ANY)
SMEM = pl.BlockSpec(memory_space=pltpu.SMEM)
VMEM = pl.BlockSpec(memory_space=pltpu.VMEM)


def split_columns(x, groups):
    rows, columns = x.shape
    return pl.pallas_call(
        split_kernel,
        in_specs=[ANYWHERE],
        out_specs=ANYWHERE,
        out_shape=jax.ShapeDtypeStruct((groups, rows, columns // groups), x.dtype),
        scratch_shapes=[
            pltpu.VMEM((groups, rows, columns // groups), x.dtype),
            pltpu.SemaphoreType.DMA((groups,)),
            pltpu.SemaphoreType.DMA((groups,)),
        ],
        compiler_params=whole_params(60),
    )(x)


def gather_kernel(col_ref, before, own, after, out_hbm, sems):
    tile = 128
    blocks = own.shape[1] // tile
    per = out_hbm.shape[2] // tile

    def target(r):
        place = pl.ds(pl.multiple_of(lax.rem(r, per) * tile, tile), tile)
        return out_hbm.at[lax.div(r, per), :, place]

    def start(r, carry):
        col = col_ref[r]
        for i, part in enumerate((before, own, after)):

            @pl.when((col >= i * blocks) & (col < (i + 1) * blocks))
            def _(i=i, part=part):
                place = pl.ds(pl.multiple_of((col - i * blocks) * tile, tile), tile)
                pltpu.make_async_copy(part.at[:, place], target(r), sems.at[r]).start()

        return carry

    def wait(r, carry):
        pltpu.make_async_copy(own.at[:, :tile], target(r), sems.at[r]).wait()
        return carry

    lax.fori_loop(0, blocks, start, 0)
    lax.fori_loop(0, blocks, wait, 0)


def gather(col, before, own, after, groups):
    rows, span = own.shape
    return pl.pallas_call(
        gather_kernel,
        in_specs=[SMEM] + [ANYWHERE] * 3,
        out_specs=ANYWHERE,
        out_shape=jax.ShapeDtypeStruct((groups, rows, span // groups), BF16),
        scratch_shapes=[pltpu.SemaphoreType.DMA((col.shape[0],))],
        compiler_params=whole_params(2),
        cost_estimate=pl.CostEstimate(flops=0, bytes_accessed=8 * MIB, transcendentals=0),
    )(col, before, own, after)


def scatter_kernel(col_ref, parts_ref, before_hbm, own_hbm, after_hbm, acc, before, after, sems):
    tile = acc.shape[2]
    blocks = own_hbm.shape[0]
    per = parts_ref.shape[2] // tile

    def clear(i, carry):
        acc[i] = jnp.zeros(acc.shape[1:], F32)
        return carry

    lax.fori_loop(0, acc.shape[0], clear, 0, unroll=8)

    def add(g, carry):
        for b in range(per):
            acc[col_ref[g * per + b]] += parts_ref[g, :, b * tile : (b + 1) * tile].astype(F32)
        return carry

    lax.fori_loop(0, parts_ref.shape[0], add, 0)

    def cast(i, carry):
        before[i] = acc[i].astype(BF16)
        after[i] = acc[2 * blocks + i].astype(BF16)
        return carry

    lax.fori_loop(0, blocks, cast, 0, unroll=4)
    copies = [
        pltpu.make_async_copy(before, before_hbm, sems.at[0]),
        pltpu.make_async_copy(after, after_hbm, sems.at[1]),
        pltpu.make_async_copy(acc.at[blocks : 2 * blocks], own_hbm, sems.at[2]),
    ]
    for copy in copies:
        copy.start()
    for copy in copies:
        copy.wait()


def scatter(col, parts):
    groups, rows, width = parts.shape
    blocks = col.shape[0]
    tile = groups * width // blocks
    shape = (blocks, rows, tile)
    return pl.pallas_call(
        scatter_kernel,
        in_specs=[SMEM, VMEM],
        out_specs=[ANYWHERE] * 3,
        out_shape=[
            jax.ShapeDtypeStruct(shape, BF16),
            jax.ShapeDtypeStruct(shape, F32),
            jax.ShapeDtypeStruct(shape, BF16),
        ],
        scratch_shapes=[
            pltpu.VMEM((3 * blocks, rows, tile), F32),
            pltpu.VMEM(shape, BF16),
            pltpu.VMEM(shape, BF16),
            pltpu.SemaphoreType.DMA((3,)),
        ],
        compiler_params=whole_params(60),
        cost_estimate=pl.CostEstimate(flops=0, bytes_accessed=8 * MIB, transcendentals=0),
    )(col, parts)


def self_kernel(chunk, w_self, x_ref, pre):
    for i in range(pre.shape[0] // chunk):
        rows = slice(i * chunk, (i + 1) * chunk)
        pre[rows, :] = dot(w_self[rows, :], x_ref[...])


def self_product(w_self, x_rows):
    size, width = x_rows.shape
    return pl.pallas_call(
        functools.partial(self_kernel, 256),
        in_specs=[VMEM] * 2,
        out_specs=VMEM,
        out_shape=jax.ShapeDtypeStruct((size, width), F32),
        compiler_params=whole_params(60),
        cost_estimate=pl.CostEstimate(
            flops=2 * size * size * width, bytes_accessed=5 * MIB, transcendentals=0
        ),
    )(w_self, x_rows)


def dense_kernel(chunk, *refs):
    half_ref, sources, targets, held = refs[0], refs[1:9], refs[9:15], refs[15:23]
    (agg_hbm, hidden_hbm, dpre_hbm, dagg_hbm, second_hbm, sent_hbm) = targets
    (tiles, turned, x_ref, picked, w_neigh, pre_ref, cot_ref, w_back) = held
    (agg, hidden, dpre, dagg, second, sent, in_sems, out_sems) = refs[23:]
    size = w_neigh.shape[0]
    pair = tiles.shape[-1]
    part = [slice(i, i + chunk) for i in range(0, size, chunk)]
    here = [slice(i, i + pair) for i in range(0, agg.shape[1], pair)]
    loads = [
        pltpu.make_async_copy(sources[k], held[k], in_sems.at[k]) for k in (0, 2, 3, 4, 5, 6, 7, 1)
    ]
    for copy in loads:
        copy.start()
    stores = []

    def store(k, src, dst, i):
        copy = pltpu.make_async_copy(src.at[part[i]], dst.at[part[i]], out_sems.at[k, i])
        copy.start()
        stores.append(copy)

    for copy in loads[:3]:
        copy.wait()
    for i in range(len(part)):
        for p in range(len(here)):
            total = dot(x_ref[part[i], here[p]], tiles[0, p])
            total = total + dot(picked[part[i], here[p]], tiles[1, p])
            agg[part[i], here[p]] = total.astype(BF16)
    for copy in loads[3:6]:
        copy.wait()
    for i in range(len(part)):
        store(0, agg, agg_hbm, i)
        pre = pre_ref[part[i], :] + dot(w_neigh[part[i], :], agg[...])
        sig = 0.5 + 0.5 * jnp.tanh(0.5 * pre)
        hidden[part[i], :] = (pre * sig).astype(BF16)
        slope = sig * (1.0 + pre * (1.0 - sig))
        dpre[part[i], :] = (cot_ref[part[i], :].astype(F32) * slope).astype(BF16)
    for copy in loads[6:]:
        copy.wait()
    for i in range(len(part)):
        store(1, hidden, hidden_hbm, i)
        store(2, dpre, dpre_hbm, i)
        dagg[part[i], :] = dot(w_back[part[i], :], dpre[...]).astype(BF16)
        for p in range(len(here)):
            second[part[i], here[p]] = dot(dagg[part[i], here[p]], turned[1, p]).astype(BF16)
        store(3, dagg, dagg_hbm, i)
        store(4, second, second_hbm, i)
    width = sent.shape[1]
    half = agg.at[pl.ds(pl.multiple_of(half_ref[0] * width, width), width)]
    for i in range(len(part)):
        sent[part[i], :] = dot(dpre[part[i], :], half[...], NT).astype(BF16)
        store(5, sent, sent_hbm, i)
    for copy in stores:
        copy.wait()


def dense(half, tiles, turned, x_rows, picked, w_neigh, pre_self, cot, w_back):
    size, width = picked.shape
    chunk = 256
    out = jax.ShapeDtypeStruct((size, width), BF16)
    args = (tiles, turned, x_rows, picked, w_neigh, pre_self, cot, w_back)
    return pl.pallas_call(
        functools.partial(dense_kernel, chunk),
        in_specs=[SMEM] + [ANYWHERE] * len(args),
        out_specs=[ANYWHERE] * 6,
        out_shape=[out] * 5 + [jax.ShapeDtypeStruct((size, size // CORES), BF16)],
        scratch_shapes=[pltpu.VMEM(arg.shape, arg.dtype) for arg in args]
        + [pltpu.VMEM((size, width), BF16)] * 5
        + [pltpu.VMEM((size, size // CORES), BF16)]
        + [pltpu.SemaphoreType.DMA((len(args),)), pltpu.SemaphoreType.DMA((6, size // chunk))],
        compiler_params=whole_params(DENSE_MIB),
        cost_estimate=pl.CostEstimate(
            flops=4 * size * size * width, bytes_accessed=16 * MIB, transcendentals=size * width
        ),
    )(half, *args)


EXTRA = 8


def own_kernel(chunk, w_back, dpre, dagg_ref, turned, own):
    pair = turned.shape[-1]
    each = own.shape[1] - EXTRA
    for i in range(0, dpre.shape[0], chunk):
        rows = slice(i, i + chunk)
        dself = dot(w_back[rows, :], dpre[...])
        for p in range(own.shape[2] // pair):
            here = slice(p * pair, (p + 1) * pair)
            total = dself[:, here] + dot(dagg_ref[rows, here], turned[0, p])
            for g in range(chunk // each):
                own[i // each + g, :each, here] = total[g * each : (g + 1) * each].astype(BF16)


def own_part(w_back, dpre, dagg, turned, groups):
    size, width = dpre.shape
    return pl.pallas_call(
        functools.partial(own_kernel, 256),
        in_specs=[VMEM] * 4,
        out_specs=VMEM,
        out_shape=jax.ShapeDtypeStruct((groups, size // groups + EXTRA, width), BF16),
        compiler_params=whole_params(OWN_MIB),
        cost_estimate=pl.CostEstimate(
            flops=2 * size * size * width, bytes_accessed=5 * MIB, transcendentals=0
        ),
    )(w_back, dpre, dagg, turned)


def weight_kernel(index_ref, dpre, agg_ref, other_ref, *outs):
    core, me = index_ref[0], index_ref[1]
    rows, width = outs[0].shape
    half = agg_ref.at[pl.ds(pl.multiple_of(core * width, width), width)]
    for step, out in enumerate(outs):
        here = pl.ds(pl.multiple_of(lax.rem(me + step, len(outs)) * rows, rows), rows)
        total = dot(dpre[here, :], half[...], NT) + other_ref[here, :].astype(F32)
        out[...] = total.astype(out.dtype)


def weight_pieces(core, me, dpre, agg_rows, other):
    size, width = dpre.shape
    shape = (size // SIDE, size // CORES)
    return pl.pallas_call(
        weight_kernel,
        in_specs=[SMEM] + [VMEM] * 3,
        out_specs=[VMEM] * SIDE,
        out_shape=[jax.ShapeDtypeStruct(shape, F32)]
        + [jax.ShapeDtypeStruct(shape, BF16)] * (SIDE - 1),
        compiler_params=whole_params(WEIGHT_MIB),
        cost_estimate=pl.CostEstimate(
            flops=size * size * width, bytes_accessed=4 * MIB, transcendentals=0
        ),
    )(jnp.stack([core, me]), dpre, agg_rows, other)


def add_kernel(index_ref, *refs):
    parts, outs = refs[:SIDE], refs[SIDE:]
    rows = outs[0].shape[0]
    for step, out in enumerate(outs):
        here = pl.ds(pl.multiple_of(lax.rem(index_ref[0] + step, SIDE) * rows, rows), rows)
        total = parts[0][here, :]
        for part in parts[1:]:
            total = total + part[here, :].astype(F32)
        out[...] = total.astype(out.dtype)


def added_pieces(me, parts):
    rows, width = parts[0].shape
    shape = (rows // SIDE, width)
    return pl.pallas_call(
        add_kernel,
        in_specs=[SMEM] + [VMEM] * SIDE,
        out_specs=[VMEM] * SIDE,
        out_shape=[jax.ShapeDtypeStruct(shape, F32)]
        + [jax.ShapeDtypeStruct(shape, BF16)] * (SIDE - 1),
        compiler_params=whole_params(WEIGHT_MIB),
        cost_estimate=pl.CostEstimate(flops=0, bytes_accessed=2 * MIB, transcendentals=0),
    )(me[None], *parts)


def final_kernel(own_ref, before_ref, after_ref, dself_ref, out_ref):
    tile = own_ref.shape[2]
    per = dself_ref.shape[2] // tile
    for b in range(own_ref.shape[0]):
        grad = dself_ref[b // per, : own_ref.shape[1], (b % per) * tile : (b % per + 1) * tile]
        total = own_ref[b] + before_ref[b].astype(F32) + after_ref[b].astype(F32)
        out_ref[:, b * tile : (b + 1) * tile] = (grad.astype(F32) + total).astype(BF16)


def finish(own, before, after, dself):
    groups, high, width = dself.shape
    blocks, rows, tile = own.shape
    steps = 4
    part = pl.BlockSpec((blocks // steps, rows, tile), lambda g: (g, 0, 0))
    return pl.pallas_call(
        final_kernel,
        grid=(steps,),
        in_specs=[part, part, part]
        + [pl.BlockSpec((groups // steps, high, width), lambda g: (g, 0, 0))],
        out_specs=pl.BlockSpec((rows, groups * width // steps), lambda g: (0, g)),
        out_shape=jax.ShapeDtypeStruct((rows, groups * width), BF16),
        compiler_params=params(FINAL_MIB),
    )(own, before, after, dself)


def shifted(value, axis, steps):
    count = lax.axis_size(axis)
    first, last = max(0, -steps), min(count, count - steps)
    return lax.ppermute(value, axis, [(source, source + steps) for source in range(first, last)])


def exchange(value, axis):
    return lax.all_to_all(value, axis, split_axis=0, concat_axis=0, tiled=True)


SIDE = 4
CORES = 2


def sent_round(pieces, axis, partner):
    count = lax.axis_size(axis)
    return [pieces[0]] + [
        lax.ppermute(piece, axis, [(i, partner(i, step + 1)) for i in range(count)])
        for step, piece in enumerate(pieces[1:])
    ]


def weight_rows(sent, dpre, agg_rows, groups):
    feat, node = lax.axis_index("feat"), lax.axis_index("node")
    other = lax.ppermute(sent, "feat", [(i, i ^ 1) for i in range(groups)])
    pieces = weight_pieces(lax.rem(feat, CORES), lax.div(node, SIDE), dpre, agg_rows, other)
    parts = sent_round(pieces, "node", lambda i, s: (i + s * SIDE) % (SIDE * SIDE))
    pieces = added_pieces(lax.rem(node, SIDE), parts)
    parts = sent_round(pieces, "node", lambda i, s: i // SIDE * SIDE + (i + s) % SIDE)
    total = parts[0]
    for part in parts[1:]:
        total = total + part.astype(F32)
    total = total.reshape(groups, EXTRA // 2, -1)
    high = total.astype(BF16)
    low = (total - high.astype(F32)).astype(BF16)
    return jnp.concatenate([high, low], axis=1)


def weight_total(rows):
    groups, count, width = rows.shape
    rows = rows.astype(F32).reshape(groups // CORES, CORES, 2, count // 2, width)
    total = jnp.sum(rows, axis=(0, 2))
    return jnp.concatenate([total[i] for i in range(CORES)], axis=1)


def paired(tiles):
    blocks, tile, _ = tiles.shape
    tiles = tiles.reshape(blocks // 2, 2, tile, tile)
    empty = jnp.zeros_like(tiles[:, 0])
    upper = jnp.concatenate([tiles[:, 0], empty], axis=2)
    lower = jnp.concatenate([empty, tiles[:, 1]], axis=2)
    return jnp.concatenate([upper, lower], axis=1)


def local(features, tile_values, tile_cols, tile_count, w_self, w_neigh, cotangent):
    feat_dev, node_dev = features.shape
    tile = tile_values.shape[-1]
    block_count = node_dev // tile
    groups = lax.axis_size("feat")
    size = w_self.shape[0]
    part, feat = lax.axis_index("node"), lax.axis_index("feat")
    col = tile_cols[:, 1] - (part - 1) * block_count
    mine = block_count // groups
    live = lax.dynamic_slice_in_dim(tile_count, feat * mine, mine) > 1
    tiles = lax.dynamic_slice_in_dim(tile_values, feat * mine, mine)
    other = jnp.where(live[:, None, None], tiles[:, 1], jnp.zeros_like(tiles[:, 1]))
    straight = jnp.stack([paired(tiles[:, 0]), paired(other)])
    turned = straight.swapaxes(2, 3)

    before = shifted(features, "node", 1)
    behind = shifted(features, "node", -1)
    x_rows = exchange(split_columns(features, groups), "feat").reshape(size, -1)
    picked = exchange(gather(col, before, features, behind, groups), "feat").reshape(size, -1)
    x_rows, self_back, neigh_back, straight, turned = lax.optimization_barrier(
        (x_rows, w_self.T, w_neigh.T, straight, turned)
    )
    pre_self = self_product(w_self, x_rows)
    core = lax.rem(feat, CORES)
    agg_rows, hidden, dpre, dagg, second, sent = dense(
        1 - core[None], straight, turned, x_rows, picked, w_neigh, pre_self, cotangent, neigh_back
    )
    second_cols = exchange(second.reshape(groups, feat_dev, -1), "feat")
    own_rows = own_part(self_back, dpre, dagg, turned, groups)
    weight = weight_rows(sent, dpre, agg_rows, groups)
    own_rows = lax.dynamic_update_slice(own_rows, weight, (0, feat_dev, 0))
    own_cols = exchange(own_rows, "feat")
    to_before, spread, to_after = scatter(col, second_cols)
    from_after = shifted(to_before, "node", -1)
    from_before = shifted(to_after, "node", 1)
    grad_w_neigh = weight_total(own_cols[:, feat_dev:])
    grad_features = finish(spread, from_before, from_after, own_cols)
    return (hidden, grad_features, grad_w_neigh)


def solution(mesh):
    placed = (
        P("feat", "node"),
        P("node", None, None, None),
        P("node", None),
        P("node"),
        P(),
        P(),
        P(None, ("node", "feat")),
    )
    return jax.shard_map(
        local,
        mesh=mesh,
        in_specs=placed,
        out_specs=(P(None, ("node", "feat")), P("feat", "node"), P(("node", "feat"), None)),
        check_vma=False,
    )
```

```python
import functools

import jax
import jax.numpy as jnp
from jax import lax
from jax.experimental import pallas as pl
from jax.experimental.pallas import tpu as pltpu
from jax.sharding import PartitionSpec as P

F32 = jnp.float32
BF16 = jnp.bfloat16
NT = (((1,), (1,)), ((), ()))
NN = (((1,), (0,)), ((), ()))
MIB = 1 << 20
DENSE_MIB = 56
OWN_MIB = 60
WEIGHT_MIB = 60
FINAL_MIB = 50
SCATTER_MIB = 56
CHUNK = 512


def dot(a, b, dims=NN):
    return lax.dot_general(a, b, dims, preferred_element_type=F32)


def whole_params(mib):
    return pltpu.CompilerParams(vmem_limit_bytes=mib * MIB)


def params(mib):
    return pltpu.CompilerParams(
        dimension_semantics=("arbitrary",), vmem_limit_bytes=mib * MIB
    )


def split_kernel(x_hbm, out_hbm, held, in_sems, out_sems):
    width = out_hbm.shape[2]
    groups = range(out_hbm.shape[0])
    loads = [
        pltpu.make_async_copy(x_hbm.at[:, g * width : (g + 1) * width], held.at[g], in_sems.at[g])
        for g in groups
    ]
    stores = [pltpu.make_async_copy(held.at[g], out_hbm.at[g], out_sems.at[g]) for g in groups]
    for copy in loads:
        copy.start()
    for load, store in zip(loads, stores):
        load.wait()
        store.start()
    for copy in stores:
        copy.wait()


ANYWHERE = pl.BlockSpec(memory_space=pl.ANY)
SMEM = pl.BlockSpec(memory_space=pltpu.SMEM)
VMEM = pl.BlockSpec(memory_space=pltpu.VMEM)


def split_columns(x, groups):
    rows, columns = x.shape
    return pl.pallas_call(
        split_kernel,
        in_specs=[ANYWHERE],
        out_specs=ANYWHERE,
        out_shape=jax.ShapeDtypeStruct((groups, rows, columns // groups), x.dtype),
        scratch_shapes=[
            pltpu.VMEM((groups, rows, columns // groups), x.dtype),
            pltpu.SemaphoreType.DMA((groups,)),
            pltpu.SemaphoreType.DMA((groups,)),
        ],
        compiler_params=whole_params(60),
    )(x)


def gather_kernel(col_ref, before, own, after, out_hbm, sems):
    tile = 128
    blocks = own.shape[1] // tile
    per = out_hbm.shape[2] // tile

    def target(r):
        place = pl.ds(pl.multiple_of(lax.rem(r, per) * tile, tile), tile)
        return out_hbm.at[lax.div(r, per), :, place]

    def start(r, carry):
        col = col_ref[r]
        for i, part in enumerate((before, own, after)):

            @pl.when((col >= i * blocks) & (col < (i + 1) * blocks))
            def _(i=i, part=part):
                place = pl.ds(pl.multiple_of((col - i * blocks) * tile, tile), tile)
                pltpu.make_async_copy(part.at[:, place], target(r), sems.at[r]).start()

        return carry

    def wait(r, carry):
        pltpu.make_async_copy(own.at[:, :tile], target(r), sems.at[r]).wait()
        return carry

    lax.fori_loop(0, blocks, start, 0)
    lax.fori_loop(0, blocks, wait, 0)


def gather(col, before, own, after, groups):
    rows, span = own.shape
    return pl.pallas_call(
        gather_kernel,
        in_specs=[SMEM] + [ANYWHERE] * 3,
        out_specs=ANYWHERE,
        out_shape=jax.ShapeDtypeStruct((groups, rows, span // groups), BF16),
        scratch_shapes=[pltpu.SemaphoreType.DMA((col.shape[0],))],
        compiler_params=whole_params(2),
        cost_estimate=pl.CostEstimate(flops=0, bytes_accessed=8 * MIB, transcendentals=0),
    )(col, before, own, after)


def scatter_kernel(
    col_ref, parts_hbm, before_hbm, own_hbm, after_hbm, parts_ref, acc, before, after, load_sem, sems
):
    tile = acc.shape[2]
    blocks = own_hbm.shape[0]
    per = parts_ref.shape[2] // tile
    load = pltpu.make_async_copy(parts_hbm, parts_ref, load_sem)
    load.start()

    def clear(i, carry):
        acc[i] = jnp.zeros(acc.shape[1:], F32)
        return carry

    lax.fori_loop(0, acc.shape[0], clear, 0, unroll=8)
    load.wait()

    def add(g, carry):
        for b in range(per):
            acc[col_ref[g * per + b]] += parts_ref[g, :, b * tile : (b + 1) * tile].astype(F32)
        return carry

    lax.fori_loop(0, parts_ref.shape[0], add, 0, unroll=2)
    copies = [
        pltpu.make_async_copy(acc.at[blocks : 2 * blocks], own_hbm, sems.at[0]),
        pltpu.make_async_copy(before, before_hbm, sems.at[1]),
        pltpu.make_async_copy(after, after_hbm, sems.at[2]),
    ]
    copies[0].start()
    for first, out, copy in ((0, before, copies[1]), (2 * blocks, after, copies[2])):

        def cast(i, carry, first=first, out=out):
            out[i] = acc[first + i].astype(BF16)
            return carry

        lax.fori_loop(0, blocks, cast, 0, unroll=8)
        copy.start()
    for copy in copies:
        copy.wait()


def scatter(col, parts):
    groups, rows, width = parts.shape
    blocks = col.shape[0]
    tile = groups * width // blocks
    shape = (blocks, rows, tile)
    return pl.pallas_call(
        scatter_kernel,
        in_specs=[SMEM, ANYWHERE],
        out_specs=[ANYWHERE] * 3,
        out_shape=[
            jax.ShapeDtypeStruct(shape, BF16),
            jax.ShapeDtypeStruct(shape, F32),
            jax.ShapeDtypeStruct(shape, BF16),
        ],
        scratch_shapes=[
            pltpu.VMEM(parts.shape, BF16),
            pltpu.VMEM((3 * blocks, rows, tile), F32),
            pltpu.VMEM(shape, BF16),
            pltpu.VMEM(shape, BF16),
            pltpu.SemaphoreType.DMA(()),
            pltpu.SemaphoreType.DMA((3,)),
        ],
        compiler_params=whole_params(SCATTER_MIB),
        cost_estimate=pl.CostEstimate(flops=0, bytes_accessed=8 * MIB, transcendentals=0),
    )(col, parts)


def self_kernel(chunk, w_self, x_ref, pre):
    for i in range(pre.shape[0] // chunk):
        rows = slice(i * chunk, (i + 1) * chunk)
        pre[rows, :] = dot(w_self[rows, :], x_ref[...])


def self_product(w_self, x_rows):
    size, width = x_rows.shape
    return pl.pallas_call(
        functools.partial(self_kernel, 256),
        in_specs=[VMEM] * 2,
        out_specs=VMEM,
        out_shape=jax.ShapeDtypeStruct((size, width), F32),
        compiler_params=whole_params(60),
        cost_estimate=pl.CostEstimate(
            flops=2 * size * size * width, bytes_accessed=5 * MIB, transcendentals=0
        ),
    )(w_self, x_rows)


def dense_kernel(chunk, *refs):
    half_ref, sources, targets, held = refs[0], refs[1:9], refs[9:15], refs[15:23]
    (agg_hbm, hidden_hbm, dpre_hbm, dagg_hbm, second_hbm, sent_hbm) = targets
    (tiles, turned, x_ref, picked, w_neigh, pre_ref, cot_ref, w_back) = held
    (agg, hidden, dpre, dagg, second, sent, in_sems, out_sems) = refs[23:]
    size = w_neigh.shape[0]
    pair = tiles.shape[-1]
    part = [slice(i, i + chunk) for i in range(0, size, chunk)]
    here = [slice(i, i + pair) for i in range(0, agg.shape[1], pair)]
    loads = [
        pltpu.make_async_copy(sources[k], held[k], in_sems.at[k]) for k in (0, 2, 3, 4, 5, 6, 7, 1)
    ]
    for copy in loads:
        copy.start()
    stores = []

    def store(k, src, dst, i):
        copy = pltpu.make_async_copy(src.at[part[i]], dst.at[part[i]], out_sems.at[k, i])
        copy.start()
        stores.append(copy)

    for copy in loads[:3]:
        copy.wait()
    for i in range(len(part)):
        for p in range(len(here)):
            total = dot(x_ref[part[i], here[p]], tiles[0, p])
            total = total + dot(picked[part[i], here[p]], tiles[1, p])
            agg[part[i], here[p]] = total.astype(BF16)
    for copy in loads[3:6]:
        copy.wait()
    for i in range(len(part)):
        store(0, agg, agg_hbm, i)
        pre = pre_ref[part[i], :] + dot(w_neigh[part[i], :], agg[...])
        sig = 0.5 + 0.5 * jnp.tanh(0.5 * pre)
        hidden[part[i], :] = (pre * sig).astype(BF16)
        slope = sig * (1.0 + pre * (1.0 - sig))
        dpre[part[i], :] = (cot_ref[part[i], :].astype(F32) * slope).astype(BF16)
    for copy in loads[6:]:
        copy.wait()
    for i in range(len(part)):
        store(1, hidden, hidden_hbm, i)
        store(2, dpre, dpre_hbm, i)
        dagg[part[i], :] = dot(w_back[part[i], :], dpre[...]).astype(BF16)
        for p in range(len(here)):
            second[part[i], here[p]] = dot(dagg[part[i], here[p]], turned[1, p]).astype(BF16)
        store(3, dagg, dagg_hbm, i)
        store(4, second, second_hbm, i)
    width = sent.shape[1]
    half = agg.at[pl.ds(pl.multiple_of(half_ref[0] * width, width), width)]
    for i in range(len(part)):
        sent[part[i], :] = dot(dpre[part[i], :], half[...], NT).astype(BF16)
        store(5, sent, sent_hbm, i)
    for copy in stores:
        copy.wait()


def dense(half, tiles, turned, x_rows, picked, w_neigh, pre_self, cot, w_back):
    size, width = picked.shape
    chunk = CHUNK
    out = jax.ShapeDtypeStruct((size, width), BF16)
    args = (tiles, turned, x_rows, picked, w_neigh, pre_self, cot, w_back)
    return pl.pallas_call(
        functools.partial(dense_kernel, chunk),
        in_specs=[SMEM] + [ANYWHERE] * len(args),
        out_specs=[ANYWHERE] * 6,
        out_shape=[out] * 5 + [jax.ShapeDtypeStruct((size, size // CORES), BF16)],
        scratch_shapes=[pltpu.VMEM(arg.shape, arg.dtype) for arg in args]
        + [pltpu.VMEM((size, width), BF16)] * 5
        + [pltpu.VMEM((size, size // CORES), BF16)]
        + [pltpu.SemaphoreType.DMA((len(args),)), pltpu.SemaphoreType.DMA((6, size // chunk))],
        compiler_params=whole_params(DENSE_MIB),
        cost_estimate=pl.CostEstimate(
            flops=4 * size * size * width, bytes_accessed=16 * MIB, transcendentals=size * width
        ),
    )(half, *args)


EXTRA = 8


def own_kernel(chunk, w_back, dpre, dagg_ref, turned, own):
    pair = turned.shape[-1]
    each = own.shape[1] - EXTRA
    for i in range(0, dpre.shape[0], chunk):
        rows = slice(i, i + chunk)
        dself = dot(w_back[rows, :], dpre[...])
        for p in range(own.shape[2] // pair):
            here = slice(p * pair, (p + 1) * pair)
            total = dself[:, here] + dot(dagg_ref[rows, here], turned[0, p])
            for g in range(chunk // each):
                own[i // each + g, :each, here] = total[g * each : (g + 1) * each].astype(BF16)


def own_part(w_back, dpre, dagg, turned, groups):
    size, width = dpre.shape
    return pl.pallas_call(
        functools.partial(own_kernel, 256),
        in_specs=[VMEM] * 4,
        out_specs=VMEM,
        out_shape=jax.ShapeDtypeStruct((groups, size // groups + EXTRA, width), BF16),
        compiler_params=whole_params(OWN_MIB),
        cost_estimate=pl.CostEstimate(
            flops=2 * size * size * width, bytes_accessed=5 * MIB, transcendentals=0
        ),
    )(w_back, dpre, dagg, turned)


def weight_kernel(index_ref, dpre, agg_ref, other_ref, *outs):
    core, me = index_ref[0], index_ref[1]
    rows, width = outs[0].shape
    half = agg_ref.at[pl.ds(pl.multiple_of(core * width, width), width)]
    for step, out in enumerate(outs):
        here = pl.ds(pl.multiple_of(lax.rem(me + step, len(outs)) * rows, rows), rows)
        total = dot(dpre[here, :], half[...], NT) + other_ref[here, :].astype(F32)
        out[...] = total.astype(out.dtype)


def weight_pieces(core, me, dpre, agg_rows, other):
    size, width = dpre.shape
    shape = (size // SIDE, size // CORES)
    return pl.pallas_call(
        weight_kernel,
        in_specs=[SMEM] + [VMEM] * 3,
        out_specs=[VMEM] * SIDE,
        out_shape=[jax.ShapeDtypeStruct(shape, F32)]
        + [jax.ShapeDtypeStruct(shape, BF16)] * (SIDE - 1),
        compiler_params=whole_params(WEIGHT_MIB),
        cost_estimate=pl.CostEstimate(
            flops=size * size * width, bytes_accessed=4 * MIB, transcendentals=0
        ),
    )(jnp.stack([core, me]), dpre, agg_rows, other)


def add_kernel(index_ref, *refs):
    parts, outs = refs[:SIDE], refs[SIDE:]
    rows = outs[0].shape[0]
    for step, out in enumerate(outs):
        here = pl.ds(pl.multiple_of(lax.rem(index_ref[0] + step, SIDE) * rows, rows), rows)
        total = parts[0][here, :]
        for part in parts[1:]:
            total = total + part[here, :].astype(F32)
        out[...] = total.astype(out.dtype)


def added_pieces(me, parts):
    rows, width = parts[0].shape
    shape = (rows // SIDE, width)
    return pl.pallas_call(
        add_kernel,
        in_specs=[SMEM] + [VMEM] * SIDE,
        out_specs=[VMEM] * SIDE,
        out_shape=[jax.ShapeDtypeStruct(shape, F32)]
        + [jax.ShapeDtypeStruct(shape, BF16)] * (SIDE - 1),
        compiler_params=whole_params(WEIGHT_MIB),
        cost_estimate=pl.CostEstimate(flops=0, bytes_accessed=2 * MIB, transcendentals=0),
    )(me[None], *parts)


def final_kernel(own_ref, before_ref, after_ref, dself_ref, out_ref):
    tile = own_ref.shape[2]
    per = dself_ref.shape[2] // tile
    for b in range(own_ref.shape[0]):
        grad = dself_ref[b // per, : own_ref.shape[1], (b % per) * tile : (b % per + 1) * tile]
        total = own_ref[b] + before_ref[b].astype(F32) + after_ref[b].astype(F32)
        out_ref[:, b * tile : (b + 1) * tile] = (grad.astype(F32) + total).astype(BF16)


def finish(own, before, after, dself):
    groups, high, width = dself.shape
    blocks, rows, tile = own.shape
    steps = 4
    part = pl.BlockSpec((blocks // steps, rows, tile), lambda g: (g, 0, 0))
    return pl.pallas_call(
        final_kernel,
        grid=(steps,),
        in_specs=[part, part, part]
        + [pl.BlockSpec((groups // steps, high, width), lambda g: (g, 0, 0))],
        out_specs=pl.BlockSpec((rows, groups * width // steps), lambda g: (0, g)),
        out_shape=jax.ShapeDtypeStruct((rows, groups * width), BF16),
        compiler_params=params(FINAL_MIB),
    )(own, before, after, dself)


def shifted(value, axis, steps):
    count = lax.axis_size(axis)
    first, last = max(0, -steps), min(count, count - steps)
    return lax.ppermute(value, axis, [(source, source + steps) for source in range(first, last)])


def exchange(value, axis):
    return lax.all_to_all(value, axis, split_axis=0, concat_axis=0, tiled=True)


SIDE = 4
CORES = 2


def sent_round(pieces, axis, partner):
    count = lax.axis_size(axis)
    return [pieces[0]] + [
        lax.ppermute(piece, axis, [(i, partner(i, step + 1)) for i in range(count)])
        for step, piece in enumerate(pieces[1:])
    ]


def weight_rows(sent, dpre, agg_rows, groups, own_rows):
    feat, node = lax.axis_index("feat"), lax.axis_index("node")
    other = lax.ppermute(sent, "feat", [(i, i ^ 1) for i in range(groups)])
    pieces = weight_pieces(lax.rem(feat, CORES), lax.div(node, SIDE), dpre, agg_rows, other)
    parts = sent_round(pieces, "node", lambda i, s: (i + s * SIDE) % (SIDE * SIDE))
    parts, own_rows = lax.optimization_barrier((parts, own_rows))
    pieces = added_pieces(lax.rem(node, SIDE), parts)
    parts = sent_round(pieces, "node", lambda i, s: i // SIDE * SIDE + (i + s) % SIDE)
    total = parts[0]
    for part in parts[1:]:
        total = total + part.astype(F32)
    total = total.reshape(groups, EXTRA // 2, -1)
    high = total.astype(BF16)
    low = (total - high.astype(F32)).astype(BF16)
    rows = jnp.concatenate([high, low], axis=1)
    return lax.dynamic_update_slice(own_rows, rows, (0, own_rows.shape[1] - EXTRA, 0))


def weight_total(rows):
    groups, count, width = rows.shape
    rows = rows.astype(F32).reshape(groups // CORES, CORES, 2, count // 2, width)
    total = jnp.sum(rows, axis=(0, 2))
    return jnp.concatenate([total[i] for i in range(CORES)], axis=1)


def paired(tiles):
    blocks, tile, _ = tiles.shape
    tiles = tiles.reshape(blocks // 2, 2, tile, tile)
    empty = jnp.zeros_like(tiles[:, 0])
    upper = jnp.concatenate([tiles[:, 0], empty], axis=2)
    lower = jnp.concatenate([empty, tiles[:, 1]], axis=2)
    return jnp.concatenate([upper, lower], axis=1)


def local(features, tile_values, tile_cols, tile_count, w_self, w_neigh, cotangent):
    feat_dev, node_dev = features.shape
    tile = tile_values.shape[-1]
    block_count = node_dev // tile
    groups = lax.axis_size("feat")
    size = w_self.shape[0]
    part, feat = lax.axis_index("node"), lax.axis_index("feat")
    col = tile_cols[:, 1] - (part - 1) * block_count
    mine = block_count // groups
    live = lax.dynamic_slice_in_dim(tile_count, feat * mine, mine) > 1
    tiles = lax.dynamic_slice_in_dim(tile_values, feat * mine, mine)
    other = jnp.where(live[:, None, None], tiles[:, 1], jnp.zeros_like(tiles[:, 1]))
    straight = jnp.stack([paired(tiles[:, 0]), paired(other)])
    turned = straight.swapaxes(2, 3)

    before = shifted(features, "node", 1)
    behind = shifted(features, "node", -1)
    x_rows = exchange(split_columns(features, groups), "feat").reshape(size, -1)
    picked = exchange(gather(col, before, features, behind, groups), "feat").reshape(size, -1)
    x_rows, self_back, neigh_back, straight, turned = lax.optimization_barrier(
        (x_rows, w_self.T, w_neigh.T, straight, turned)
    )
    pre_self = self_product(w_self, x_rows)
    core = lax.rem(feat, CORES)
    agg_rows, hidden, dpre, dagg, second, sent = dense(
        1 - core[None], straight, turned, x_rows, picked, w_neigh, pre_self, cotangent, neigh_back
    )
    second_cols = exchange(second.reshape(groups, feat_dev, -1), "feat")
    own_rows = own_part(self_back, dpre, dagg, turned, groups)
    own_cols = exchange(weight_rows(sent, dpre, agg_rows, groups, own_rows), "feat")
    to_before, spread, to_after = scatter(col, second_cols)
    from_after = shifted(to_before, "node", -1)
    from_before = shifted(to_after, "node", 1)
    grad_w_neigh = weight_total(own_cols[:, feat_dev:])
    grad_features = finish(spread, from_before, from_after, own_cols)
    return (hidden, grad_features, grad_w_neigh)


def solution(mesh):
    placed = (
        P("feat", "node"),
        P("node", None, None, None),
        P("node", None),
        P("node"),
        P(),
        P(),
        P(None, ("node", "feat")),
    )
    return jax.shard_map(
        local,
        mesh=mesh,
        in_specs=placed,
        out_specs=(P(None, ("node", "feat")), P("feat", "node"), P(("node", "feat"), None)),
        check_vma=False,
    )
```

```python
import functools

import jax
import jax.numpy as jnp
from jax import lax
from jax.experimental import pallas as pl
from jax.experimental.pallas import tpu as pltpu
from jax.sharding import PartitionSpec as P

F32 = jnp.float32
BF16 = jnp.bfloat16
NT = (((1,), (1,)), ((), ()))
NN = (((1,), (0,)), ((), ()))
MIB = 1 << 20
DENSE_MIB = 56
OWN_MIB = 60
WEIGHT_MIB = 60
FINAL_MIB = 50
SCATTER_MIB = 56
CHUNK = 512


def dot(a, b, dims=NN):
    return lax.dot_general(a, b, dims, preferred_element_type=F32)


def whole_params(mib):
    return pltpu.CompilerParams(vmem_limit_bytes=mib * MIB)


def params(mib):
    return pltpu.CompilerParams(
        dimension_semantics=("arbitrary",), vmem_limit_bytes=mib * MIB
    )


def split_kernel(x_hbm, out_hbm, held, in_sems, out_sems):
    width = out_hbm.shape[2]
    groups = range(out_hbm.shape[0])
    loads = [
        pltpu.make_async_copy(x_hbm.at[:, g * width : (g + 1) * width], held.at[g], in_sems.at[g])
        for g in groups
    ]
    stores = [pltpu.make_async_copy(held.at[g], out_hbm.at[g], out_sems.at[g]) for g in groups]
    for copy in loads:
        copy.start()
    for load, store in zip(loads, stores):
        load.wait()
        store.start()
    for copy in stores:
        copy.wait()


ANYWHERE = pl.BlockSpec(memory_space=pl.ANY)
SMEM = pl.BlockSpec(memory_space=pltpu.SMEM)
VMEM = pl.BlockSpec(memory_space=pltpu.VMEM)


def split_columns(x, groups):
    rows, columns = x.shape
    return pl.pallas_call(
        split_kernel,
        in_specs=[ANYWHERE],
        out_specs=ANYWHERE,
        out_shape=jax.ShapeDtypeStruct((groups, rows, columns // groups), x.dtype),
        scratch_shapes=[
            pltpu.VMEM((groups, rows, columns // groups), x.dtype),
            pltpu.SemaphoreType.DMA((groups,)),
            pltpu.SemaphoreType.DMA((groups,)),
        ],
        compiler_params=whole_params(60),
    )(x)


def gather_kernel(col_ref, before, own, after, out_hbm, sems):
    tile = 128
    blocks = own.shape[1] // tile
    per = out_hbm.shape[2] // tile

    def target(r):
        place = pl.ds(pl.multiple_of(lax.rem(r, per) * tile, tile), tile)
        return out_hbm.at[lax.div(r, per), :, place]

    def start(r, carry):
        col = col_ref[r]
        for i, part in enumerate((before, own, after)):

            @pl.when((col >= i * blocks) & (col < (i + 1) * blocks))
            def _(i=i, part=part):
                place = pl.ds(pl.multiple_of((col - i * blocks) * tile, tile), tile)
                pltpu.make_async_copy(part.at[:, place], target(r), sems.at[r]).start()

        return carry

    def wait(r, carry):
        pltpu.make_async_copy(own.at[:, :tile], target(r), sems.at[r]).wait()
        return carry

    lax.fori_loop(0, blocks, start, 0)
    lax.fori_loop(0, blocks, wait, 0)


def gather(col, before, own, after, groups):
    rows, span = own.shape
    return pl.pallas_call(
        gather_kernel,
        in_specs=[SMEM] + [ANYWHERE] * 3,
        out_specs=ANYWHERE,
        out_shape=jax.ShapeDtypeStruct((groups, rows, span // groups), BF16),
        scratch_shapes=[pltpu.SemaphoreType.DMA((col.shape[0],))],
        compiler_params=whole_params(2),
        cost_estimate=pl.CostEstimate(flops=0, bytes_accessed=8 * MIB, transcendentals=0),
    )(col, before, own, after)


def scatter_kernel(
    col_ref, parts_hbm, before_hbm, own_hbm, after_hbm, parts_ref, acc, before, after, load_sem, sems
):
    tile = acc.shape[2]
    blocks = own_hbm.shape[0]
    per = parts_ref.shape[2] // tile
    load = pltpu.make_async_copy(parts_hbm, parts_ref, load_sem)
    load.start()

    def clear(i, carry):
        acc[i] = jnp.zeros(acc.shape[1:], F32)
        return carry

    lax.fori_loop(0, acc.shape[0], clear, 0, unroll=8)
    load.wait()

    def add(g, carry):
        for b in range(per):
            acc[col_ref[g * per + b]] += parts_ref[g, :, b * tile : (b + 1) * tile].astype(F32)
        return carry

    lax.fori_loop(0, parts_ref.shape[0], add, 0, unroll=2)
    copies = [
        pltpu.make_async_copy(acc.at[blocks : 2 * blocks], own_hbm, sems.at[0]),
        pltpu.make_async_copy(before, before_hbm, sems.at[1]),
        pltpu.make_async_copy(after, after_hbm, sems.at[2]),
    ]
    copies[0].start()
    for first, out, copy in ((0, before, copies[1]), (2 * blocks, after, copies[2])):

        def cast(i, carry, first=first, out=out):
            out[i] = acc[first + i].astype(BF16)
            return carry

        lax.fori_loop(0, blocks, cast, 0, unroll=8)
        copy.start()
    for copy in copies:
        copy.wait()


def scatter(col, parts):
    groups, rows, width = parts.shape
    blocks = col.shape[0]
    tile = groups * width // blocks
    shape = (blocks, rows, tile)
    return pl.pallas_call(
        scatter_kernel,
        in_specs=[SMEM, ANYWHERE],
        out_specs=[ANYWHERE] * 3,
        out_shape=[
            jax.ShapeDtypeStruct(shape, BF16),
            jax.ShapeDtypeStruct(shape, F32),
            jax.ShapeDtypeStruct(shape, BF16),
        ],
        scratch_shapes=[
            pltpu.VMEM(parts.shape, BF16),
            pltpu.VMEM((3 * blocks, rows, tile), F32),
            pltpu.VMEM(shape, BF16),
            pltpu.VMEM(shape, BF16),
            pltpu.SemaphoreType.DMA(()),
            pltpu.SemaphoreType.DMA((3,)),
        ],
        compiler_params=whole_params(SCATTER_MIB),
        cost_estimate=pl.CostEstimate(flops=0, bytes_accessed=8 * MIB, transcendentals=0),
    )(col, parts)


def self_kernel(chunk, w_self, x_ref, pre):
    for i in range(pre.shape[0] // chunk):
        rows = slice(i * chunk, (i + 1) * chunk)
        pre[rows, :] = dot(w_self[rows, :], x_ref[...])


def self_product(w_self, x_rows):
    size, width = x_rows.shape
    return pl.pallas_call(
        functools.partial(self_kernel, 256),
        in_specs=[VMEM] * 2,
        out_specs=VMEM,
        out_shape=jax.ShapeDtypeStruct((size, width), F32),
        compiler_params=whole_params(60),
        cost_estimate=pl.CostEstimate(
            flops=2 * size * size * width, bytes_accessed=5 * MIB, transcendentals=0
        ),
    )(w_self, x_rows)


def dense_kernel(chunk, *refs):
    half_ref, sources, targets, held = refs[0], refs[1:9], refs[9:15], refs[15:23]
    (agg_hbm, hidden_hbm, dpre_hbm, dagg_hbm, second_hbm, sent_hbm) = targets
    (tiles, turned, x_ref, picked, w_neigh, pre_ref, cot_ref, w_back) = held
    (agg, hidden, dpre, dagg, second, sent, in_sems, out_sems) = refs[23:]
    size = w_neigh.shape[0]
    pair = tiles.shape[-1]
    part = [slice(i, i + chunk) for i in range(0, size, chunk)]
    here = [slice(i, i + pair) for i in range(0, agg.shape[1], pair)]
    loads = [
        pltpu.make_async_copy(sources[k], held[k], in_sems.at[k]) for k in (0, 2, 3, 4, 5, 6, 7, 1)
    ]
    for copy in loads:
        copy.start()
    stores = []

    def store(k, src, dst, i):
        copy = pltpu.make_async_copy(src.at[part[i]], dst.at[part[i]], out_sems.at[k, i])
        copy.start()
        stores.append(copy)

    for copy in loads[:3]:
        copy.wait()
    for i in range(len(part)):
        for p in range(len(here)):
            total = dot(x_ref[part[i], here[p]], tiles[0, p])
            total = total + dot(picked[part[i], here[p]], tiles[1, p])
            agg[part[i], here[p]] = total.astype(BF16)
    for copy in loads[3:6]:
        copy.wait()
    for i in range(len(part)):
        store(0, agg, agg_hbm, i)
        pre = pre_ref[part[i], :] + dot(w_neigh[part[i], :], agg[...])
        sig = 0.5 + 0.5 * jnp.tanh(0.5 * pre)
        hidden[part[i], :] = (pre * sig).astype(BF16)
        slope = sig * (1.0 + pre * (1.0 - sig))
        dpre[part[i], :] = (cot_ref[part[i], :].astype(F32) * slope).astype(BF16)
    for copy in loads[6:]:
        copy.wait()
    for i in range(len(part)):
        store(1, hidden, hidden_hbm, i)
        store(2, dpre, dpre_hbm, i)
        dagg[part[i], :] = dot(w_back[part[i], :], dpre[...]).astype(BF16)
        for p in range(len(here)):
            second[part[i], here[p]] = dot(dagg[part[i], here[p]], turned[1, p]).astype(BF16)
        store(3, dagg, dagg_hbm, i)
        store(4, second, second_hbm, i)
    width = sent.shape[1]
    half = agg.at[pl.ds(pl.multiple_of(half_ref[0] * width, width), width)]
    for i in range(len(part)):
        sent[part[i], :] = dot(dpre[part[i], :], half[...], NT).astype(BF16)
        store(5, sent, sent_hbm, i)
    for copy in stores:
        copy.wait()


def dense(half, tiles, turned, x_rows, picked, w_neigh, pre_self, cot, w_back):
    size, width = picked.shape
    chunk = CHUNK
    out = jax.ShapeDtypeStruct((size, width), BF16)
    args = (tiles, turned, x_rows, picked, w_neigh, pre_self, cot, w_back)
    return pl.pallas_call(
        functools.partial(dense_kernel, chunk),
        in_specs=[SMEM] + [ANYWHERE] * len(args),
        out_specs=[ANYWHERE] * 6,
        out_shape=[out] * 5 + [jax.ShapeDtypeStruct((size, size // CORES), BF16)],
        scratch_shapes=[pltpu.VMEM(arg.shape, arg.dtype) for arg in args]
        + [pltpu.VMEM((size, width), BF16)] * 5
        + [pltpu.VMEM((size, size // CORES), BF16)]
        + [pltpu.SemaphoreType.DMA((len(args),)), pltpu.SemaphoreType.DMA((6, size // chunk))],
        compiler_params=whole_params(DENSE_MIB),
        cost_estimate=pl.CostEstimate(
            flops=4 * size * size * width, bytes_accessed=16 * MIB, transcendentals=size * width
        ),
    )(half, *args)


def own_kernel(chunk, w_back, dpre, dagg_ref, turned, own):
    pair = turned.shape[-1]
    each = own.shape[1]
    for i in range(0, dpre.shape[0], chunk):
        rows = slice(i, i + chunk)
        dself = dot(w_back[rows, :], dpre[...])
        for p in range(own.shape[2] // pair):
            here = slice(p * pair, (p + 1) * pair)
            total = dself[:, here] + dot(dagg_ref[rows, here], turned[0, p])
            for g in range(chunk // each):
                own[i // each + g, :, here] = total[g * each : (g + 1) * each].astype(BF16)


def own_part(w_back, dpre, dagg, turned, groups):
    size, width = dpre.shape
    return pl.pallas_call(
        functools.partial(own_kernel, 256),
        in_specs=[VMEM] * 4,
        out_specs=VMEM,
        out_shape=jax.ShapeDtypeStruct((groups, size // groups, width), BF16),
        compiler_params=whole_params(OWN_MIB),
        cost_estimate=pl.CostEstimate(
            flops=2 * size * size * width, bytes_accessed=5 * MIB, transcendentals=0
        ),
    )(w_back, dpre, dagg, turned)


def weight_kernel(core_ref, me_ref, dpre, agg_ref, other_ref, *outs):
    core, me = core_ref[0], me_ref[0]
    rows, width = outs[0].shape
    half = agg_ref.at[pl.ds(pl.multiple_of(core * width, width), width)]
    for step, out in enumerate(outs):
        here = pl.ds(pl.multiple_of(lax.rem(me + step, len(outs)) * rows, rows), rows)
        total = dot(dpre[here, :], half[...], NT) + other_ref[here, :].astype(F32)
        out[...] = total.astype(out.dtype)


def weight_pieces(core, me, dpre, agg_rows, other):
    size, width = dpre.shape
    shape = (size // SIDE, size // CORES)
    return pl.pallas_call(
        weight_kernel,
        in_specs=[SMEM] * 2 + [VMEM] * 3,
        out_specs=[VMEM] * SIDE,
        out_shape=[jax.ShapeDtypeStruct(shape, F32)]
        + [jax.ShapeDtypeStruct(shape, BF16)] * (SIDE - 1),
        compiler_params=whole_params(WEIGHT_MIB),
        cost_estimate=pl.CostEstimate(
            flops=size * size * width, bytes_accessed=4 * MIB, transcendentals=0
        ),
    )(core[None], me[None], dpre, agg_rows, other)


def add_kernel(index_ref, *refs):
    parts, outs = refs[:SIDE], refs[SIDE:]
    rows = outs[0].shape[0]
    for step, out in enumerate(outs):
        here = pl.ds(pl.multiple_of(lax.rem(index_ref[0] + step, SIDE) * rows, rows), rows)
        total = parts[0][here, :]
        for part in parts[1:]:
            total = total + part[here, :].astype(F32)
        out[...] = total.astype(out.dtype)


def added_pieces(me, parts):
    rows, width = parts[0].shape
    shape = (rows // SIDE, width)
    return pl.pallas_call(
        add_kernel,
        in_specs=[SMEM] + [VMEM] * SIDE,
        out_specs=[VMEM] * SIDE,
        out_shape=[jax.ShapeDtypeStruct(shape, F32)]
        + [jax.ShapeDtypeStruct(shape, BF16)] * (SIDE - 1),
        compiler_params=whole_params(WEIGHT_MIB),
        cost_estimate=pl.CostEstimate(flops=0, bytes_accessed=2 * MIB, transcendentals=0),
    )(me[None], *parts)


def final_kernel(own_ref, before_ref, after_ref, dself_ref, out_ref):
    tile = own_ref.shape[2]
    per = dself_ref.shape[2] // tile
    for b in range(own_ref.shape[0]):
        grad = dself_ref[b // per, : own_ref.shape[1], (b % per) * tile : (b % per + 1) * tile]
        total = own_ref[b] + before_ref[b].astype(F32) + after_ref[b].astype(F32)
        out_ref[:, b * tile : (b + 1) * tile] = (grad.astype(F32) + total).astype(BF16)


def finish(own, before, after, dself):
    groups, high, width = dself.shape
    blocks, rows, tile = own.shape
    steps = 4
    part = pl.BlockSpec((blocks // steps, rows, tile), lambda g: (g, 0, 0))
    return pl.pallas_call(
        final_kernel,
        grid=(steps,),
        in_specs=[part, part, part]
        + [pl.BlockSpec((groups // steps, high, width), lambda g: (g, 0, 0))],
        out_specs=pl.BlockSpec((rows, groups * width // steps), lambda g: (0, g)),
        out_shape=jax.ShapeDtypeStruct((rows, groups * width), BF16),
        compiler_params=params(FINAL_MIB),
    )(own, before, after, dself)


def shifted(value, axis, steps):
    count = lax.axis_size(axis)
    first, last = max(0, -steps), min(count, count - steps)
    return lax.ppermute(value, axis, [(source, source + steps) for source in range(first, last)])


def exchange(value, axis):
    return lax.all_to_all(value, axis, split_axis=0, concat_axis=0, tiled=True)


SIDE = 4
CORES = 2


def sent_round(pieces, axis, partner):
    count = lax.axis_size(axis)
    return [pieces[0]] + [
        lax.ppermute(piece, axis, [(i, partner(i, step + 1)) for i in range(count)])
        for step, piece in enumerate(pieces[1:])
    ]


def weight_parts(sent, dpre, agg_rows, groups, own_rows, second_cols):
    feat, node = lax.axis_index("feat"), lax.axis_index("node")
    other = lax.ppermute(sent, "feat", [(i, i ^ 1) for i in range(groups)])
    pieces = weight_pieces(lax.rem(feat, CORES), lax.div(node, SIDE), dpre, agg_rows, other)
    parts = sent_round(pieces, "node", lambda i, s: (i + s * SIDE) % (SIDE * SIDE))
    parts, own_rows = lax.optimization_barrier((parts, own_rows))
    pieces = added_pieces(lax.rem(node, SIDE), parts)
    _, second_cols, own_rows = lax.optimization_barrier((pieces, second_cols, own_rows))
    parts = sent_round(pieces, "node", lambda i, s: i // SIDE * SIDE + (i + s) % SIDE)
    return parts, own_rows, second_cols


def piece_at(pieces, index):
    return lax.dynamic_index_in_dim(pieces, index, 0, keepdims=False)


def weight_total(parts, groups, halo):
    feat = lax.axis_index("feat")
    value = parts[0]
    for part in parts[1:]:
        value = value + part.astype(F32)
    width = value.shape[1]
    half = groups // 2
    while half >= CORES:
        if half == CORES:
            value, _ = lax.optimization_barrier((value, halo))
        bit = lax.rem(lax.div(feat, half), 2)
        pieces = value.reshape(2, -1, width)
        flip = [(i, i ^ half) for i in range(groups)]
        value = piece_at(pieces, bit) + lax.ppermute(piece_at(pieces, 1 - bit), "feat", flip)
        half //= 2
    core = lax.rem(feat, CORES)
    pieces = value.reshape(CORES, -1, width)
    flip = [(i, i ^ 1) for i in range(groups)]
    other = lax.ppermute(piece_at(pieces, 1 - core), "feat", flip)
    kept = piece_at(pieces, core)
    first, second = jnp.where(core == 0, kept, other), jnp.where(core == 0, other, kept)
    return jnp.concatenate([first, second], axis=1)


def paired(tiles):
    blocks, tile, _ = tiles.shape
    tiles = tiles.reshape(blocks // 2, 2, tile, tile)
    empty = jnp.zeros_like(tiles[:, 0])
    upper = jnp.concatenate([tiles[:, 0], empty], axis=2)
    lower = jnp.concatenate([empty, tiles[:, 1]], axis=2)
    return jnp.concatenate([upper, lower], axis=1)


def local(features, tile_values, tile_cols, tile_count, w_self, w_neigh, cotangent):
    feat_dev, node_dev = features.shape
    tile = tile_values.shape[-1]
    block_count = node_dev // tile
    groups = lax.axis_size("feat")
    size = w_self.shape[0]
    part, feat = lax.axis_index("node"), lax.axis_index("feat")
    col = tile_cols[:, 1] - (part - 1) * block_count
    mine = block_count // groups
    live = lax.dynamic_slice_in_dim(tile_count, feat * mine, mine) > 1
    tiles = lax.dynamic_slice_in_dim(tile_values, feat * mine, mine)
    other = jnp.where(live[:, None, None], tiles[:, 1], jnp.zeros_like(tiles[:, 1]))
    straight = jnp.stack([paired(tiles[:, 0]), paired(other)])
    turned = straight.swapaxes(2, 3)

    before = shifted(features, "node", 1)
    behind = shifted(features, "node", -1)
    x_rows = exchange(split_columns(features, groups), "feat").reshape(size, -1)
    picked = exchange(gather(col, before, features, behind, groups), "feat").reshape(size, -1)
    x_rows, self_back, neigh_back, straight, turned = lax.optimization_barrier(
        (x_rows, w_self.T, w_neigh.T, straight, turned)
    )
    pre_self = self_product(w_self, x_rows)
    core = lax.rem(feat, CORES)
    agg_rows, hidden, dpre, dagg, second, sent = dense(
        1 - core[None], straight, turned, x_rows, picked, w_neigh, pre_self, cotangent, neigh_back
    )
    second_cols = exchange(second.reshape(groups, feat_dev, -1), "feat")
    own_rows = own_part(self_back, dpre, dagg, turned, groups)
    parts, own_rows, second_cols = weight_parts(
        sent, dpre, agg_rows, groups, own_rows, second_cols
    )
    own_cols = exchange(own_rows, "feat")
    to_before, spread, to_after = scatter(col, second_cols)
    from_after = shifted(to_before, "node", -1)
    from_before = shifted(to_after, "node", 1)
    parts, _ = lax.optimization_barrier((parts, spread))
    grad_w_neigh = weight_total(parts, groups, (from_after, from_before))
    grad_features = finish(spread, from_before, from_after, own_cols)
    return (hidden, grad_features, grad_w_neigh)


def solution(mesh):
    placed = (
        P("feat", "node"),
        P("node", None, None, None),
        P("node", None),
        P("node"),
        P(),
        P(),
        P(None, ("node", "feat")),
    )
    return jax.shard_map(
        local,
        mesh=mesh,
        in_specs=placed,
        out_specs=(P(None, ("node", "feat")), P("feat", "node"), P(("node", "feat"), None)),
        check_vma=False,
    )
```

```python
import functools

import jax
import jax.numpy as jnp
from jax import lax
from jax.experimental import pallas as pl
from jax.experimental.pallas import tpu as pltpu
from jax.sharding import PartitionSpec as P

F32 = jnp.float32
BF16 = jnp.bfloat16
NT = (((1,), (1,)), ((), ()))
NN = (((1,), (0,)), ((), ()))
MIB = 1 << 20
DENSE_MIB = 56
OWN_MIB = 60
WEIGHT_MIB = 60
FINAL_MIB = 50
SCATTER_MIB = 56
CHUNK = 512


def dot(a, b, dims=NN):
    return lax.dot_general(a, b, dims, preferred_element_type=F32)


def whole_params(mib):
    return pltpu.CompilerParams(vmem_limit_bytes=mib * MIB)


def params(mib):
    return pltpu.CompilerParams(
        dimension_semantics=("arbitrary",), vmem_limit_bytes=mib * MIB
    )


def split_kernel(x_hbm, out_hbm, held, in_sems, out_sems):
    width = out_hbm.shape[2]
    groups = range(out_hbm.shape[0])
    loads = [
        pltpu.make_async_copy(x_hbm.at[:, g * width : (g + 1) * width], held.at[g], in_sems.at[g])
        for g in groups
    ]
    stores = [pltpu.make_async_copy(held.at[g], out_hbm.at[g], out_sems.at[g]) for g in groups]
    for copy in loads:
        copy.start()
    for load, store in zip(loads, stores):
        load.wait()
        store.start()
    for copy in stores:
        copy.wait()


ANYWHERE = pl.BlockSpec(memory_space=pl.ANY)
SMEM = pl.BlockSpec(memory_space=pltpu.SMEM)
VMEM = pl.BlockSpec(memory_space=pltpu.VMEM)


def split_columns(x, groups):
    rows, columns = x.shape
    return pl.pallas_call(
        split_kernel,
        in_specs=[ANYWHERE],
        out_specs=ANYWHERE,
        out_shape=jax.ShapeDtypeStruct((groups, rows, columns // groups), x.dtype),
        scratch_shapes=[
            pltpu.VMEM((groups, rows, columns // groups), x.dtype),
            pltpu.SemaphoreType.DMA((groups,)),
            pltpu.SemaphoreType.DMA((groups,)),
        ],
        compiler_params=whole_params(60),
    )(x)


def gather_kernel(col_ref, before, own, after, out_hbm, sems):
    tile = 128
    blocks = own.shape[1] // tile
    per = out_hbm.shape[2] // tile

    def target(r):
        place = pl.ds(pl.multiple_of(lax.rem(r, per) * tile, tile), tile)
        return out_hbm.at[lax.div(r, per), :, place]

    def start(r, carry):
        col = col_ref[r]
        for i, part in enumerate((before, own, after)):

            @pl.when((col >= i * blocks) & (col < (i + 1) * blocks))
            def _(i=i, part=part):
                place = pl.ds(pl.multiple_of((col - i * blocks) * tile, tile), tile)
                pltpu.make_async_copy(part.at[:, place], target(r), sems.at[r]).start()

        return carry

    def wait(r, carry):
        pltpu.make_async_copy(own.at[:, :tile], target(r), sems.at[r]).wait()
        return carry

    lax.fori_loop(0, blocks, start, 0)
    lax.fori_loop(0, blocks, wait, 0)


def gather(col, before, own, after, groups):
    rows, span = own.shape
    return pl.pallas_call(
        gather_kernel,
        in_specs=[SMEM] + [ANYWHERE] * 3,
        out_specs=ANYWHERE,
        out_shape=jax.ShapeDtypeStruct((groups, rows, span // groups), BF16),
        scratch_shapes=[pltpu.SemaphoreType.DMA((col.shape[0],))],
        compiler_params=whole_params(2),
        cost_estimate=pl.CostEstimate(flops=0, bytes_accessed=8 * MIB, transcendentals=0),
    )(col, before, own, after)


def scatter_kernel(
    col_ref, parts_hbm, before_hbm, own_hbm, after_hbm, parts_ref, acc, before, after, load_sem, sems
):
    tile = acc.shape[2]
    blocks = own_hbm.shape[0]
    per = parts_ref.shape[2] // tile
    load = pltpu.make_async_copy(parts_hbm, parts_ref, load_sem)
    load.start()

    def clear(i, carry):
        acc[i] = jnp.zeros(acc.shape[1:], F32)
        return carry

    lax.fori_loop(0, acc.shape[0], clear, 0, unroll=8)
    load.wait()

    def add(g, carry):
        for b in range(per):
            acc[col_ref[g * per + b]] += parts_ref[g, :, b * tile : (b + 1) * tile].astype(F32)
        return carry

    lax.fori_loop(0, parts_ref.shape[0], add, 0, unroll=2)
    copies = [
        pltpu.make_async_copy(acc.at[blocks : 2 * blocks], own_hbm, sems.at[0]),
        pltpu.make_async_copy(before, before_hbm, sems.at[1]),
        pltpu.make_async_copy(after, after_hbm, sems.at[2]),
    ]
    copies[0].start()
    for first, out, copy in ((0, before, copies[1]), (2 * blocks, after, copies[2])):

        def cast(i, carry, first=first, out=out):
            out[i] = acc[first + i].astype(BF16)
            return carry

        lax.fori_loop(0, blocks, cast, 0, unroll=8)
        copy.start()
    for copy in copies:
        copy.wait()


def scatter(col, parts):
    groups, rows, width = parts.shape
    blocks = col.shape[0]
    tile = groups * width // blocks
    shape = (blocks, rows, tile)
    return pl.pallas_call(
        scatter_kernel,
        in_specs=[SMEM, ANYWHERE],
        out_specs=[ANYWHERE] * 3,
        out_shape=[
            jax.ShapeDtypeStruct(shape, BF16),
            jax.ShapeDtypeStruct(shape, F32),
            jax.ShapeDtypeStruct(shape, BF16),
        ],
        scratch_shapes=[
            pltpu.VMEM(parts.shape, BF16),
            pltpu.VMEM((3 * blocks, rows, tile), F32),
            pltpu.VMEM(shape, BF16),
            pltpu.VMEM(shape, BF16),
            pltpu.SemaphoreType.DMA(()),
            pltpu.SemaphoreType.DMA((3,)),
        ],
        compiler_params=whole_params(SCATTER_MIB),
        cost_estimate=pl.CostEstimate(flops=0, bytes_accessed=8 * MIB, transcendentals=0),
    )(col, parts)


def self_kernel(chunk, w_self, x_ref, pre):
    for i in range(pre.shape[0] // chunk):
        rows = slice(i * chunk, (i + 1) * chunk)
        pre[rows, :] = dot(w_self[rows, :], x_ref[...])


def self_product(w_self, x_rows):
    size, width = x_rows.shape
    return pl.pallas_call(
        functools.partial(self_kernel, 256),
        in_specs=[VMEM] * 2,
        out_specs=VMEM,
        out_shape=jax.ShapeDtypeStruct((size, width), F32),
        compiler_params=whole_params(60),
        cost_estimate=pl.CostEstimate(
            flops=2 * size * size * width, bytes_accessed=5 * MIB, transcendentals=0
        ),
    )(w_self, x_rows)


def dense_kernel(chunk, *refs):
    half_ref, sources, targets, held = refs[0], refs[1:9], refs[9:15], refs[15:23]
    (agg_hbm, hidden_hbm, dpre_hbm, dagg_hbm, second_hbm, sent_hbm) = targets
    (tiles, turned, x_ref, picked, w_neigh, pre_ref, cot_ref, w_back) = held
    (agg, hidden, dpre, dagg, second, sent, in_sems, out_sems) = refs[23:]
    size = w_neigh.shape[0]
    pair = tiles.shape[-1]
    part = [slice(i, i + chunk) for i in range(0, size, chunk)]
    here = [slice(i, i + pair) for i in range(0, agg.shape[1], pair)]
    loads = [
        pltpu.make_async_copy(sources[k], held[k], in_sems.at[k]) for k in (0, 2, 3, 4, 5, 6, 7, 1)
    ]
    for copy in loads:
        copy.start()
    stores = []

    def store(k, src, dst, i):
        copy = pltpu.make_async_copy(src.at[part[i]], dst.at[part[i]], out_sems.at[k, i])
        copy.start()
        stores.append(copy)

    for copy in loads[:3]:
        copy.wait()
    for i in range(len(part)):
        for p in range(len(here)):
            total = dot(x_ref[part[i], here[p]], tiles[0, p])
            total = total + dot(picked[part[i], here[p]], tiles[1, p])
            agg[part[i], here[p]] = total.astype(BF16)
    for copy in loads[3:6]:
        copy.wait()
    for i in range(len(part)):
        store(0, agg, agg_hbm, i)
        pre = pre_ref[part[i], :] + dot(w_neigh[part[i], :], agg[...])
        sig = 0.5 + 0.5 * jnp.tanh(0.5 * pre)
        hidden[part[i], :] = (pre * sig).astype(BF16)
        slope = sig * (1.0 + pre * (1.0 - sig))
        dpre[part[i], :] = (cot_ref[part[i], :].astype(F32) * slope).astype(BF16)
    for copy in loads[6:]:
        copy.wait()
    for i in range(len(part)):
        store(1, hidden, hidden_hbm, i)
        store(2, dpre, dpre_hbm, i)
        dagg[part[i], :] = dot(w_back[part[i], :], dpre[...]).astype(BF16)
        for p in range(len(here)):
            second[part[i], here[p]] = dot(dagg[part[i], here[p]], turned[1, p]).astype(BF16)
        store(3, dagg, dagg_hbm, i)
        store(4, second, second_hbm, i)
    width = sent.shape[1]
    half = agg.at[pl.ds(pl.multiple_of(half_ref[0] * width, width), width)]
    for i in range(len(part)):
        sent[part[i], :] = dot(dpre[part[i], :], half[...], NT).astype(BF16)
        store(5, sent, sent_hbm, i)
    for copy in stores:
        copy.wait()


def dense(half, tiles, turned, x_rows, picked, w_neigh, pre_self, cot, w_back):
    size, width = picked.shape
    chunk = CHUNK
    out = jax.ShapeDtypeStruct((size, width), BF16)
    args = (tiles, turned, x_rows, picked, w_neigh, pre_self, cot, w_back)
    return pl.pallas_call(
        functools.partial(dense_kernel, chunk),
        in_specs=[SMEM] + [ANYWHERE] * len(args),
        out_specs=[ANYWHERE] * 6,
        out_shape=[out] * 5 + [jax.ShapeDtypeStruct((size, size // CORES), BF16)],
        scratch_shapes=[pltpu.VMEM(arg.shape, arg.dtype) for arg in args]
        + [pltpu.VMEM((size, width), BF16)] * 5
        + [pltpu.VMEM((size, size // CORES), BF16)]
        + [pltpu.SemaphoreType.DMA((len(args),)), pltpu.SemaphoreType.DMA((6, size // chunk))],
        compiler_params=whole_params(DENSE_MIB),
        cost_estimate=pl.CostEstimate(
            flops=4 * size * size * width, bytes_accessed=16 * MIB, transcendentals=size * width
        ),
    )(half, *args)


def own_kernel(chunk, w_back, dpre, dagg_ref, turned, own):
    pair = turned.shape[-1]
    each = own.shape[1]
    for i in range(0, dpre.shape[0], chunk):
        rows = slice(i, i + chunk)
        dself = dot(w_back[rows, :], dpre[...])
        for p in range(own.shape[2] // pair):
            here = slice(p * pair, (p + 1) * pair)
            total = dself[:, here] + dot(dagg_ref[rows, here], turned[0, p])
            for g in range(chunk // each):
                own[i // each + g, :, here] = total[g * each : (g + 1) * each].astype(BF16)


def own_part(w_back, dpre, dagg, turned, groups):
    size, width = dpre.shape
    return pl.pallas_call(
        functools.partial(own_kernel, 256),
        in_specs=[VMEM] * 4,
        out_specs=VMEM,
        out_shape=jax.ShapeDtypeStruct((groups, size // groups, width), BF16),
        compiler_params=whole_params(OWN_MIB),
        cost_estimate=pl.CostEstimate(
            flops=2 * size * size * width, bytes_accessed=5 * MIB, transcendentals=0
        ),
    )(w_back, dpre, dagg, turned)


def weight_kernel(core_ref, me_ref, dpre, agg_ref, other_ref, *outs):
    core, me = core_ref[0], me_ref[0]
    rows, width = outs[0].shape
    half = agg_ref.at[pl.ds(pl.multiple_of(core * width, width), width)]
    each = rows // SIDE

    def picked(ref, there):
        first = lax.rem(me + there, SIDE) * each
        places = [pl.multiple_of(i * rows + first, each) for i in range(SIDE)]
        return jnp.concatenate([ref[pl.ds(place, each), :] for place in places], axis=0)

    for step, out in enumerate(outs):
        total = dot(picked(dpre, step), half[...], NT) + picked(other_ref, step).astype(F32)
        out[...] = total.astype(out.dtype)


def weight_pieces(core, me, dpre, agg_rows, other):
    size, width = dpre.shape
    shape = (size // SIDE, size // CORES)
    return pl.pallas_call(
        weight_kernel,
        in_specs=[SMEM] * 2 + [VMEM] * 3,
        out_specs=[VMEM] * SIDE,
        out_shape=[jax.ShapeDtypeStruct(shape, F32)]
        + [jax.ShapeDtypeStruct(shape, BF16)] * (SIDE - 1),
        compiler_params=whole_params(WEIGHT_MIB),
        cost_estimate=pl.CostEstimate(
            flops=size * size * width, bytes_accessed=4 * MIB, transcendentals=0
        ),
    )(core[None], me[None], dpre, agg_rows, other)


def add_kernel(index_ref, *refs):
    parts, outs = refs[:SIDE], refs[SIDE:]
    rows = outs[0].shape[0]
    for step, out in enumerate(outs):
        here = pl.ds(pl.multiple_of(lax.rem(index_ref[0] + step, SIDE) * rows, rows), rows)
        total = parts[0][here, :]
        for part in parts[1:]:
            total = total + part[here, :].astype(F32)
        out[...] = total.astype(out.dtype)


def added_pieces(me, parts):
    rows, width = parts[0].shape
    shape = (rows // SIDE, width)
    return pl.pallas_call(
        add_kernel,
        in_specs=[SMEM] + [VMEM] * SIDE,
        out_specs=[VMEM] * SIDE,
        out_shape=[jax.ShapeDtypeStruct(shape, F32)]
        + [jax.ShapeDtypeStruct(shape, BF16)] * (SIDE - 1),
        compiler_params=whole_params(WEIGHT_MIB),
        cost_estimate=pl.CostEstimate(flops=0, bytes_accessed=2 * MIB, transcendentals=0),
    )(me[None], *parts)


def final_kernel(own_ref, before_ref, after_ref, dself_ref, out_ref):
    tile = own_ref.shape[2]
    per = dself_ref.shape[2] // tile
    for b in range(own_ref.shape[0]):
        grad = dself_ref[b // per, : own_ref.shape[1], (b % per) * tile : (b % per + 1) * tile]
        total = own_ref[b] + before_ref[b].astype(F32) + after_ref[b].astype(F32)
        out_ref[:, b * tile : (b + 1) * tile] = (grad.astype(F32) + total).astype(BF16)


def finish(own, before, after, dself):
    groups, high, width = dself.shape
    blocks, rows, tile = own.shape
    steps = 4
    part = pl.BlockSpec((blocks // steps, rows, tile), lambda g: (g, 0, 0))
    return pl.pallas_call(
        final_kernel,
        grid=(steps,),
        in_specs=[part, part, part]
        + [pl.BlockSpec((groups // steps, high, width), lambda g: (g, 0, 0))],
        out_specs=pl.BlockSpec((rows, groups * width // steps), lambda g: (0, g)),
        out_shape=jax.ShapeDtypeStruct((rows, groups * width), BF16),
        compiler_params=params(FINAL_MIB),
    )(own, before, after, dself)


def shifted(value, axis, steps):
    count = lax.axis_size(axis)
    first, last = max(0, -steps), min(count, count - steps)
    return lax.ppermute(value, axis, [(source, source + steps) for source in range(first, last)])


def exchange(value, axis):
    return lax.all_to_all(value, axis, split_axis=0, concat_axis=0, tiled=True)


SIDE = 4
CORES = 2


def sent_round(pieces, axis, partner):
    count = lax.axis_size(axis)
    return [pieces[0]] + [
        lax.ppermute(piece, axis, [(i, partner(i, step + 1)) for i in range(count)])
        for step, piece in enumerate(pieces[1:])
    ]


def weight_pieces_along_x(sent, dpre, agg_rows, groups, own_rows):
    feat, node = lax.axis_index("feat"), lax.axis_index("node")
    other = lax.ppermute(sent, "feat", [(i, i ^ 1) for i in range(groups)])
    pieces = weight_pieces(lax.rem(feat, CORES), lax.rem(node, SIDE), dpre, agg_rows, other)
    parts = sent_round(pieces, "node", lambda i, s: i // SIDE * SIDE + (i + s) % SIDE)
    parts, own_rows = lax.optimization_barrier((parts, own_rows))
    return added_pieces(lax.div(node, SIDE), parts)


def piece_at(pieces, index):
    return lax.dynamic_index_in_dim(pieces, index, 0, keepdims=False)


def weight_total(pieces, groups, halo):
    feat = lax.axis_index("feat")
    parts = sent_round(pieces, "node", lambda i, s: (i + s * SIDE) % (SIDE * SIDE))
    value = parts[0]
    for part in parts[1:]:
        value = value + part.astype(F32)
    width = value.shape[1]
    half = groups // 2
    while half >= CORES:
        if half == 2 * CORES:
            value, _ = lax.optimization_barrier((value, halo))
        bit = lax.rem(lax.div(feat, half), 2)
        pieces = value.reshape(2, -1, width)
        flip = [(i, i ^ half) for i in range(groups)]
        value = piece_at(pieces, bit) + lax.ppermute(piece_at(pieces, 1 - bit), "feat", flip)
        half //= 2
    core = lax.rem(feat, CORES)
    pieces = value.reshape(CORES, -1, width)
    flip = [(i, i ^ 1) for i in range(groups)]
    other = lax.ppermute(piece_at(pieces, 1 - core), "feat", flip)
    kept = piece_at(pieces, core)
    first, second = jnp.where(core == 0, kept, other), jnp.where(core == 0, other, kept)
    return jnp.concatenate([first, second], axis=1)


def paired(tiles):
    blocks, tile, _ = tiles.shape
    tiles = tiles.reshape(blocks // 2, 2, tile, tile)
    empty = jnp.zeros_like(tiles[:, 0])
    upper = jnp.concatenate([tiles[:, 0], empty], axis=2)
    lower = jnp.concatenate([empty, tiles[:, 1]], axis=2)
    return jnp.concatenate([upper, lower], axis=1)


def local(features, tile_values, tile_cols, tile_count, w_self, w_neigh, cotangent):
    feat_dev, node_dev = features.shape
    tile = tile_values.shape[-1]
    block_count = node_dev // tile
    groups = lax.axis_size("feat")
    size = w_self.shape[0]
    part, feat = lax.axis_index("node"), lax.axis_index("feat")
    col = tile_cols[:, 1] - (part - 1) * block_count
    mine = block_count // groups
    live = lax.dynamic_slice_in_dim(tile_count, feat * mine, mine) > 1
    tiles = lax.dynamic_slice_in_dim(tile_values, feat * mine, mine)
    other = jnp.where(live[:, None, None], tiles[:, 1], jnp.zeros_like(tiles[:, 1]))
    straight = jnp.stack([paired(tiles[:, 0]), paired(other)])
    turned = straight.swapaxes(2, 3)

    before = shifted(features, "node", 1)
    behind = shifted(features, "node", -1)
    x_rows = exchange(split_columns(features, groups), "feat").reshape(size, -1)
    picked = exchange(gather(col, before, features, behind, groups), "feat").reshape(size, -1)
    x_rows, self_back, neigh_back, straight, turned = lax.optimization_barrier(
        (x_rows, w_self.T, w_neigh.T, straight, turned)
    )
    pre_self = self_product(w_self, x_rows)
    core = lax.rem(feat, CORES)
    agg_rows, hidden, dpre, dagg, second, sent = dense(
        1 - core[None], straight, turned, x_rows, picked, w_neigh, pre_self, cotangent, neigh_back
    )
    second_cols = exchange(second.reshape(groups, feat_dev, -1), "feat")
    own_rows = own_part(self_back, dpre, dagg, turned, groups)
    pieces = weight_pieces_along_x(sent, dpre, agg_rows, groups, own_rows)
    _, second_cols, own_rows = lax.optimization_barrier((pieces, second_cols, own_rows))
    own_cols = exchange(own_rows, "feat")
    to_before, spread, to_after = scatter(col, second_cols)
    from_after = shifted(to_before, "node", -1)
    from_before = shifted(to_after, "node", 1)
    pieces, _ = lax.optimization_barrier((pieces, spread))
    grad_w_neigh = weight_total(pieces, groups, (from_after, from_before))
    grad_features = finish(spread, from_before, from_after, own_cols)
    return (hidden, grad_features, grad_w_neigh)


def solution(mesh):
    placed = (
        P("feat", "node"),
        P("node", None, None, None),
        P("node", None),
        P("node"),
        P(),
        P(),
        P(None, ("node", "feat")),
    )
    return jax.shard_map(
        local,
        mesh=mesh,
        in_specs=placed,
        out_specs=(P(None, ("node", "feat")), P("feat", "node"), P(("node", "feat"), None)),
        check_vma=False,
    )
```

```python
import functools

import jax
import jax.numpy as jnp
from jax import lax
from jax.experimental import pallas as pl
from jax.experimental.pallas import tpu as pltpu
from jax.sharding import PartitionSpec as P

F32 = jnp.float32
BF16 = jnp.bfloat16
NT = (((1,), (1,)), ((), ()))
NN = (((1,), (0,)), ((), ()))
MIB = 1 << 20
DENSE_MIB = 56
OWN_MIB = 60
WEIGHT_MIB = 8
FINAL_MIB = 50
SCATTER_MIB = 56
CHUNK = 512


def dot(a, b, dims=NN):
    return lax.dot_general(a, b, dims, preferred_element_type=F32)


def whole_params(mib):
    return pltpu.CompilerParams(vmem_limit_bytes=mib * MIB)


def params(mib):
    return pltpu.CompilerParams(
        dimension_semantics=("arbitrary",), vmem_limit_bytes=mib * MIB
    )


def split_kernel(x_hbm, out_hbm, held, in_sems, out_sems):
    width = out_hbm.shape[2]
    groups = range(out_hbm.shape[0])
    loads = [
        pltpu.make_async_copy(x_hbm.at[:, g * width : (g + 1) * width], held.at[g], in_sems.at[g])
        for g in groups
    ]
    stores = [pltpu.make_async_copy(held.at[g], out_hbm.at[g], out_sems.at[g]) for g in groups]
    for copy in loads:
        copy.start()
    for load, store in zip(loads, stores):
        load.wait()
        store.start()
    for copy in stores:
        copy.wait()


ANYWHERE = pl.BlockSpec(memory_space=pl.ANY)
SMEM = pl.BlockSpec(memory_space=pltpu.SMEM)
VMEM = pl.BlockSpec(memory_space=pltpu.VMEM)


def split_columns(x, groups):
    rows, columns = x.shape
    return pl.pallas_call(
        split_kernel,
        in_specs=[ANYWHERE],
        out_specs=ANYWHERE,
        out_shape=jax.ShapeDtypeStruct((groups, rows, columns // groups), x.dtype),
        scratch_shapes=[
            pltpu.VMEM((groups, rows, columns // groups), x.dtype),
            pltpu.SemaphoreType.DMA((groups,)),
            pltpu.SemaphoreType.DMA((groups,)),
        ],
        compiler_params=whole_params(60),
    )(x)


def gather_kernel(col_ref, before, own, after, out_hbm, sems):
    tile = 128
    blocks = own.shape[1] // tile
    per = out_hbm.shape[2] // tile

    def target(r):
        place = pl.ds(pl.multiple_of(lax.rem(r, per) * tile, tile), tile)
        return out_hbm.at[lax.div(r, per), :, place]

    def start(r, carry):
        col = col_ref[r]
        for i, part in enumerate((before, own, after)):

            @pl.when((col >= i * blocks) & (col < (i + 1) * blocks))
            def _(i=i, part=part):
                place = pl.ds(pl.multiple_of((col - i * blocks) * tile, tile), tile)
                pltpu.make_async_copy(part.at[:, place], target(r), sems.at[r]).start()

        return carry

    def wait(r, carry):
        pltpu.make_async_copy(own.at[:, :tile], target(r), sems.at[r]).wait()
        return carry

    lax.fori_loop(0, blocks, start, 0)
    lax.fori_loop(0, blocks, wait, 0)


def gather(col, before, own, after, groups):
    rows, span = own.shape
    return pl.pallas_call(
        gather_kernel,
        in_specs=[SMEM] + [ANYWHERE] * 3,
        out_specs=ANYWHERE,
        out_shape=jax.ShapeDtypeStruct((groups, rows, span // groups), BF16),
        scratch_shapes=[pltpu.SemaphoreType.DMA((col.shape[0],))],
        compiler_params=whole_params(2),
        cost_estimate=pl.CostEstimate(flops=0, bytes_accessed=8 * MIB, transcendentals=0),
    )(col, before, own, after)


def scatter_kernel(
    col_ref, parts_hbm, before_hbm, own_hbm, after_hbm, parts_ref, acc, before, after, load_sem, sems
):
    tile = acc.shape[2]
    blocks = own_hbm.shape[0]
    per = parts_ref.shape[2] // tile
    load = pltpu.make_async_copy(parts_hbm, parts_ref, load_sem)
    load.start()

    def clear(i, carry):
        acc[i] = jnp.zeros(acc.shape[1:], F32)
        return carry

    lax.fori_loop(0, acc.shape[0], clear, 0, unroll=8)
    load.wait()

    def add(g, carry):
        for b in range(per):
            acc[col_ref[g * per + b]] += parts_ref[g, :, b * tile : (b + 1) * tile].astype(F32)
        return carry

    lax.fori_loop(0, parts_ref.shape[0], add, 0, unroll=2)
    copies = [
        pltpu.make_async_copy(acc.at[blocks : 2 * blocks], own_hbm, sems.at[0]),
        pltpu.make_async_copy(before, before_hbm, sems.at[1]),
        pltpu.make_async_copy(after, after_hbm, sems.at[2]),
    ]
    copies[0].start()
    for first, out, copy in ((0, before, copies[1]), (2 * blocks, after, copies[2])):

        def cast(i, carry, first=first, out=out):
            out[i] = acc[first + i].astype(BF16)
            return carry

        lax.fori_loop(0, blocks, cast, 0, unroll=8)
        copy.start()
    for copy in copies:
        copy.wait()


def scatter(col, parts):
    groups, rows, width = parts.shape
    blocks = col.shape[0]
    tile = groups * width // blocks
    shape = (blocks, rows, tile)
    return pl.pallas_call(
        scatter_kernel,
        in_specs=[SMEM, ANYWHERE],
        out_specs=[ANYWHERE] * 3,
        out_shape=[
            jax.ShapeDtypeStruct(shape, BF16),
            jax.ShapeDtypeStruct(shape, F32),
            jax.ShapeDtypeStruct(shape, BF16),
        ],
        scratch_shapes=[
            pltpu.VMEM(parts.shape, BF16),
            pltpu.VMEM((3 * blocks, rows, tile), F32),
            pltpu.VMEM(shape, BF16),
            pltpu.VMEM(shape, BF16),
            pltpu.SemaphoreType.DMA(()),
            pltpu.SemaphoreType.DMA((3,)),
        ],
        compiler_params=whole_params(SCATTER_MIB),
        cost_estimate=pl.CostEstimate(flops=0, bytes_accessed=8 * MIB, transcendentals=0),
    )(col, parts)


def self_kernel(chunk, w_self, x_ref, pre):
    for i in range(pre.shape[0] // chunk):
        rows = slice(i * chunk, (i + 1) * chunk)
        pre[rows, :] = dot(w_self[rows, :], x_ref[...])


def self_product(w_self, x_rows):
    size, width = x_rows.shape
    return pl.pallas_call(
        functools.partial(self_kernel, 256),
        in_specs=[VMEM] * 2,
        out_specs=VMEM,
        out_shape=jax.ShapeDtypeStruct((size, width), F32),
        compiler_params=whole_params(60),
        cost_estimate=pl.CostEstimate(
            flops=2 * size * size * width, bytes_accessed=5 * MIB, transcendentals=0
        ),
    )(w_self, x_rows)


def dense_kernel(chunk, *refs):
    core_ref, sources, targets, held = refs[0], refs[1:9], refs[9:16], refs[16:24]
    (agg_hbm, hidden_hbm, dpre_hbm, dagg_hbm, second_hbm, sent_hbm, kept_hbm) = targets
    (tiles, turned, x_ref, picked, w_neigh, pre_ref, cot_ref, w_back) = held
    (agg, hidden, dpre, dagg, second, sent, kept, in_sems, out_sems) = refs[24:]
    size = w_neigh.shape[0]
    pair = tiles.shape[-1]
    part = [slice(i, i + chunk) for i in range(0, size, chunk)]
    here = [slice(i, i + pair) for i in range(0, agg.shape[1], pair)]
    loads = [
        pltpu.make_async_copy(sources[k], held[k], in_sems.at[k]) for k in (0, 2, 3, 4, 5, 6, 7, 1)
    ]
    for copy in loads:
        copy.start()
    stores = []

    def store(k, src, dst, i):
        copy = pltpu.make_async_copy(src.at[part[i]], dst.at[part[i]], out_sems.at[k, i])
        copy.start()
        stores.append(copy)

    for copy in loads[:3]:
        copy.wait()
    for i in range(len(part)):
        for p in range(len(here)):
            total = dot(x_ref[part[i], here[p]], tiles[0, p])
            total = total + dot(picked[part[i], here[p]], tiles[1, p])
            agg[part[i], here[p]] = total.astype(BF16)
    for copy in loads[3:6]:
        copy.wait()
    for i in range(len(part)):
        store(0, agg, agg_hbm, i)
        pre = pre_ref[part[i], :] + dot(w_neigh[part[i], :], agg[...])
        sig = 0.5 + 0.5 * jnp.tanh(0.5 * pre)
        hidden[part[i], :] = (pre * sig).astype(BF16)
        slope = sig * (1.0 + pre * (1.0 - sig))
        dpre[part[i], :] = (cot_ref[part[i], :].astype(F32) * slope).astype(BF16)
    for copy in loads[6:]:
        copy.wait()
    for i in range(len(part)):
        store(1, hidden, hidden_hbm, i)
        store(2, dpre, dpre_hbm, i)
        dagg[part[i], :] = dot(w_back[part[i], :], dpre[...]).astype(BF16)
        for p in range(len(here)):
            second[part[i], here[p]] = dot(dagg[part[i], here[p]], turned[1, p]).astype(BF16)
        store(3, dagg, dagg_hbm, i)
        store(4, second, second_hbm, i)
    width = sent.shape[1]
    core = core_ref[0]
    for k, owner, out, target in ((5, 1 - core, sent, sent_hbm), (6, core, kept, kept_hbm)):
        half = agg.at[pl.ds(pl.multiple_of(owner * width, width), width)]
        for i in range(len(part)):
            out[part[i], :] = dot(dpre[part[i], :], half[...], NT).astype(BF16)
            store(k, out, target, i)
    for copy in stores:
        copy.wait()


def dense(core, tiles, turned, x_rows, picked, w_neigh, pre_self, cot, w_back):
    size, width = picked.shape
    chunk = CHUNK
    out = jax.ShapeDtypeStruct((size, width), BF16)
    args = (tiles, turned, x_rows, picked, w_neigh, pre_self, cot, w_back)
    return pl.pallas_call(
        functools.partial(dense_kernel, chunk),
        in_specs=[SMEM] + [ANYWHERE] * len(args),
        out_specs=[ANYWHERE] * 7,
        out_shape=[out] * 5 + [jax.ShapeDtypeStruct((size, size // CORES), BF16)] * 2,
        scratch_shapes=[pltpu.VMEM(arg.shape, arg.dtype) for arg in args]
        + [pltpu.VMEM((size, width), BF16)] * 5
        + [pltpu.VMEM((size, size // CORES), BF16)] * 2
        + [pltpu.SemaphoreType.DMA((len(args),)), pltpu.SemaphoreType.DMA((7, size // chunk))],
        compiler_params=whole_params(DENSE_MIB),
        cost_estimate=pl.CostEstimate(
            flops=4 * size * size * width, bytes_accessed=16 * MIB, transcendentals=size * width
        ),
    )(core, *args)


def own_kernel(chunk, w_back, dpre, dagg_ref, turned, own):
    pair = turned.shape[-1]
    each = own.shape[1]
    for i in range(0, dpre.shape[0], chunk):
        rows = slice(i, i + chunk)
        dself = dot(w_back[rows, :], dpre[...])
        for p in range(own.shape[2] // pair):
            here = slice(p * pair, (p + 1) * pair)
            total = dself[:, here] + dot(dagg_ref[rows, here], turned[0, p])
            for g in range(chunk // each):
                own[i // each + g, :, here] = total[g * each : (g + 1) * each].astype(BF16)


def own_part(w_back, dpre, dagg, turned, groups):
    size, width = dpre.shape
    return pl.pallas_call(
        functools.partial(own_kernel, 256),
        in_specs=[VMEM] * 4,
        out_specs=VMEM,
        out_shape=jax.ShapeDtypeStruct((groups, size // groups, width), BF16),
        compiler_params=whole_params(OWN_MIB),
        cost_estimate=pl.CostEstimate(
            flops=2 * size * size * width, bytes_accessed=5 * MIB, transcendentals=0
        ),
    )(w_back, dpre, dagg, turned)


def weight_kernel(me_ref, kept_ref, other_ref, *outs):
    rows = outs[0].shape[0]
    each = rows // SIDE
    for step, out in enumerate(outs):
        first = lax.rem(me_ref[0] + step, SIDE) * each
        for i in range(SIDE):
            there = pl.ds(pl.multiple_of(i * rows + first, each), each)
            total = kept_ref[there, :].astype(F32) + other_ref[there, :].astype(F32)
            out[i * each : (i + 1) * each, :] = total.astype(out.dtype)


def weight_pieces(me, kept, other):
    size, width = kept.shape
    shape = (size // SIDE, width)
    return pl.pallas_call(
        weight_kernel,
        in_specs=[SMEM] + [VMEM] * 2,
        out_specs=[VMEM] * SIDE,
        out_shape=[jax.ShapeDtypeStruct(shape, F32)]
        + [jax.ShapeDtypeStruct(shape, BF16)] * (SIDE - 1),
        compiler_params=whole_params(WEIGHT_MIB),
        cost_estimate=pl.CostEstimate(flops=0, bytes_accessed=4 * MIB, transcendentals=0),
    )(me[None], kept, other)


def add_kernel(index_ref, *refs):
    parts, outs = refs[:SIDE], refs[SIDE:]
    rows = outs[0].shape[0]
    for step, out in enumerate(outs):
        here = pl.ds(pl.multiple_of(lax.rem(index_ref[0] + step, SIDE) * rows, rows), rows)
        total = parts[0][here, :]
        for part in parts[1:]:
            total = total + part[here, :].astype(F32)
        out[...] = total.astype(out.dtype)


def added_pieces(me, parts):
    rows, width = parts[0].shape
    shape = (rows // SIDE, width)
    return pl.pallas_call(
        add_kernel,
        in_specs=[SMEM] + [VMEM] * SIDE,
        out_specs=[VMEM] * SIDE,
        out_shape=[jax.ShapeDtypeStruct(shape, F32)]
        + [jax.ShapeDtypeStruct(shape, BF16)] * (SIDE - 1),
        compiler_params=whole_params(WEIGHT_MIB),
        cost_estimate=pl.CostEstimate(flops=0, bytes_accessed=2 * MIB, transcendentals=0),
    )(me[None], *parts)


def final_kernel(own_ref, before_ref, after_ref, dself_ref, out_ref):
    tile = own_ref.shape[2]
    per = dself_ref.shape[2] // tile
    for b in range(own_ref.shape[0]):
        grad = dself_ref[b // per, : own_ref.shape[1], (b % per) * tile : (b % per + 1) * tile]
        total = own_ref[b] + before_ref[b].astype(F32) + after_ref[b].astype(F32)
        out_ref[:, b * tile : (b + 1) * tile] = (grad.astype(F32) + total).astype(BF16)


def finish(own, before, after, dself):
    groups, high, width = dself.shape
    blocks, rows, tile = own.shape
    steps = 4
    part = pl.BlockSpec((blocks // steps, rows, tile), lambda g: (g, 0, 0))
    return pl.pallas_call(
        final_kernel,
        grid=(steps,),
        in_specs=[part, part, part]
        + [pl.BlockSpec((groups // steps, high, width), lambda g: (g, 0, 0))],
        out_specs=pl.BlockSpec((rows, groups * width // steps), lambda g: (0, g)),
        out_shape=jax.ShapeDtypeStruct((rows, groups * width), BF16),
        compiler_params=params(FINAL_MIB),
    )(own, before, after, dself)


def shifted(value, axis, steps):
    count = lax.axis_size(axis)
    first, last = max(0, -steps), min(count, count - steps)
    return lax.ppermute(value, axis, [(source, source + steps) for source in range(first, last)])


def exchange(value, axis):
    return lax.all_to_all(value, axis, split_axis=0, concat_axis=0, tiled=True)


SIDE = 4
CORES = 2


def sent_round(pieces, axis, partner):
    count = lax.axis_size(axis)
    return [pieces[0]] + [
        lax.ppermute(piece, axis, [(i, partner(i, step + 1)) for i in range(count)])
        for step, piece in enumerate(pieces[1:])
    ]


def weight_terms(sent, kept, groups, own_rows):
    node = lax.axis_index("node")
    other = lax.ppermute(sent, "feat", [(i, i ^ 1) for i in range(groups)])
    pieces = weight_pieces(lax.rem(node, SIDE), kept, other)
    parts = sent_round(pieces, "node", lambda i, s: i // SIDE * SIDE + (i + s) % SIDE)
    parts, own_rows = lax.optimization_barrier((parts, own_rows))
    pieces = added_pieces(lax.div(node, SIDE), parts)
    return sent_round(pieces, "node", lambda i, s: (i + s * SIDE) % (SIDE * SIDE))


def piece_at(pieces, index):
    return lax.dynamic_index_in_dim(pieces, index, 0, keepdims=False)


def weight_total(parts, groups, halo):
    feat = lax.axis_index("feat")
    value = parts[0]
    for part in parts[1:]:
        value = value + part.astype(F32)
    width = value.shape[1]
    half = groups // 2
    while half >= CORES:
        if half == 2 * CORES:
            value, _ = lax.optimization_barrier((value, halo))
        bit = lax.rem(lax.div(feat, half), 2)
        pieces = value.reshape(2, -1, width)
        flip = [(i, i ^ half) for i in range(groups)]
        value = piece_at(pieces, bit) + lax.ppermute(piece_at(pieces, 1 - bit), "feat", flip)
        half //= 2
    core = lax.rem(feat, CORES)
    pieces = value.reshape(CORES, -1, width)
    flip = [(i, i ^ 1) for i in range(groups)]
    other = lax.ppermute(piece_at(pieces, 1 - core), "feat", flip)
    kept = piece_at(pieces, core)
    first, second = jnp.where(core == 0, kept, other), jnp.where(core == 0, other, kept)
    return jnp.concatenate([first, second], axis=1)


def paired(tiles):
    blocks, tile, _ = tiles.shape
    tiles = tiles.reshape(blocks // 2, 2, tile, tile)
    empty = jnp.zeros_like(tiles[:, 0])
    upper = jnp.concatenate([tiles[:, 0], empty], axis=2)
    lower = jnp.concatenate([empty, tiles[:, 1]], axis=2)
    return jnp.concatenate([upper, lower], axis=1)


def local(features, tile_values, tile_cols, tile_count, w_self, w_neigh, cotangent):
    feat_dev, node_dev = features.shape
    tile = tile_values.shape[-1]
    block_count = node_dev // tile
    groups = lax.axis_size("feat")
    size = w_self.shape[0]
    part, feat = lax.axis_index("node"), lax.axis_index("feat")
    col = tile_cols[:, 1] - (part - 1) * block_count
    mine = block_count // groups
    live = lax.dynamic_slice_in_dim(tile_count, feat * mine, mine) > 1
    tiles = lax.dynamic_slice_in_dim(tile_values, feat * mine, mine)
    other = jnp.where(live[:, None, None], tiles[:, 1], jnp.zeros_like(tiles[:, 1]))
    straight = jnp.stack([paired(tiles[:, 0]), paired(other)])
    turned = straight.swapaxes(2, 3)

    before = shifted(features, "node", 1)
    behind = shifted(features, "node", -1)
    x_rows = exchange(split_columns(features, groups), "feat").reshape(size, -1)
    picked = exchange(gather(col, before, features, behind, groups), "feat").reshape(size, -1)
    x_rows, self_back, neigh_back, straight, turned = lax.optimization_barrier(
        (x_rows, w_self.T, w_neigh.T, straight, turned)
    )
    pre_self = self_product(w_self, x_rows)
    core = lax.rem(feat, CORES)
    _, hidden, dpre, dagg, second, sent, kept = dense(
        core[None], straight, turned, x_rows, picked, w_neigh, pre_self, cotangent, neigh_back
    )
    second_cols = exchange(second.reshape(groups, feat_dev, -1), "feat")
    own_rows = own_part(self_back, dpre, dagg, turned, groups)
    terms = weight_terms(sent, kept, groups, own_rows)
    terms, second_cols, own_rows = lax.optimization_barrier((terms, second_cols, own_rows))
    to_before, spread, to_after = scatter(col, second_cols)
    own_cols = exchange(own_rows, "feat")
    from_after = shifted(to_before, "node", -1)
    from_before = shifted(to_after, "node", 1)
    terms, _ = lax.optimization_barrier((terms, spread))
    grad_w_neigh = weight_total(terms, groups, (from_after, from_before))
    grad_features = finish(spread, from_before, from_after, own_cols)
    return (hidden, grad_features, grad_w_neigh)


def solution(mesh):
    placed = (
        P("feat", "node"),
        P("node", None, None, None),
        P("node", None),
        P("node"),
        P(),
        P(),
        P(None, ("node", "feat")),
    )
    return jax.shard_map(
        local,
        mesh=mesh,
        in_specs=placed,
        out_specs=(P(None, ("node", "feat")), P("feat", "node"), P(("node", "feat"), None)),
        check_vma=False,
    )
```

```python
import functools

import jax
import jax.numpy as jnp
from jax import lax
from jax.experimental import pallas as pl
from jax.experimental.pallas import tpu as pltpu
from jax.sharding import PartitionSpec as P

F32 = jnp.float32
BF16 = jnp.bfloat16
NT = (((1,), (1,)), ((), ()))
NN = (((1,), (0,)), ((), ()))
MIB = 1 << 20
DENSE_MIB = 56
OWN_MIB = 60
WEIGHT_MIB = 8
FINAL_MIB = 50
SCATTER_MIB = 56
CHUNK = 512


def dot(a, b, dims=NN):
    return lax.dot_general(a, b, dims, preferred_element_type=F32)


def whole_params(mib):
    return pltpu.CompilerParams(vmem_limit_bytes=mib * MIB)


def params(mib):
    return pltpu.CompilerParams(
        dimension_semantics=("arbitrary",), vmem_limit_bytes=mib * MIB
    )


def split_kernel(x_hbm, out_hbm, held, in_sems, out_sems):
    width = out_hbm.shape[2]
    groups = range(out_hbm.shape[0])
    loads = [
        pltpu.make_async_copy(x_hbm.at[:, g * width : (g + 1) * width], held.at[g], in_sems.at[g])
        for g in groups
    ]
    stores = [pltpu.make_async_copy(held.at[g], out_hbm.at[g], out_sems.at[g]) for g in groups]
    for copy in loads:
        copy.start()
    for load, store in zip(loads, stores):
        load.wait()
        store.start()
    for copy in stores:
        copy.wait()


ANYWHERE = pl.BlockSpec(memory_space=pl.ANY)
SMEM = pl.BlockSpec(memory_space=pltpu.SMEM)
VMEM = pl.BlockSpec(memory_space=pltpu.VMEM)


def split_columns(x, groups):
    rows, columns = x.shape
    return pl.pallas_call(
        split_kernel,
        in_specs=[ANYWHERE],
        out_specs=ANYWHERE,
        out_shape=jax.ShapeDtypeStruct((groups, rows, columns // groups), x.dtype),
        scratch_shapes=[
            pltpu.VMEM((groups, rows, columns // groups), x.dtype),
            pltpu.SemaphoreType.DMA((groups,)),
            pltpu.SemaphoreType.DMA((groups,)),
        ],
        compiler_params=whole_params(60),
    )(x)


def gather_kernel(col_ref, before, own, after, out_hbm, sems):
    tile = 128
    blocks = own.shape[1] // tile
    per = out_hbm.shape[2] // tile

    def target(r):
        place = pl.ds(pl.multiple_of(lax.rem(r, per) * tile, tile), tile)
        return out_hbm.at[lax.div(r, per), :, place]

    def start(r, carry):
        col = col_ref[r]
        for i, part in enumerate((before, own, after)):

            @pl.when((col >= i * blocks) & (col < (i + 1) * blocks))
            def _(i=i, part=part):
                place = pl.ds(pl.multiple_of((col - i * blocks) * tile, tile), tile)
                pltpu.make_async_copy(part.at[:, place], target(r), sems.at[r]).start()

        return carry

    def wait(r, carry):
        pltpu.make_async_copy(own.at[:, :tile], target(r), sems.at[r]).wait()
        return carry

    lax.fori_loop(0, blocks, start, 0)
    lax.fori_loop(0, blocks, wait, 0)


def gather(col, before, own, after, groups):
    rows, span = own.shape
    return pl.pallas_call(
        gather_kernel,
        in_specs=[SMEM] + [ANYWHERE] * 3,
        out_specs=ANYWHERE,
        out_shape=jax.ShapeDtypeStruct((groups, rows, span // groups), BF16),
        scratch_shapes=[pltpu.SemaphoreType.DMA((col.shape[0],))],
        compiler_params=whole_params(2),
        cost_estimate=pl.CostEstimate(flops=0, bytes_accessed=8 * MIB, transcendentals=0),
    )(col, before, own, after)


def scatter_kernel(
    col_ref, parts_hbm, before_hbm, own_hbm, after_hbm, parts_ref, acc, before, after, load_sem, sems
):
    tile = acc.shape[2]
    blocks = own_hbm.shape[0]
    per = parts_ref.shape[2] // tile
    load = pltpu.make_async_copy(parts_hbm, parts_ref, load_sem)
    load.start()

    def clear(i, carry):
        acc[i] = jnp.zeros(acc.shape[1:], F32)
        return carry

    lax.fori_loop(0, acc.shape[0], clear, 0, unroll=8)
    load.wait()

    def add(g, carry):
        for b in range(per):
            acc[col_ref[g * per + b]] += parts_ref[g, :, b * tile : (b + 1) * tile].astype(F32)
        return carry

    lax.fori_loop(0, parts_ref.shape[0], add, 0, unroll=2)
    copies = [
        pltpu.make_async_copy(acc.at[blocks : 2 * blocks], own_hbm, sems.at[0]),
        pltpu.make_async_copy(before, before_hbm, sems.at[1]),
        pltpu.make_async_copy(after, after_hbm, sems.at[2]),
    ]
    copies[0].start()
    for first, out, copy in ((0, before, copies[1]), (2 * blocks, after, copies[2])):

        def cast(i, carry, first=first, out=out):
            out[i] = acc[first + i].astype(BF16)
            return carry

        lax.fori_loop(0, blocks, cast, 0, unroll=8)
        copy.start()
    for copy in copies:
        copy.wait()


def scatter(col, parts):
    groups, rows, width = parts.shape
    blocks = col.shape[0]
    tile = groups * width // blocks
    shape = (blocks, rows, tile)
    return pl.pallas_call(
        scatter_kernel,
        in_specs=[SMEM, ANYWHERE],
        out_specs=[ANYWHERE] * 3,
        out_shape=[
            jax.ShapeDtypeStruct(shape, BF16),
            jax.ShapeDtypeStruct(shape, F32),
            jax.ShapeDtypeStruct(shape, BF16),
        ],
        scratch_shapes=[
            pltpu.VMEM(parts.shape, BF16),
            pltpu.VMEM((3 * blocks, rows, tile), F32),
            pltpu.VMEM(shape, BF16),
            pltpu.VMEM(shape, BF16),
            pltpu.SemaphoreType.DMA(()),
            pltpu.SemaphoreType.DMA((3,)),
        ],
        compiler_params=whole_params(SCATTER_MIB),
        cost_estimate=pl.CostEstimate(flops=0, bytes_accessed=8 * MIB, transcendentals=0),
    )(col, parts)


def self_kernel(chunk, w_self, x_ref, pre):
    for i in range(pre.shape[0] // chunk):
        rows = slice(i * chunk, (i + 1) * chunk)
        pre[rows, :] = dot(w_self[rows, :], x_ref[...])


def self_product(w_self, x_rows):
    size, width = x_rows.shape
    return pl.pallas_call(
        functools.partial(self_kernel, 256),
        in_specs=[VMEM] * 2,
        out_specs=VMEM,
        out_shape=jax.ShapeDtypeStruct((size, width), F32),
        compiler_params=whole_params(60),
        cost_estimate=pl.CostEstimate(
            flops=2 * size * size * width, bytes_accessed=5 * MIB, transcendentals=0
        ),
    )(w_self, x_rows)


def dense_kernel(chunk, *refs):
    core_ref, sources, targets, held = refs[0], refs[1:9], refs[9:16], refs[16:24]
    (agg_hbm, hidden_hbm, dpre_hbm, dagg_hbm, second_hbm, sent_hbm, kept_hbm) = targets
    (tiles, turned, x_ref, picked, w_neigh, pre_ref, cot_ref, w_back) = held
    (agg, hidden, dpre, dagg, second, sent, kept, in_sems, out_sems) = refs[24:]
    size = w_neigh.shape[0]
    pair = tiles.shape[-1]
    part = [slice(i, i + chunk) for i in range(0, size, chunk)]
    here = [slice(i, i + pair) for i in range(0, agg.shape[1], pair)]
    loads = [
        pltpu.make_async_copy(sources[k], held[k], in_sems.at[k]) for k in (0, 2, 3, 4, 5, 6, 7, 1)
    ]
    for copy in loads:
        copy.start()
    stores = []

    def store(k, src, dst, i):
        copy = pltpu.make_async_copy(src.at[part[i]], dst.at[part[i]], out_sems.at[k, i])
        copy.start()
        stores.append(copy)

    for copy in loads[:3]:
        copy.wait()
    for i in range(len(part)):
        for p in range(len(here)):
            total = dot(x_ref[part[i], here[p]], tiles[0, p])
            total = total + dot(picked[part[i], here[p]], tiles[1, p])
            agg[part[i], here[p]] = total.astype(BF16)
    for copy in loads[3:6]:
        copy.wait()
    for i in range(len(part)):
        store(0, agg, agg_hbm, i)
        pre = pre_ref[part[i], :] + dot(w_neigh[part[i], :], agg[...])
        sig = 0.5 + 0.5 * jnp.tanh(0.5 * pre)
        hidden[part[i], :] = (pre * sig).astype(BF16)
        slope = sig * (1.0 + pre * (1.0 - sig))
        dpre[part[i], :] = (cot_ref[part[i], :].astype(F32) * slope).astype(BF16)
    for copy in loads[6:]:
        copy.wait()
    for i in range(len(part)):
        store(1, hidden, hidden_hbm, i)
        store(2, dpre, dpre_hbm, i)
        dagg[part[i], :] = dot(w_back[part[i], :], dpre[...]).astype(BF16)
        for p in range(len(here)):
            second[part[i], here[p]] = dot(dagg[part[i], here[p]], turned[1, p]).astype(BF16)
        store(3, dagg, dagg_hbm, i)
        store(4, second, second_hbm, i)
    width = sent.shape[1]
    core = core_ref[0]
    for k, owner, out, target in ((5, 1 - core, sent, sent_hbm), (6, core, kept, kept_hbm)):
        half = agg.at[pl.ds(pl.multiple_of(owner * width, width), width)]
        for i in range(len(part)):
            out[part[i], :] = dot(dpre[part[i], :], half[...], NT).astype(BF16)
            store(k, out, target, i)
    for copy in stores:
        copy.wait()


def dense(core, tiles, turned, x_rows, picked, w_neigh, pre_self, cot, w_back):
    size, width = picked.shape
    chunk = CHUNK
    out = jax.ShapeDtypeStruct((size, width), BF16)
    args = (tiles, turned, x_rows, picked, w_neigh, pre_self, cot, w_back)
    return pl.pallas_call(
        functools.partial(dense_kernel, chunk),
        in_specs=[SMEM] + [ANYWHERE] * len(args),
        out_specs=[ANYWHERE] * 7,
        out_shape=[out] * 5 + [jax.ShapeDtypeStruct((size, size // CORES), BF16)] * 2,
        scratch_shapes=[pltpu.VMEM(arg.shape, arg.dtype) for arg in args]
        + [pltpu.VMEM((size, width), BF16)] * 5
        + [pltpu.VMEM((size, size // CORES), BF16)] * 2
        + [pltpu.SemaphoreType.DMA((len(args),)), pltpu.SemaphoreType.DMA((7, size // chunk))],
        compiler_params=whole_params(DENSE_MIB),
        cost_estimate=pl.CostEstimate(
            flops=4 * size * size * width, bytes_accessed=16 * MIB, transcendentals=size * width
        ),
    )(core, *args)


EXTRA = 8


def own_kernel(chunk, w_back, dpre, dagg_ref, turned, own):
    pair = turned.shape[-1]
    each = own.shape[1] - EXTRA
    for i in range(0, dpre.shape[0], chunk):
        rows = slice(i, i + chunk)
        dself = dot(w_back[rows, :], dpre[...])
        for p in range(own.shape[2] // pair):
            here = slice(p * pair, (p + 1) * pair)
            total = dself[:, here] + dot(dagg_ref[rows, here], turned[0, p])
            for g in range(chunk // each):
                own[i // each + g, :each, here] = total[g * each : (g + 1) * each].astype(BF16)


def own_part(w_back, dpre, dagg, turned, groups):
    size, width = dpre.shape
    return pl.pallas_call(
        functools.partial(own_kernel, 256),
        in_specs=[VMEM] * 4,
        out_specs=VMEM,
        out_shape=jax.ShapeDtypeStruct((groups, size // groups + EXTRA, width), BF16),
        compiler_params=whole_params(OWN_MIB),
        cost_estimate=pl.CostEstimate(
            flops=2 * size * size * width, bytes_accessed=5 * MIB, transcendentals=0
        ),
    )(w_back, dpre, dagg, turned)


def weight_kernel(me_ref, kept_ref, other_ref, *outs):
    rows = outs[0].shape[0]
    each = rows // SIDE
    for step, out in enumerate(outs):
        first = lax.rem(me_ref[0] + step, SIDE) * each
        for i in range(SIDE):
            there = pl.ds(pl.multiple_of(i * rows + first, each), each)
            total = kept_ref[there, :].astype(F32) + other_ref[there, :].astype(F32)
            out[i * each : (i + 1) * each, :] = total.astype(out.dtype)


def weight_pieces(me, kept, other):
    size, width = kept.shape
    shape = (size // SIDE, width)
    return pl.pallas_call(
        weight_kernel,
        in_specs=[SMEM] + [VMEM] * 2,
        out_specs=[VMEM] * SIDE,
        out_shape=[jax.ShapeDtypeStruct(shape, F32)]
        + [jax.ShapeDtypeStruct(shape, BF16)] * (SIDE - 1),
        compiler_params=whole_params(WEIGHT_MIB),
        cost_estimate=pl.CostEstimate(flops=0, bytes_accessed=4 * MIB, transcendentals=0),
    )(me[None], kept, other)


def add_kernel(index_ref, *refs):
    parts, outs = refs[:SIDE], refs[SIDE:]
    rows = outs[0].shape[0]
    for step, out in enumerate(outs):
        here = pl.ds(pl.multiple_of(lax.rem(index_ref[0] + step, SIDE) * rows, rows), rows)
        total = parts[0][here, :]
        for part in parts[1:]:
            total = total + part[here, :].astype(F32)
        out[...] = total.astype(out.dtype)


def added_pieces(me, parts):
    rows, width = parts[0].shape
    shape = (rows // SIDE, width)
    return pl.pallas_call(
        add_kernel,
        in_specs=[SMEM] + [VMEM] * SIDE,
        out_specs=[VMEM] * SIDE,
        out_shape=[jax.ShapeDtypeStruct(shape, F32)]
        + [jax.ShapeDtypeStruct(shape, BF16)] * (SIDE - 1),
        compiler_params=whole_params(WEIGHT_MIB),
        cost_estimate=pl.CostEstimate(flops=0, bytes_accessed=2 * MIB, transcendentals=0),
    )(me[None], *parts)


def final_kernel(own_ref, before_ref, after_ref, dself_ref, out_ref):
    tile = own_ref.shape[2]
    per = dself_ref.shape[2] // tile
    for b in range(own_ref.shape[0]):
        grad = dself_ref[b // per, : own_ref.shape[1], (b % per) * tile : (b % per + 1) * tile]
        total = own_ref[b] + before_ref[b].astype(F32) + after_ref[b].astype(F32)
        out_ref[:, b * tile : (b + 1) * tile] = (grad.astype(F32) + total).astype(BF16)


def finish(own, before, after, dself):
    groups, high, width = dself.shape
    blocks, rows, tile = own.shape
    steps = 4
    part = pl.BlockSpec((blocks // steps, rows, tile), lambda g: (g, 0, 0))
    return pl.pallas_call(
        final_kernel,
        grid=(steps,),
        in_specs=[part, part, part]
        + [pl.BlockSpec((groups // steps, high, width), lambda g: (g, 0, 0))],
        out_specs=pl.BlockSpec((rows, groups * width // steps), lambda g: (0, g)),
        out_shape=jax.ShapeDtypeStruct((rows, groups * width), BF16),
        compiler_params=params(FINAL_MIB),
    )(own, before, after, dself)


def shifted(value, axis, steps):
    count = lax.axis_size(axis)
    first, last = max(0, -steps), min(count, count - steps)
    return lax.ppermute(value, axis, [(source, source + steps) for source in range(first, last)])


def exchange(value, axis):
    return lax.all_to_all(value, axis, split_axis=0, concat_axis=0, tiled=True)


SIDE = 4
CORES = 2


def sent_round(pieces, axis, partner):
    count = lax.axis_size(axis)
    return [pieces[0]] + [
        lax.ppermute(piece, axis, [(i, partner(i, step + 1)) for i in range(count)])
        for step, piece in enumerate(pieces[1:])
    ]


def weight_rows(sent, kept, groups, own_rows):
    node = lax.axis_index("node")
    other = lax.ppermute(sent, "feat", [(i, i ^ 1) for i in range(groups)])
    pieces = weight_pieces(lax.rem(node, SIDE), kept, other)
    parts = sent_round(pieces, "node", lambda i, s: i // SIDE * SIDE + (i + s) % SIDE)
    parts, own_rows = lax.optimization_barrier((parts, own_rows))
    pieces = added_pieces(lax.div(node, SIDE), parts)
    parts = sent_round(pieces, "node", lambda i, s: (i + s * SIDE) % (SIDE * SIDE))
    total = parts[0]
    for part in parts[1:]:
        total = total + part.astype(F32)
    total = total.reshape(groups, EXTRA // 2, -1)
    high = total.astype(BF16)
    low = (total - high.astype(F32)).astype(BF16)
    rows = jnp.concatenate([high, low], axis=1)
    return lax.dynamic_update_slice(own_rows, rows, (0, own_rows.shape[1] - EXTRA, 0))


def weight_total(rows):
    groups, count, width = rows.shape
    rows = rows.astype(F32).reshape(groups // CORES, CORES, 2, count // 2, width)
    total = jnp.sum(rows, axis=(0, 2))
    return jnp.concatenate([total[i] for i in range(CORES)], axis=1)


def paired(tiles):
    blocks, tile, _ = tiles.shape
    tiles = tiles.reshape(blocks // 2, 2, tile, tile)
    empty = jnp.zeros_like(tiles[:, 0])
    upper = jnp.concatenate([tiles[:, 0], empty], axis=2)
    lower = jnp.concatenate([empty, tiles[:, 1]], axis=2)
    return jnp.concatenate([upper, lower], axis=1)


def local(features, tile_values, tile_cols, tile_count, w_self, w_neigh, cotangent):
    feat_dev, node_dev = features.shape
    tile = tile_values.shape[-1]
    block_count = node_dev // tile
    groups = lax.axis_size("feat")
    size = w_self.shape[0]
    part, feat = lax.axis_index("node"), lax.axis_index("feat")
    col = tile_cols[:, 1] - (part - 1) * block_count
    mine = block_count // groups
    live = lax.dynamic_slice_in_dim(tile_count, feat * mine, mine) > 1
    tiles = lax.dynamic_slice_in_dim(tile_values, feat * mine, mine)
    other = jnp.where(live[:, None, None], tiles[:, 1], jnp.zeros_like(tiles[:, 1]))
    straight = jnp.stack([paired(tiles[:, 0]), paired(other)])
    turned = straight.swapaxes(2, 3)

    before = shifted(features, "node", 1)
    behind = shifted(features, "node", -1)
    x_rows = exchange(split_columns(features, groups), "feat").reshape(size, -1)
    picked = exchange(gather(col, before, features, behind, groups), "feat").reshape(size, -1)
    x_rows, self_back, neigh_back, straight, turned = lax.optimization_barrier(
        (x_rows, w_self.T, w_neigh.T, straight, turned)
    )
    pre_self = self_product(w_self, x_rows)
    core = lax.rem(feat, CORES)
    _, hidden, dpre, dagg, second, sent, kept = dense(
        core[None], straight, turned, x_rows, picked, w_neigh, pre_self, cotangent, neigh_back
    )
    second_cols = exchange(second.reshape(groups, feat_dev, -1), "feat")
    own_rows = own_part(self_back, dpre, dagg, turned, groups)
    own_cols = exchange(weight_rows(sent, kept, groups, own_rows), "feat")
    to_before, spread, to_after = scatter(col, second_cols)
    from_after = shifted(to_before, "node", -1)
    from_before = shifted(to_after, "node", 1)
    grad_w_neigh = weight_total(own_cols[:, feat_dev:])
    grad_features = finish(spread, from_before, from_after, own_cols)
    return (hidden, grad_features, grad_w_neigh)


def solution(mesh):
    placed = (
        P("feat", "node"),
        P("node", None, None, None),
        P("node", None),
        P("node"),
        P(),
        P(),
        P(None, ("node", "feat")),
    )
    return jax.shard_map(
        local,
        mesh=mesh,
        in_specs=placed,
        out_specs=(P(None, ("node", "feat")), P("feat", "node"), P(("node", "feat"), None)),
        check_vma=False,
    )
```

```python
import functools

import jax
import jax.numpy as jnp
from jax import lax
from jax.experimental import pallas as pl
from jax.experimental.pallas import tpu as pltpu
from jax.sharding import PartitionSpec as P

F32 = jnp.float32
BF16 = jnp.bfloat16
NT = (((1,), (1,)), ((), ()))
NN = (((1,), (0,)), ((), ()))
MIB = 1 << 20
DENSE_MIB = 56
OWN_MIB = 60
WEIGHT_MIB = 8
FINAL_MIB = 16
SCATTER_MIB = 56
CHUNK = 512


def dot(a, b, dims=NN):
    return lax.dot_general(a, b, dims, preferred_element_type=F32)


def whole_params(mib):
    return pltpu.CompilerParams(vmem_limit_bytes=mib * MIB)


def params(mib):
    return pltpu.CompilerParams(
        dimension_semantics=("arbitrary",), vmem_limit_bytes=mib * MIB
    )


def split_kernel(x_hbm, out_hbm, held, in_sems, out_sems):
    width = out_hbm.shape[2]
    groups = range(out_hbm.shape[0])
    loads = [
        pltpu.make_async_copy(x_hbm.at[:, g * width : (g + 1) * width], held.at[g], in_sems.at[g])
        for g in groups
    ]
    stores = [pltpu.make_async_copy(held.at[g], out_hbm.at[g], out_sems.at[g]) for g in groups]
    for copy in loads:
        copy.start()
    for load, store in zip(loads, stores):
        load.wait()
        store.start()
    for copy in stores:
        copy.wait()


ANYWHERE = pl.BlockSpec(memory_space=pl.ANY)
SMEM = pl.BlockSpec(memory_space=pltpu.SMEM)
VMEM = pl.BlockSpec(memory_space=pltpu.VMEM)


def split_columns(x, groups):
    rows, columns = x.shape
    return pl.pallas_call(
        split_kernel,
        in_specs=[ANYWHERE],
        out_specs=ANYWHERE,
        out_shape=jax.ShapeDtypeStruct((groups, rows, columns // groups), x.dtype),
        scratch_shapes=[
            pltpu.VMEM((groups, rows, columns // groups), x.dtype),
            pltpu.SemaphoreType.DMA((groups,)),
            pltpu.SemaphoreType.DMA((groups,)),
        ],
        compiler_params=whole_params(60),
    )(x)


def gather_kernel(col_ref, before, own, after, out_hbm, sems):
    tile = 128
    blocks = own.shape[1] // tile
    per = out_hbm.shape[2] // tile

    def target(r):
        place = pl.ds(pl.multiple_of(lax.rem(r, per) * tile, tile), tile)
        return out_hbm.at[lax.div(r, per), :, place]

    def start(r, carry):
        col = col_ref[r]
        for i, part in enumerate((before, own, after)):

            @pl.when((col >= i * blocks) & (col < (i + 1) * blocks))
            def _(i=i, part=part):
                place = pl.ds(pl.multiple_of((col - i * blocks) * tile, tile), tile)
                pltpu.make_async_copy(part.at[:, place], target(r), sems.at[r]).start()

        return carry

    def wait(r, carry):
        pltpu.make_async_copy(own.at[:, :tile], target(r), sems.at[r]).wait()
        return carry

    lax.fori_loop(0, blocks, start, 0)
    lax.fori_loop(0, blocks, wait, 0)


def gather(col, before, own, after, groups):
    rows, span = own.shape
    return pl.pallas_call(
        gather_kernel,
        in_specs=[SMEM] + [ANYWHERE] * 3,
        out_specs=ANYWHERE,
        out_shape=jax.ShapeDtypeStruct((groups, rows, span // groups), BF16),
        scratch_shapes=[pltpu.SemaphoreType.DMA((col.shape[0],))],
        compiler_params=whole_params(2),
        cost_estimate=pl.CostEstimate(flops=0, bytes_accessed=8 * MIB, transcendentals=0),
    )(col, before, own, after)


def scatter_kernel(
    col_ref, parts_hbm, before_hbm, own_hbm, after_hbm, parts_ref, acc, before, after, load_sem, sems
):
    tile = acc.shape[2]
    blocks = own_hbm.shape[0]
    per = parts_ref.shape[2] // tile
    load = pltpu.make_async_copy(parts_hbm, parts_ref, load_sem)
    load.start()

    def clear(i, carry):
        acc[i] = jnp.zeros(acc.shape[1:], F32)
        return carry

    lax.fori_loop(0, acc.shape[0], clear, 0, unroll=8)
    load.wait()

    def add(g, carry):
        for b in range(per):
            acc[col_ref[g * per + b]] += parts_ref[g, :, b * tile : (b + 1) * tile].astype(F32)
        return carry

    lax.fori_loop(0, parts_ref.shape[0], add, 0, unroll=2)
    copies = [
        pltpu.make_async_copy(acc.at[blocks : 2 * blocks], own_hbm, sems.at[0]),
        pltpu.make_async_copy(before, before_hbm, sems.at[1]),
        pltpu.make_async_copy(after, after_hbm, sems.at[2]),
    ]
    copies[0].start()
    for first, out, copy in ((0, before, copies[1]), (2 * blocks, after, copies[2])):

        def cast(i, carry, first=first, out=out):
            out[i] = acc[first + i].astype(BF16)
            return carry

        lax.fori_loop(0, blocks, cast, 0, unroll=8)
        copy.start()
    for copy in copies:
        copy.wait()


def scatter(col, parts):
    groups, rows, width = parts.shape
    blocks = col.shape[0]
    tile = groups * width // blocks
    shape = (blocks, rows, tile)
    return pl.pallas_call(
        scatter_kernel,
        in_specs=[SMEM, ANYWHERE],
        out_specs=[ANYWHERE] * 3,
        out_shape=[
            jax.ShapeDtypeStruct(shape, BF16),
            jax.ShapeDtypeStruct(shape, F32),
            jax.ShapeDtypeStruct(shape, BF16),
        ],
        scratch_shapes=[
            pltpu.VMEM(parts.shape, BF16),
            pltpu.VMEM((3 * blocks, rows, tile), F32),
            pltpu.VMEM(shape, BF16),
            pltpu.VMEM(shape, BF16),
            pltpu.SemaphoreType.DMA(()),
            pltpu.SemaphoreType.DMA((3,)),
        ],
        compiler_params=whole_params(SCATTER_MIB),
        cost_estimate=pl.CostEstimate(flops=0, bytes_accessed=8 * MIB, transcendentals=0),
    )(col, parts)


def self_kernel(chunk, w_self, x_ref, pre):
    for i in range(pre.shape[0] // chunk):
        rows = slice(i * chunk, (i + 1) * chunk)
        pre[rows, :] = dot(w_self[rows, :], x_ref[...])


def self_product(w_self, x_rows):
    size, width = x_rows.shape
    return pl.pallas_call(
        functools.partial(self_kernel, 256),
        in_specs=[VMEM] * 2,
        out_specs=VMEM,
        out_shape=jax.ShapeDtypeStruct((size, width), F32),
        compiler_params=whole_params(60),
        cost_estimate=pl.CostEstimate(
            flops=2 * size * size * width, bytes_accessed=5 * MIB, transcendentals=0
        ),
    )(w_self, x_rows)


def dense_kernel(chunk, *refs):
    core_ref, sources, targets, held = refs[0], refs[1:9], refs[9:16], refs[16:24]
    (agg_hbm, hidden_hbm, dpre_hbm, dagg_hbm, second_hbm, sent_hbm, kept_hbm) = targets
    (tiles, turned, x_ref, picked, w_neigh, pre_ref, cot_ref, w_back) = held
    (agg, hidden, dpre, dagg, second, sent, kept, in_sems, out_sems) = refs[24:]
    size = w_neigh.shape[0]
    pair = tiles.shape[-1]
    part = [slice(i, i + chunk) for i in range(0, size, chunk)]
    here = [slice(i, i + pair) for i in range(0, agg.shape[1], pair)]
    loads = [
        pltpu.make_async_copy(sources[k], held[k], in_sems.at[k]) for k in (0, 2, 3, 4, 5, 6, 7, 1)
    ]
    for copy in loads:
        copy.start()
    stores = []

    def store(k, src, dst, i):
        copy = pltpu.make_async_copy(src.at[part[i]], dst.at[part[i]], out_sems.at[k, i])
        copy.start()
        stores.append(copy)

    for copy in loads[:3]:
        copy.wait()
    for i in range(len(part)):
        for p in range(len(here)):
            total = dot(x_ref[part[i], here[p]], tiles[0, p])
            total = total + dot(picked[part[i], here[p]], tiles[1, p])
            agg[part[i], here[p]] = total.astype(BF16)
    for copy in loads[3:6]:
        copy.wait()
    for i in range(len(part)):
        store(0, agg, agg_hbm, i)
        pre = pre_ref[part[i], :] + dot(w_neigh[part[i], :], agg[...])
        sig = 0.5 + 0.5 * jnp.tanh(0.5 * pre)
        hidden[part[i], :] = (pre * sig).astype(BF16)
        slope = sig * (1.0 + pre * (1.0 - sig))
        dpre[part[i], :] = (cot_ref[part[i], :].astype(F32) * slope).astype(BF16)
    for copy in loads[6:]:
        copy.wait()
    for i in range(len(part)):
        store(1, hidden, hidden_hbm, i)
        store(2, dpre, dpre_hbm, i)
        dagg[part[i], :] = dot(w_back[part[i], :], dpre[...]).astype(BF16)
        for p in range(len(here)):
            second[part[i], here[p]] = dot(dagg[part[i], here[p]], turned[1, p]).astype(BF16)
        store(3, dagg, dagg_hbm, i)
        store(4, second, second_hbm, i)
    width = sent.shape[1]
    core = core_ref[0]
    for k, owner, out, target in ((5, 1 - core, sent, sent_hbm), (6, core, kept, kept_hbm)):
        half = agg.at[pl.ds(pl.multiple_of(owner * width, width), width)]
        for i in range(len(part)):
            out[part[i], :] = dot(dpre[part[i], :], half[...], NT).astype(BF16)
            store(k, out, target, i)
    for copy in stores:
        copy.wait()


def dense(core, tiles, turned, x_rows, picked, w_neigh, pre_self, cot, w_back):
    size, width = picked.shape
    chunk = CHUNK
    out = jax.ShapeDtypeStruct((size, width), BF16)
    args = (tiles, turned, x_rows, picked, w_neigh, pre_self, cot, w_back)
    return pl.pallas_call(
        functools.partial(dense_kernel, chunk),
        in_specs=[SMEM] + [ANYWHERE] * len(args),
        out_specs=[ANYWHERE] * 7,
        out_shape=[out] * 5 + [jax.ShapeDtypeStruct((size, size // CORES), BF16)] * 2,
        scratch_shapes=[pltpu.VMEM(arg.shape, arg.dtype) for arg in args]
        + [pltpu.VMEM((size, width), BF16)] * 5
        + [pltpu.VMEM((size, size // CORES), BF16)] * 2
        + [pltpu.SemaphoreType.DMA((len(args),)), pltpu.SemaphoreType.DMA((7, size // chunk))],
        compiler_params=whole_params(DENSE_MIB),
        cost_estimate=pl.CostEstimate(
            flops=4 * size * size * width, bytes_accessed=16 * MIB, transcendentals=size * width
        ),
    )(core, *args)


EXTRA = 8


def own_kernel(chunk, w_back, dpre, dagg_ref, turned, own):
    pair = turned.shape[-1]
    each = own.shape[1] - EXTRA
    for i in range(0, dpre.shape[0], chunk):
        rows = slice(i, i + chunk)
        dself = dot(w_back[rows, :], dpre[...])
        for p in range(own.shape[2] // pair):
            here = slice(p * pair, (p + 1) * pair)
            total = dself[:, here] + dot(dagg_ref[rows, here], turned[0, p])
            for g in range(chunk // each):
                own[i // each + g, :each, here] = total[g * each : (g + 1) * each].astype(BF16)


def own_part(w_back, dpre, dagg, turned, groups):
    size, width = dpre.shape
    return pl.pallas_call(
        functools.partial(own_kernel, 256),
        in_specs=[VMEM] * 4,
        out_specs=VMEM,
        out_shape=jax.ShapeDtypeStruct((groups, size // groups + EXTRA, width), BF16),
        compiler_params=whole_params(OWN_MIB),
        cost_estimate=pl.CostEstimate(
            flops=2 * size * size * width, bytes_accessed=5 * MIB, transcendentals=0
        ),
    )(w_back, dpre, dagg, turned)


def weight_kernel(me_ref, kept_ref, other_ref, *outs):
    rows = outs[0].shape[0]
    each = rows // SIDE
    for step, out in enumerate(outs):
        first = lax.rem(me_ref[0] + step, SIDE) * each
        for i in range(SIDE):
            there = pl.ds(pl.multiple_of(i * rows + first, each), each)
            total = kept_ref[there, :].astype(F32) + other_ref[there, :].astype(F32)
            out[i * each : (i + 1) * each, :] = total.astype(out.dtype)


def weight_pieces(me, kept, other):
    size, width = kept.shape
    shape = (size // SIDE, width)
    return pl.pallas_call(
        weight_kernel,
        in_specs=[SMEM] + [VMEM] * 2,
        out_specs=[VMEM] * SIDE,
        out_shape=[jax.ShapeDtypeStruct(shape, F32)]
        + [jax.ShapeDtypeStruct(shape, BF16)] * (SIDE - 1),
        compiler_params=whole_params(WEIGHT_MIB),
        cost_estimate=pl.CostEstimate(flops=0, bytes_accessed=4 * MIB, transcendentals=0),
    )(me[None], kept, other)


def add_kernel(index_ref, *refs):
    parts, outs = refs[:SIDE], refs[SIDE:]
    rows = outs[0].shape[0]
    for step, out in enumerate(outs):
        here = pl.ds(pl.multiple_of(lax.rem(index_ref[0] + step, SIDE) * rows, rows), rows)
        total = parts[0][here, :]
        for part in parts[1:]:
            total = total + part[here, :].astype(F32)
        out[...] = total.astype(out.dtype)


def added_pieces(me, parts):
    rows, width = parts[0].shape
    shape = (rows // SIDE, width)
    return pl.pallas_call(
        add_kernel,
        in_specs=[SMEM] + [VMEM] * SIDE,
        out_specs=[VMEM] * SIDE,
        out_shape=[jax.ShapeDtypeStruct(shape, F32)]
        + [jax.ShapeDtypeStruct(shape, BF16)] * (SIDE - 1),
        compiler_params=whole_params(WEIGHT_MIB),
        cost_estimate=pl.CostEstimate(flops=0, bytes_accessed=2 * MIB, transcendentals=0),
    )(me[None], *parts)


def base_kernel(spread_ref, own_ref, out_ref):
    rows, tile = spread_ref.shape[1:]
    per = own_ref.shape[2] // tile
    for b in range(spread_ref.shape[0]):
        part = own_ref[b // per, :rows, (b % per) * tile : (b % per + 1) * tile]
        out_ref[b] = spread_ref[b] + part.astype(F32)


def based(spread, own):
    groups, high, width = own.shape
    blocks, rows, tile = spread.shape
    steps = 4
    part = pl.BlockSpec((blocks // steps, rows, tile), lambda g: (g, 0, 0))
    return pl.pallas_call(
        base_kernel,
        grid=(steps,),
        in_specs=[part, pl.BlockSpec((groups // steps, high, width), lambda g: (g, 0, 0))],
        out_specs=part,
        out_shape=jax.ShapeDtypeStruct(spread.shape, F32),
        compiler_params=params(FINAL_MIB),
    )(spread, own)


def final_kernel(base_ref, before_ref, after_ref, out_ref):
    tile = base_ref.shape[2]
    for b in range(base_ref.shape[0]):
        total = base_ref[b] + before_ref[b].astype(F32) + after_ref[b].astype(F32)
        out_ref[:, b * tile : (b + 1) * tile] = total.astype(BF16)


def finish(base, before, after):
    blocks, rows, tile = base.shape
    steps = 4
    part = pl.BlockSpec((blocks // steps, rows, tile), lambda g: (g, 0, 0))
    return pl.pallas_call(
        final_kernel,
        grid=(steps,),
        in_specs=[part, part, part],
        out_specs=pl.BlockSpec((rows, blocks * tile // steps), lambda g: (0, g)),
        out_shape=jax.ShapeDtypeStruct((rows, blocks * tile), BF16),
        compiler_params=params(FINAL_MIB),
    )(base, before, after)


def shifted(value, axis, steps):
    count = lax.axis_size(axis)
    first, last = max(0, -steps), min(count, count - steps)
    return lax.ppermute(value, axis, [(source, source + steps) for source in range(first, last)])


def exchange(value, axis):
    return lax.all_to_all(value, axis, split_axis=0, concat_axis=0, tiled=True)


SIDE = 4
CORES = 2


def sent_round(pieces, axis, partner):
    count = lax.axis_size(axis)
    return [pieces[0]] + [
        lax.ppermute(piece, axis, [(i, partner(i, step + 1)) for i in range(count)])
        for step, piece in enumerate(pieces[1:])
    ]


def weight_rows(sent, kept, groups, own_rows, spread):
    node = lax.axis_index("node")
    other = lax.ppermute(sent, "feat", [(i, i ^ 1) for i in range(groups)])
    pieces = weight_pieces(lax.rem(node, SIDE), kept, other)
    parts = sent_round(pieces, "node", lambda i, s: i // SIDE * SIDE + (i + s) % SIDE)
    parts, own_rows = lax.optimization_barrier((parts, own_rows))
    pieces = added_pieces(lax.div(node, SIDE), parts)
    parts = sent_round(pieces, "node", lambda i, s: (i + s * SIDE) % (SIDE * SIDE))
    parts, _ = lax.optimization_barrier((parts, spread))
    total = parts[0]
    for part in parts[1:]:
        total = total + part.astype(F32)
    total = total.reshape(groups, EXTRA // 2, -1)
    high = total.astype(BF16)
    low = (total - high.astype(F32)).astype(BF16)
    rows = jnp.concatenate([high, low], axis=1)
    return lax.dynamic_update_slice(own_rows, rows, (0, own_rows.shape[1] - EXTRA, 0))


def weight_total(rows):
    groups, count, width = rows.shape
    rows = rows.astype(F32).reshape(groups // CORES, CORES, 2, count // 2, width)
    total = jnp.sum(rows, axis=(0, 2))
    return jnp.concatenate([total[i] for i in range(CORES)], axis=1)


def paired(tiles):
    blocks, tile, _ = tiles.shape
    tiles = tiles.reshape(blocks // 2, 2, tile, tile)
    empty = jnp.zeros_like(tiles[:, 0])
    upper = jnp.concatenate([tiles[:, 0], empty], axis=2)
    lower = jnp.concatenate([empty, tiles[:, 1]], axis=2)
    return jnp.concatenate([upper, lower], axis=1)


def local(features, tile_values, tile_cols, tile_count, w_self, w_neigh, cotangent):
    feat_dev, node_dev = features.shape
    tile = tile_values.shape[-1]
    block_count = node_dev // tile
    groups = lax.axis_size("feat")
    size = w_self.shape[0]
    part, feat = lax.axis_index("node"), lax.axis_index("feat")
    col = tile_cols[:, 1] - (part - 1) * block_count
    mine = block_count // groups
    live = lax.dynamic_slice_in_dim(tile_count, feat * mine, mine) > 1
    tiles = lax.dynamic_slice_in_dim(tile_values, feat * mine, mine)
    other = jnp.where(live[:, None, None], tiles[:, 1], jnp.zeros_like(tiles[:, 1]))
    straight = jnp.stack([paired(tiles[:, 0]), paired(other)])
    turned = straight.swapaxes(2, 3)

    before = shifted(features, "node", 1)
    behind = shifted(features, "node", -1)
    x_rows = exchange(split_columns(features, groups), "feat").reshape(size, -1)
    picked = exchange(gather(col, before, features, behind, groups), "feat").reshape(size, -1)
    x_rows, self_back, neigh_back, straight, turned = lax.optimization_barrier(
        (x_rows, w_self.T, w_neigh.T, straight, turned)
    )
    pre_self = self_product(w_self, x_rows)
    core = lax.rem(feat, CORES)
    _, hidden, dpre, dagg, second, sent, kept = dense(
        core[None], straight, turned, x_rows, picked, w_neigh, pre_self, cotangent, neigh_back
    )
    second_cols = exchange(second.reshape(groups, feat_dev, -1), "feat")
    own_rows = own_part(self_back, dpre, dagg, turned, groups)
    to_before, spread, to_after = scatter(col, second_cols)
    own_cols = exchange(weight_rows(sent, kept, groups, own_rows, spread), "feat")
    from_after = shifted(to_before, "node", -1)
    from_before = shifted(to_after, "node", 1)
    grad_w_neigh = weight_total(own_cols[:, feat_dev:])
    grad_features = finish(based(spread, own_cols), from_before, from_after)
    return (hidden, grad_features, grad_w_neigh)


def solution(mesh):
    placed = (
        P("feat", "node"),
        P("node", None, None, None),
        P("node", None),
        P("node"),
        P(),
        P(),
        P(None, ("node", "feat")),
    )
    return jax.shard_map(
        local,
        mesh=mesh,
        in_specs=placed,
        out_specs=(P(None, ("node", "feat")), P("feat", "node"), P(("node", "feat"), None)),
        check_vma=False,
    )
```

```python
import functools

import jax
import jax.numpy as jnp
from jax import lax
from jax.experimental import pallas as pl
from jax.experimental.pallas import tpu as pltpu
from jax.sharding import PartitionSpec as P

F32 = jnp.float32
BF16 = jnp.bfloat16
NT = (((1,), (1,)), ((), ()))
NN = (((1,), (0,)), ((), ()))
MIB = 1 << 20
DENSE_MIB = 56
OWN_MIB = 60
WEIGHT_MIB = 8
FINAL_MIB = 16
SCATTER_MIB = 56
CHUNK = 512


def dot(a, b, dims=NN):
    return lax.dot_general(a, b, dims, preferred_element_type=F32)


def whole_params(mib):
    return pltpu.CompilerParams(vmem_limit_bytes=mib * MIB)


def params(mib):
    return pltpu.CompilerParams(
        dimension_semantics=("arbitrary",), vmem_limit_bytes=mib * MIB
    )


def split_kernel(x_hbm, out_hbm, held, in_sems, out_sems):
    width = out_hbm.shape[2]
    groups = range(out_hbm.shape[0])
    loads = [
        pltpu.make_async_copy(x_hbm.at[:, g * width : (g + 1) * width], held.at[g], in_sems.at[g])
        for g in groups
    ]
    stores = [pltpu.make_async_copy(held.at[g], out_hbm.at[g], out_sems.at[g]) for g in groups]
    for copy in loads:
        copy.start()
    for load, store in zip(loads, stores):
        load.wait()
        store.start()
    for copy in stores:
        copy.wait()


ANYWHERE = pl.BlockSpec(memory_space=pl.ANY)
SMEM = pl.BlockSpec(memory_space=pltpu.SMEM)
VMEM = pl.BlockSpec(memory_space=pltpu.VMEM)


def split_columns(x, groups):
    rows, columns = x.shape
    return pl.pallas_call(
        split_kernel,
        in_specs=[ANYWHERE],
        out_specs=ANYWHERE,
        out_shape=jax.ShapeDtypeStruct((groups, rows, columns // groups), x.dtype),
        scratch_shapes=[
            pltpu.VMEM((groups, rows, columns // groups), x.dtype),
            pltpu.SemaphoreType.DMA((groups,)),
            pltpu.SemaphoreType.DMA((groups,)),
        ],
        compiler_params=whole_params(60),
    )(x)


def gather_kernel(col_ref, before, own, after, out_hbm, sems):
    tile = 128
    blocks = own.shape[1] // tile
    per = out_hbm.shape[2] // tile

    def target(r):
        place = pl.ds(pl.multiple_of(lax.rem(r, per) * tile, tile), tile)
        return out_hbm.at[lax.div(r, per), :, place]

    def start(r, carry):
        col = col_ref[r]
        for i, part in enumerate((before, own, after)):

            @pl.when((col >= i * blocks) & (col < (i + 1) * blocks))
            def _(i=i, part=part):
                place = pl.ds(pl.multiple_of((col - i * blocks) * tile, tile), tile)
                pltpu.make_async_copy(part.at[:, place], target(r), sems.at[r]).start()

        return carry

    def wait(r, carry):
        pltpu.make_async_copy(own.at[:, :tile], target(r), sems.at[r]).wait()
        return carry

    lax.fori_loop(0, blocks, start, 0)
    lax.fori_loop(0, blocks, wait, 0)


def gather(col, before, own, after, groups):
    rows, span = own.shape
    return pl.pallas_call(
        gather_kernel,
        in_specs=[SMEM] + [ANYWHERE] * 3,
        out_specs=ANYWHERE,
        out_shape=jax.ShapeDtypeStruct((groups, rows, span // groups), BF16),
        scratch_shapes=[pltpu.SemaphoreType.DMA((col.shape[0],))],
        compiler_params=whole_params(2),
        cost_estimate=pl.CostEstimate(flops=0, bytes_accessed=8 * MIB, transcendentals=0),
    )(col, before, own, after)


def scatter_kernel(
    col_ref, parts_hbm, before_hbm, own_hbm, after_hbm, parts_ref, acc, before, after, load_sem, sems
):
    tile = acc.shape[2]
    blocks = own_hbm.shape[0]
    per = parts_ref.shape[2] // tile
    load = pltpu.make_async_copy(parts_hbm, parts_ref, load_sem)
    load.start()

    def clear(i, carry):
        acc[i] = jnp.zeros(acc.shape[1:], F32)
        return carry

    lax.fori_loop(0, acc.shape[0], clear, 0, unroll=8)
    load.wait()

    def add(g, carry):
        for b in range(per):
            acc[col_ref[g * per + b]] += parts_ref[g, :, b * tile : (b + 1) * tile].astype(F32)
        return carry

    lax.fori_loop(0, parts_ref.shape[0], add, 0, unroll=2)
    copies = [
        pltpu.make_async_copy(acc.at[blocks : 2 * blocks], own_hbm, sems.at[0]),
        pltpu.make_async_copy(before, before_hbm, sems.at[1]),
        pltpu.make_async_copy(after, after_hbm, sems.at[2]),
    ]
    copies[0].start()
    for first, out, copy in ((0, before, copies[1]), (2 * blocks, after, copies[2])):

        def cast(i, carry, first=first, out=out):
            out[i] = acc[first + i].astype(BF16)
            return carry

        lax.fori_loop(0, blocks, cast, 0, unroll=8)
        copy.start()
    for copy in copies:
        copy.wait()


def scatter(col, parts):
    groups, rows, width = parts.shape
    blocks = col.shape[0]
    tile = groups * width // blocks
    shape = (blocks, rows, tile)
    return pl.pallas_call(
        scatter_kernel,
        in_specs=[SMEM, ANYWHERE],
        out_specs=[ANYWHERE] * 3,
        out_shape=[
            jax.ShapeDtypeStruct(shape, BF16),
            jax.ShapeDtypeStruct(shape, F32),
            jax.ShapeDtypeStruct(shape, BF16),
        ],
        scratch_shapes=[
            pltpu.VMEM(parts.shape, BF16),
            pltpu.VMEM((3 * blocks, rows, tile), F32),
            pltpu.VMEM(shape, BF16),
            pltpu.VMEM(shape, BF16),
            pltpu.SemaphoreType.DMA(()),
            pltpu.SemaphoreType.DMA((3,)),
        ],
        compiler_params=whole_params(SCATTER_MIB),
        cost_estimate=pl.CostEstimate(flops=0, bytes_accessed=8 * MIB, transcendentals=0),
    )(col, parts)


def self_kernel(chunk, w_self, x_ref, pre):
    for i in range(pre.shape[0] // chunk):
        rows = slice(i * chunk, (i + 1) * chunk)
        pre[rows, :] = dot(w_self[rows, :], x_ref[...])


def self_product(w_self, x_rows):
    size, width = x_rows.shape
    return pl.pallas_call(
        functools.partial(self_kernel, 256),
        in_specs=[VMEM] * 2,
        out_specs=VMEM,
        out_shape=jax.ShapeDtypeStruct((size, width), F32),
        compiler_params=whole_params(60),
        cost_estimate=pl.CostEstimate(
            flops=2 * size * size * width, bytes_accessed=5 * MIB, transcendentals=0
        ),
    )(w_self, x_rows)


def dense_kernel(chunk, *refs):
    core_ref, sources, targets, held = refs[0], refs[1:9], refs[9:16], refs[16:24]
    (agg_hbm, hidden_hbm, dpre_hbm, dagg_hbm, second_hbm, sent_hbm, kept_hbm) = targets
    (tiles, turned, x_ref, picked, w_neigh, pre_ref, cot_ref, w_back) = held
    (agg, hidden, dpre, dagg, second, sent, kept, in_sems, out_sems) = refs[24:]
    size = w_neigh.shape[0]
    pair = tiles.shape[-1]
    part = [slice(i, i + chunk) for i in range(0, size, chunk)]
    here = [slice(i, i + pair) for i in range(0, agg.shape[1], pair)]
    loads = [
        pltpu.make_async_copy(sources[k], held[k], in_sems.at[k]) for k in (0, 2, 3, 4, 5, 6, 7, 1)
    ]
    for copy in loads:
        copy.start()
    stores = []

    def store(k, src, dst, i):
        copy = pltpu.make_async_copy(src.at[part[i]], dst.at[part[i]], out_sems.at[k, i])
        copy.start()
        stores.append(copy)

    for copy in loads[:3]:
        copy.wait()
    for i in range(len(part)):
        for p in range(len(here)):
            total = dot(x_ref[part[i], here[p]], tiles[0, p])
            total = total + dot(picked[part[i], here[p]], tiles[1, p])
            agg[part[i], here[p]] = total.astype(BF16)
    for copy in loads[3:6]:
        copy.wait()
    for i in range(len(part)):
        store(0, agg, agg_hbm, i)
        pre = pre_ref[part[i], :] + dot(w_neigh[part[i], :], agg[...])
        sig = 0.5 + 0.5 * jnp.tanh(0.5 * pre)
        hidden[part[i], :] = (pre * sig).astype(BF16)
        slope = sig * (1.0 + pre * (1.0 - sig))
        dpre[part[i], :] = (cot_ref[part[i], :].astype(F32) * slope).astype(BF16)
    for copy in loads[6:]:
        copy.wait()
    for i in range(len(part)):
        store(1, hidden, hidden_hbm, i)
        store(2, dpre, dpre_hbm, i)
        dagg[part[i], :] = dot(w_back[part[i], :], dpre[...]).astype(BF16)
        for p in range(len(here)):
            second[part[i], here[p]] = dot(dagg[part[i], here[p]], turned[1, p]).astype(BF16)
        store(3, dagg, dagg_hbm, i)
        store(4, second, second_hbm, i)
    width = sent.shape[1]
    core = core_ref[0]
    for k, owner, out, target in ((5, 1 - core, sent, sent_hbm), (6, core, kept, kept_hbm)):
        half = agg.at[pl.ds(pl.multiple_of(owner * width, width), width)]
        for i in range(len(part)):
            out[part[i], :] = dot(dpre[part[i], :], half[...], NT).astype(BF16)
            store(k, out, target, i)
    for copy in stores:
        copy.wait()


def dense(core, tiles, turned, x_rows, picked, w_neigh, pre_self, cot, w_back):
    size, width = picked.shape
    chunk = CHUNK
    out = jax.ShapeDtypeStruct((size, width), BF16)
    args = (tiles, turned, x_rows, picked, w_neigh, pre_self, cot, w_back)
    return pl.pallas_call(
        functools.partial(dense_kernel, chunk),
        in_specs=[SMEM] + [ANYWHERE] * len(args),
        out_specs=[ANYWHERE] * 7,
        out_shape=[out] * 5 + [jax.ShapeDtypeStruct((size, size // CORES), BF16)] * 2,
        scratch_shapes=[pltpu.VMEM(arg.shape, arg.dtype) for arg in args]
        + [pltpu.VMEM((size, width), BF16)] * 5
        + [pltpu.VMEM((size, size // CORES), BF16)] * 2
        + [pltpu.SemaphoreType.DMA((len(args),)), pltpu.SemaphoreType.DMA((7, size // chunk))],
        compiler_params=whole_params(DENSE_MIB),
        cost_estimate=pl.CostEstimate(
            flops=4 * size * size * width, bytes_accessed=16 * MIB, transcendentals=size * width
        ),
    )(core, *args)


EXTRA = 8


def own_kernel(chunk, w_back, dpre, dagg_ref, turned, own):
    pair = turned.shape[-1]
    each = own.shape[1] - EXTRA
    for i in range(0, dpre.shape[0], chunk):
        rows = slice(i, i + chunk)
        dself = dot(w_back[rows, :], dpre[...])
        for p in range(own.shape[2] // pair):
            here = slice(p * pair, (p + 1) * pair)
            total = dself[:, here] + dot(dagg_ref[rows, here], turned[0, p])
            for g in range(chunk // each):
                own[i // each + g, :each, here] = total[g * each : (g + 1) * each].astype(BF16)


def own_part(w_back, dpre, dagg, turned, groups):
    size, width = dpre.shape
    return pl.pallas_call(
        functools.partial(own_kernel, 256),
        in_specs=[VMEM] * 4,
        out_specs=VMEM,
        out_shape=jax.ShapeDtypeStruct((groups, size // groups + EXTRA, width), BF16),
        compiler_params=whole_params(OWN_MIB),
        cost_estimate=pl.CostEstimate(
            flops=2 * size * size * width, bytes_accessed=5 * MIB, transcendentals=0
        ),
    )(w_back, dpre, dagg, turned)


def weight_kernel(me_ref, kept_ref, other_ref, *outs):
    rows = outs[0].shape[0]
    each = rows // SIDE
    for step, out in enumerate(outs):
        first = lax.rem(me_ref[0] + step, SIDE) * each
        for i in range(SIDE):
            there = pl.ds(pl.multiple_of(i * rows + first, each), each)
            total = kept_ref[there, :].astype(F32) + other_ref[there, :].astype(F32)
            out[i * each : (i + 1) * each, :] = total.astype(out.dtype)


def weight_pieces(me, kept, other):
    size, width = kept.shape
    shape = (size // SIDE, width)
    return pl.pallas_call(
        weight_kernel,
        in_specs=[SMEM] + [VMEM] * 2,
        out_specs=[VMEM] * SIDE,
        out_shape=[jax.ShapeDtypeStruct(shape, F32)]
        + [jax.ShapeDtypeStruct(shape, BF16)] * (SIDE - 1),
        compiler_params=whole_params(WEIGHT_MIB),
        cost_estimate=pl.CostEstimate(flops=0, bytes_accessed=4 * MIB, transcendentals=0),
    )(me[None], kept, other)


def add_kernel(index_ref, *refs):
    parts, outs = refs[:SIDE], refs[SIDE:]
    rows = outs[0].shape[0]
    for step, out in enumerate(outs):
        here = pl.ds(pl.multiple_of(lax.rem(index_ref[0] + step, SIDE) * rows, rows), rows)
        total = parts[0][here, :]
        for part in parts[1:]:
            total = total + part[here, :].astype(F32)
        out[...] = total.astype(out.dtype)


def added_pieces(me, parts):
    rows, width = parts[0].shape
    shape = (rows // SIDE, width)
    return pl.pallas_call(
        add_kernel,
        in_specs=[SMEM] + [VMEM] * SIDE,
        out_specs=[VMEM] * SIDE,
        out_shape=[jax.ShapeDtypeStruct(shape, F32)]
        + [jax.ShapeDtypeStruct(shape, BF16)] * (SIDE - 1),
        compiler_params=whole_params(WEIGHT_MIB),
        cost_estimate=pl.CostEstimate(flops=0, bytes_accessed=2 * MIB, transcendentals=0),
    )(me[None], *parts)


def base_kernel(spread_ref, own_ref, out_ref, weight_ref):
    rows, tile = spread_ref.shape[1:]
    width = own_ref.shape[2]
    per = width // tile
    count = weight_ref.shape[0]
    for b in range(spread_ref.shape[0]):
        part = own_ref[b // per, :rows, (b % per) * tile : (b % per + 1) * tile]
        out_ref[b] = spread_ref[b] + part.astype(F32)

    @pl.when(pl.program_id(0) == 0)
    def _():
        weight_ref[...] = jnp.zeros_like(weight_ref)

    for core in range(CORES):
        here = slice(core * width, (core + 1) * width)
        for group in range(core, own_ref.shape[0], CORES):
            terms = own_ref[group, rows:, :].astype(F32)
            weight_ref[:, here] += terms[:count] + terms[count:]


def based(spread, own):
    groups, high, width = own.shape
    blocks, rows, tile = spread.shape
    steps = 4
    part = pl.BlockSpec((blocks // steps, rows, tile), lambda g: (g, 0, 0))
    weight = ((high - rows) // 2, CORES * width)
    return pl.pallas_call(
        base_kernel,
        grid=(steps,),
        in_specs=[part, pl.BlockSpec((groups // steps, high, width), lambda g: (g, 0, 0))],
        out_specs=[part, pl.BlockSpec(weight, lambda g: (0, 0))],
        out_shape=[
            jax.ShapeDtypeStruct(spread.shape, F32),
            jax.ShapeDtypeStruct(weight, F32),
        ],
        compiler_params=params(FINAL_MIB),
    )(spread, own)


def final_kernel(
    base_ref, before_hbm, after_hbm, out_hbm, before_ref, after_ref, out_ref, in_sems, out_sems
):
    blocks, _, tile = base_ref.shape
    steps = out_sems.shape[0]
    each = blocks // steps
    loads, stores = [], []
    for i in range(steps):
        part = slice(i * each, (i + 1) * each)
        columns = slice(i * each * tile, (i + 1) * each * tile)
        loads.append(
            [
                pltpu.make_async_copy(before_hbm.at[part], before_ref.at[part], in_sems.at[0, i]),
                pltpu.make_async_copy(after_hbm.at[part], after_ref.at[part], in_sems.at[1, i]),
            ]
        )
        stores.append(
            pltpu.make_async_copy(out_ref.at[:, columns], out_hbm.at[:, columns], out_sems.at[i])
        )
        for copy in loads[i]:
            copy.start()
    for i in range(steps):
        for copy in loads[i]:
            copy.wait()
        for b in range(i * each, (i + 1) * each):
            total = base_ref[b] + before_ref[b].astype(F32) + after_ref[b].astype(F32)
            out_ref[:, b * tile : (b + 1) * tile] = total.astype(BF16)
        stores[i].start()
    for copy in stores:
        copy.wait()


def finish(base, before, after):
    blocks, rows, tile = base.shape
    steps = 4
    return pl.pallas_call(
        final_kernel,
        in_specs=[VMEM, ANYWHERE, ANYWHERE],
        out_specs=ANYWHERE,
        out_shape=jax.ShapeDtypeStruct((rows, blocks * tile), BF16),
        scratch_shapes=[
            pltpu.VMEM(before.shape, BF16),
            pltpu.VMEM(after.shape, BF16),
            pltpu.VMEM((rows, blocks * tile), BF16),
            pltpu.SemaphoreType.DMA((2, steps)),
            pltpu.SemaphoreType.DMA((steps,)),
        ],
        compiler_params=whole_params(FINAL_MIB),
    )(base, before, after)


def shifted(value, axis, steps):
    count = lax.axis_size(axis)
    first, last = max(0, -steps), min(count, count - steps)
    return lax.ppermute(value, axis, [(source, source + steps) for source in range(first, last)])


def exchange(value, axis):
    return lax.all_to_all(value, axis, split_axis=0, concat_axis=0, tiled=True)


SIDE = 4
CORES = 2


def sent_round(pieces, axis, partner):
    count = lax.axis_size(axis)
    return [pieces[0]] + [
        lax.ppermute(piece, axis, [(i, partner(i, step + 1)) for i in range(count)])
        for step, piece in enumerate(pieces[1:])
    ]


def weight_rows(sent, kept, groups, own_rows, spread):
    node = lax.axis_index("node")
    other = lax.ppermute(sent, "feat", [(i, i ^ 1) for i in range(groups)])
    pieces = weight_pieces(lax.rem(node, SIDE), kept, other)
    parts = sent_round(pieces, "node", lambda i, s: i // SIDE * SIDE + (i + s) % SIDE)
    parts, own_rows = lax.optimization_barrier((parts, own_rows))
    pieces = added_pieces(lax.div(node, SIDE), parts)
    parts = sent_round(pieces, "node", lambda i, s: (i + s * SIDE) % (SIDE * SIDE))
    parts, _ = lax.optimization_barrier((parts, spread))
    total = parts[0]
    for part in parts[1:]:
        total = total + part.astype(F32)
    total = total.reshape(groups, EXTRA // 2, -1)
    high = total.astype(BF16)
    low = (total - high.astype(F32)).astype(BF16)
    rows = jnp.concatenate([high, low], axis=1)
    return lax.dynamic_update_slice(own_rows, rows, (0, own_rows.shape[1] - EXTRA, 0))


def paired(tiles):
    blocks, tile, _ = tiles.shape
    tiles = tiles.reshape(blocks // 2, 2, tile, tile)
    empty = jnp.zeros_like(tiles[:, 0])
    upper = jnp.concatenate([tiles[:, 0], empty], axis=2)
    lower = jnp.concatenate([empty, tiles[:, 1]], axis=2)
    return jnp.concatenate([upper, lower], axis=1)


def local(features, tile_values, tile_cols, tile_count, w_self, w_neigh, cotangent):
    feat_dev, node_dev = features.shape
    tile = tile_values.shape[-1]
    block_count = node_dev // tile
    groups = lax.axis_size("feat")
    size = w_self.shape[0]
    part, feat = lax.axis_index("node"), lax.axis_index("feat")
    col = tile_cols[:, 1] - (part - 1) * block_count
    mine = block_count // groups
    live = lax.dynamic_slice_in_dim(tile_count, feat * mine, mine) > 1
    tiles = lax.dynamic_slice_in_dim(tile_values, feat * mine, mine)
    other = jnp.where(live[:, None, None], tiles[:, 1], jnp.zeros_like(tiles[:, 1]))
    straight = jnp.stack([paired(tiles[:, 0]), paired(other)])
    turned = straight.swapaxes(2, 3)

    before = shifted(features, "node", 1)
    behind = shifted(features, "node", -1)
    x_rows = exchange(split_columns(features, groups), "feat").reshape(size, -1)
    picked = exchange(gather(col, before, features, behind, groups), "feat").reshape(size, -1)
    x_rows, self_back, neigh_back, straight, turned = lax.optimization_barrier(
        (x_rows, w_self.T, w_neigh.T, straight, turned)
    )
    pre_self = self_product(w_self, x_rows)
    core = lax.rem(feat, CORES)
    _, hidden, dpre, dagg, second, sent, kept = dense(
        core[None], straight, turned, x_rows, picked, w_neigh, pre_self, cotangent, neigh_back
    )
    second_cols = exchange(second.reshape(groups, feat_dev, -1), "feat")
    own_rows = own_part(self_back, dpre, dagg, turned, groups)
    to_before, spread, to_after = scatter(col, second_cols)
    own_cols = exchange(weight_rows(sent, kept, groups, own_rows, spread), "feat")
    from_after = shifted(to_before, "node", -1)
    from_before = shifted(to_after, "node", 1)
    base, grad_w_neigh = based(spread, own_cols)
    grad_features = finish(base, from_before, from_after)
    return (hidden, grad_features, grad_w_neigh)


def solution(mesh):
    placed = (
        P("feat", "node"),
        P("node", None, None, None),
        P("node", None),
        P("node"),
        P(),
        P(),
        P(None, ("node", "feat")),
    )
    return jax.shard_map(
        local,
        mesh=mesh,
        in_specs=placed,
        out_specs=(P(None, ("node", "feat")), P("feat", "node"), P(("node", "feat"), None)),
        check_vma=False,
    )
```

```python
import functools

import jax
import jax.numpy as jnp
from jax import lax
from jax.experimental import pallas as pl
from jax.experimental.pallas import tpu as pltpu
from jax.sharding import PartitionSpec as P

F32 = jnp.float32
BF16 = jnp.bfloat16
NT = (((1,), (1,)), ((), ()))
NN = (((1,), (0,)), ((), ()))
MIB = 1 << 20
DENSE_MIB = 56
OWN_MIB = 60
WEIGHT_MIB = 8
FINAL_MIB = 16
SCATTER_MIB = 56
CHUNK = 512


def dot(a, b, dims=NN):
    return lax.dot_general(a, b, dims, preferred_element_type=F32)


def whole_params(mib):
    return pltpu.CompilerParams(vmem_limit_bytes=mib * MIB)


def params(mib):
    return pltpu.CompilerParams(
        dimension_semantics=("arbitrary",), vmem_limit_bytes=mib * MIB
    )


def split_kernel(x_hbm, out_hbm, held, in_sems, out_sems):
    width = out_hbm.shape[2]
    groups = range(out_hbm.shape[0])
    loads = [
        pltpu.make_async_copy(x_hbm.at[:, g * width : (g + 1) * width], held.at[g], in_sems.at[g])
        for g in groups
    ]
    stores = [pltpu.make_async_copy(held.at[g], out_hbm.at[g], out_sems.at[g]) for g in groups]
    for copy in loads:
        copy.start()
    for load, store in zip(loads, stores):
        load.wait()
        store.start()
    for copy in stores:
        copy.wait()


ANYWHERE = pl.BlockSpec(memory_space=pl.ANY)
SMEM = pl.BlockSpec(memory_space=pltpu.SMEM)
VMEM = pl.BlockSpec(memory_space=pltpu.VMEM)


def split_columns(x, groups):
    rows, columns = x.shape
    return pl.pallas_call(
        split_kernel,
        in_specs=[ANYWHERE],
        out_specs=ANYWHERE,
        out_shape=jax.ShapeDtypeStruct((groups, rows, columns // groups), x.dtype),
        scratch_shapes=[
            pltpu.VMEM((groups, rows, columns // groups), x.dtype),
            pltpu.SemaphoreType.DMA((groups,)),
            pltpu.SemaphoreType.DMA((groups,)),
        ],
        compiler_params=whole_params(60),
    )(x)


def gather_kernel(col_ref, before, own, after, out_hbm, sems):
    tile = 128
    blocks = own.shape[1] // tile
    per = out_hbm.shape[2] // tile

    def target(r):
        place = pl.ds(pl.multiple_of(lax.rem(r, per) * tile, tile), tile)
        return out_hbm.at[lax.div(r, per), :, place]

    def start(r, carry):
        col = col_ref[r]
        for i, part in enumerate((before, own, after)):

            @pl.when((col >= i * blocks) & (col < (i + 1) * blocks))
            def _(i=i, part=part):
                place = pl.ds(pl.multiple_of((col - i * blocks) * tile, tile), tile)
                pltpu.make_async_copy(part.at[:, place], target(r), sems.at[r]).start()

        return carry

    def wait(r, carry):
        pltpu.make_async_copy(own.at[:, :tile], target(r), sems.at[r]).wait()
        return carry

    lax.fori_loop(0, blocks, start, 0)
    lax.fori_loop(0, blocks, wait, 0)


def gather(col, before, own, after, groups):
    rows, span = own.shape
    return pl.pallas_call(
        gather_kernel,
        in_specs=[SMEM] + [ANYWHERE] * 3,
        out_specs=ANYWHERE,
        out_shape=jax.ShapeDtypeStruct((groups, rows, span // groups), BF16),
        scratch_shapes=[pltpu.SemaphoreType.DMA((col.shape[0],))],
        compiler_params=whole_params(2),
        cost_estimate=pl.CostEstimate(flops=0, bytes_accessed=8 * MIB, transcendentals=0),
    )(col, before, own, after)


def scatter_kernel(
    col_ref, parts_hbm, before_hbm, own_hbm, after_hbm, parts_ref, acc, before, after, load_sem, sems
):
    tile = acc.shape[2]
    blocks = own_hbm.shape[0]
    per = parts_ref.shape[2] // tile
    load = pltpu.make_async_copy(parts_hbm, parts_ref, load_sem)
    load.start()

    def clear(i, carry):
        acc[i] = jnp.zeros(acc.shape[1:], F32)
        return carry

    lax.fori_loop(0, acc.shape[0], clear, 0, unroll=8)
    load.wait()

    def add(g, carry):
        for b in range(per):
            acc[col_ref[g * per + b]] += parts_ref[g, :, b * tile : (b + 1) * tile].astype(F32)
        return carry

    lax.fori_loop(0, parts_ref.shape[0], add, 0, unroll=2)
    copies = [
        pltpu.make_async_copy(acc.at[blocks : 2 * blocks], own_hbm, sems.at[0]),
        pltpu.make_async_copy(before, before_hbm, sems.at[1]),
        pltpu.make_async_copy(after, after_hbm, sems.at[2]),
    ]
    copies[0].start()
    for first, out, copy in ((0, before, copies[1]), (2 * blocks, after, copies[2])):

        def cast(i, carry, first=first, out=out):
            out[i] = acc[first + i].astype(BF16)
            return carry

        lax.fori_loop(0, blocks, cast, 0, unroll=8)
        copy.start()
    for copy in copies:
        copy.wait()


def scatter(col, parts):
    groups, rows, width = parts.shape
    blocks = col.shape[0]
    tile = groups * width // blocks
    shape = (blocks, rows, tile)
    return pl.pallas_call(
        scatter_kernel,
        in_specs=[SMEM, ANYWHERE],
        out_specs=[ANYWHERE] * 3,
        out_shape=[
            jax.ShapeDtypeStruct(shape, BF16),
            jax.ShapeDtypeStruct(shape, F32),
            jax.ShapeDtypeStruct(shape, BF16),
        ],
        scratch_shapes=[
            pltpu.VMEM(parts.shape, BF16),
            pltpu.VMEM((3 * blocks, rows, tile), F32),
            pltpu.VMEM(shape, BF16),
            pltpu.VMEM(shape, BF16),
            pltpu.SemaphoreType.DMA(()),
            pltpu.SemaphoreType.DMA((3,)),
        ],
        compiler_params=whole_params(SCATTER_MIB),
        cost_estimate=pl.CostEstimate(flops=0, bytes_accessed=8 * MIB, transcendentals=0),
    )(col, parts)


def self_kernel(chunk, w_self, x_ref, pre):
    for i in range(pre.shape[0] // chunk):
        rows = slice(i * chunk, (i + 1) * chunk)
        pre[rows, :] = dot(w_self[rows, :], x_ref[...])


def self_product(w_self, x_rows):
    size, width = x_rows.shape
    return pl.pallas_call(
        functools.partial(self_kernel, 256),
        in_specs=[VMEM] * 2,
        out_specs=VMEM,
        out_shape=jax.ShapeDtypeStruct((size, width), F32),
        compiler_params=whole_params(60),
        cost_estimate=pl.CostEstimate(
            flops=2 * size * size * width, bytes_accessed=5 * MIB, transcendentals=0
        ),
    )(w_self, x_rows)


def dense_kernel(chunk, *refs):
    core_ref, sources, targets, held = refs[0], refs[1:9], refs[9:15], refs[15:23]
    (hidden_hbm, dpre_hbm, dagg_hbm, second_hbm, sent_hbm, kept_hbm) = targets
    (tiles, turned, x_ref, picked, w_neigh, pre_ref, cot_ref, w_back) = held
    (agg, hidden, dpre, dagg, second, sent, kept, in_sems, out_sems) = refs[23:]
    size = w_neigh.shape[0]
    pair = tiles.shape[-1]
    part = [slice(i, i + chunk) for i in range(0, size, chunk)]
    here = [slice(i, i + pair) for i in range(0, agg.shape[1], pair)]
    loads = [
        pltpu.make_async_copy(sources[k], held[k], in_sems.at[k]) for k in (0, 2, 3, 4, 5, 6, 7, 1)
    ]
    for copy in loads[:6]:
        copy.start()
    stores = []

    def store(k, src, dst, i):
        copy = pltpu.make_async_copy(src.at[part[i]], dst.at[part[i]], out_sems.at[k, i])
        copy.start()
        stores.append(copy)

    for copy in loads[:3]:
        copy.wait()
    for copy in loads[6:]:
        copy.start()
    for i in range(len(part)):
        for p in range(len(here)):
            total = dot(x_ref[part[i], here[p]], tiles[0, p])
            total = total + dot(picked[part[i], here[p]], tiles[1, p])
            agg[part[i], here[p]] = total.astype(BF16)
    for copy in loads[3:6]:
        copy.wait()
    for i in range(len(part)):
        pre = pre_ref[part[i], :] + dot(w_neigh[part[i], :], agg[...])
        sig = 0.5 + 0.5 * jnp.tanh(0.5 * pre)
        hidden[part[i], :] = (pre * sig).astype(BF16)
        slope = sig * (1.0 + pre * (1.0 - sig))
        dpre[part[i], :] = (cot_ref[part[i], :].astype(F32) * slope).astype(BF16)
    for copy in loads[6:]:
        copy.wait()
    for i in range(len(part)):
        store(1, hidden, hidden_hbm, i)
        store(2, dpre, dpre_hbm, i)
        dagg[part[i], :] = dot(w_back[part[i], :], dpre[...]).astype(BF16)
        for p in range(len(here)):
            second[part[i], here[p]] = dot(dagg[part[i], here[p]], turned[1, p]).astype(BF16)
        store(3, dagg, dagg_hbm, i)
        store(4, second, second_hbm, i)
    width = sent.shape[1]
    core = core_ref[0]
    for k, owner, out, target in ((5, 1 - core, sent, sent_hbm), (6, core, kept, kept_hbm)):
        half = agg.at[pl.ds(pl.multiple_of(owner * width, width), width)]
        for i in range(len(part)):
            out[part[i], :] = dot(dpre[part[i], :], half[...], NT).astype(BF16)
            store(k, out, target, i)
    for copy in stores:
        copy.wait()


def dense(core, tiles, turned, x_rows, picked, w_neigh, pre_self, cot, w_back):
    size, width = picked.shape
    chunk = CHUNK
    out = jax.ShapeDtypeStruct((size, width), BF16)
    args = (tiles, turned, x_rows, picked, w_neigh, pre_self, cot, w_back)
    return pl.pallas_call(
        functools.partial(dense_kernel, chunk),
        in_specs=[SMEM] + [ANYWHERE] * len(args),
        out_specs=[ANYWHERE] * 6,
        out_shape=[out] * 4 + [jax.ShapeDtypeStruct((size, size // CORES), BF16)] * 2,
        scratch_shapes=[pltpu.VMEM(arg.shape, arg.dtype) for arg in args]
        + [pltpu.VMEM((size, width), BF16)] * 5
        + [pltpu.VMEM((size, size // CORES), BF16)] * 2
        + [pltpu.SemaphoreType.DMA((len(args),)), pltpu.SemaphoreType.DMA((7, size // chunk))],
        compiler_params=whole_params(DENSE_MIB),
        cost_estimate=pl.CostEstimate(
            flops=4 * size * size * width, bytes_accessed=16 * MIB, transcendentals=size * width
        ),
    )(core, *args)


EXTRA = 8


def own_kernel(chunk, w_back, dpre, dagg_ref, turned, own):
    pair = turned.shape[-1]
    each = own.shape[1] - EXTRA
    for i in range(0, dpre.shape[0], chunk):
        rows = slice(i, i + chunk)
        dself = dot(w_back[rows, :], dpre[...])
        for p in range(own.shape[2] // pair):
            here = slice(p * pair, (p + 1) * pair)
            total = dself[:, here] + dot(dagg_ref[rows, here], turned[0, p])
            for g in range(chunk // each):
                own[i // each + g, :each, here] = total[g * each : (g + 1) * each].astype(BF16)


def own_part(w_back, dpre, dagg, turned, groups):
    size, width = dpre.shape
    return pl.pallas_call(
        functools.partial(own_kernel, 256),
        in_specs=[VMEM] * 4,
        out_specs=VMEM,
        out_shape=jax.ShapeDtypeStruct((groups, size // groups + EXTRA, width), BF16),
        compiler_params=whole_params(OWN_MIB),
        cost_estimate=pl.CostEstimate(
            flops=2 * size * size * width, bytes_accessed=5 * MIB, transcendentals=0
        ),
    )(w_back, dpre, dagg, turned)


def weight_kernel(me_ref, kept_ref, other_ref, *outs):
    rows = outs[0].shape[0]
    each = rows // SIDE
    for step, out in enumerate(outs):
        first = lax.rem(me_ref[0] + step, SIDE) * each
        for i in range(SIDE):
            there = pl.ds(pl.multiple_of(i * rows + first, each), each)
            total = kept_ref[there, :].astype(F32) + other_ref[there, :].astype(F32)
            out[i * each : (i + 1) * each, :] = total.astype(out.dtype)


def weight_pieces(me, kept, other):
    size, width = kept.shape
    shape = (size // SIDE, width)
    return pl.pallas_call(
        weight_kernel,
        in_specs=[SMEM] + [VMEM] * 2,
        out_specs=[VMEM] * SIDE,
        out_shape=[jax.ShapeDtypeStruct(shape, F32)]
        + [jax.ShapeDtypeStruct(shape, BF16)] * (SIDE - 1),
        compiler_params=whole_params(WEIGHT_MIB),
        cost_estimate=pl.CostEstimate(flops=0, bytes_accessed=4 * MIB, transcendentals=0),
    )(me[None], kept, other)


def add_kernel(index_ref, *refs):
    parts, outs = refs[:SIDE], refs[SIDE:]
    rows = outs[0].shape[0]
    for step, out in enumerate(outs):
        here = pl.ds(pl.multiple_of(lax.rem(index_ref[0] + step, SIDE) * rows, rows), rows)
        total = parts[0][here, :]
        for part in parts[1:]:
            total = total + part[here, :].astype(F32)
        out[...] = total.astype(out.dtype)


def added_pieces(me, parts):
    rows, width = parts[0].shape
    shape = (rows // SIDE, width)
    return pl.pallas_call(
        add_kernel,
        in_specs=[SMEM] + [VMEM] * SIDE,
        out_specs=[VMEM] * SIDE,
        out_shape=[jax.ShapeDtypeStruct(shape, F32)]
        + [jax.ShapeDtypeStruct(shape, BF16)] * (SIDE - 1),
        compiler_params=whole_params(WEIGHT_MIB),
        cost_estimate=pl.CostEstimate(flops=0, bytes_accessed=2 * MIB, transcendentals=0),
    )(me[None], *parts)


def base_kernel(spread_ref, own_ref, out_ref, weight_ref):
    rows, tile = spread_ref.shape[1:]
    width = own_ref.shape[2]
    per = width // tile
    count = weight_ref.shape[0]
    for b in range(spread_ref.shape[0]):
        part = own_ref[b // per, :rows, (b % per) * tile : (b % per + 1) * tile]
        out_ref[b] = spread_ref[b] + part.astype(F32)

    @pl.when(pl.program_id(0) == 0)
    def _():
        weight_ref[...] = jnp.zeros_like(weight_ref)

    for core in range(CORES):
        here = slice(core * width, (core + 1) * width)
        for group in range(core, own_ref.shape[0], CORES):
            terms = own_ref[group, rows:, :].astype(F32)
            weight_ref[:, here] += terms[:count] + terms[count:]


def based(spread, own):
    groups, high, width = own.shape
    blocks, rows, tile = spread.shape
    steps = 4
    part = pl.BlockSpec((blocks // steps, rows, tile), lambda g: (g, 0, 0))
    weight = ((high - rows) // 2, CORES * width)
    return pl.pallas_call(
        base_kernel,
        grid=(steps,),
        in_specs=[part, pl.BlockSpec((groups // steps, high, width), lambda g: (g, 0, 0))],
        out_specs=[part, pl.BlockSpec(weight, lambda g: (0, 0))],
        out_shape=[
            jax.ShapeDtypeStruct(spread.shape, F32),
            jax.ShapeDtypeStruct(weight, F32),
        ],
        compiler_params=params(FINAL_MIB),
    )(spread, own)


def final_kernel(
    base_ref, before_hbm, after_hbm, out_hbm, before_ref, after_ref, out_ref, in_sems, out_sems
):
    blocks, _, tile = base_ref.shape
    steps = out_sems.shape[0]
    each = blocks // steps
    loads, stores = [], []
    for i in range(steps):
        part = slice(i * each, (i + 1) * each)
        columns = slice(i * each * tile, (i + 1) * each * tile)
        loads.append(
            [
                pltpu.make_async_copy(before_hbm.at[part], before_ref.at[part], in_sems.at[0, i]),
                pltpu.make_async_copy(after_hbm.at[part], after_ref.at[part], in_sems.at[1, i]),
            ]
        )
        stores.append(
            pltpu.make_async_copy(out_ref.at[:, columns], out_hbm.at[:, columns], out_sems.at[i])
        )
        for copy in loads[i]:
            copy.start()
    for i in range(steps):
        for copy in loads[i]:
            copy.wait()
        for b in range(i * each, (i + 1) * each):
            total = base_ref[b] + before_ref[b].astype(F32) + after_ref[b].astype(F32)
            out_ref[:, b * tile : (b + 1) * tile] = total.astype(BF16)
        stores[i].start()
    for copy in stores:
        copy.wait()


def finish(base, before, after):
    blocks, rows, tile = base.shape
    steps = 4
    return pl.pallas_call(
        final_kernel,
        in_specs=[VMEM, ANYWHERE, ANYWHERE],
        out_specs=ANYWHERE,
        out_shape=jax.ShapeDtypeStruct((rows, blocks * tile), BF16),
        scratch_shapes=[
            pltpu.VMEM(before.shape, BF16),
            pltpu.VMEM(after.shape, BF16),
            pltpu.VMEM((rows, blocks * tile), BF16),
            pltpu.SemaphoreType.DMA((2, steps)),
            pltpu.SemaphoreType.DMA((steps,)),
        ],
        compiler_params=whole_params(FINAL_MIB),
    )(base, before, after)


def shifted(value, axis, steps):
    count = lax.axis_size(axis)
    first, last = max(0, -steps), min(count, count - steps)
    return lax.ppermute(value, axis, [(source, source + steps) for source in range(first, last)])


def exchange(value, axis):
    return lax.all_to_all(value, axis, split_axis=0, concat_axis=0, tiled=True)


SIDE = 4
CORES = 2


def sent_round(pieces, axis, partner):
    count = lax.axis_size(axis)
    return [pieces[0]] + [
        lax.ppermute(piece, axis, [(i, partner(i, step + 1)) for i in range(count)])
        for step, piece in enumerate(pieces[1:])
    ]


def weight_rows(sent, kept, groups, own_rows, spread):
    node = lax.axis_index("node")
    other = lax.ppermute(sent, "feat", [(i, i ^ 1) for i in range(groups)])
    pieces = weight_pieces(lax.rem(node, SIDE), kept, other)
    parts = sent_round(pieces, "node", lambda i, s: i // SIDE * SIDE + (i + s) % SIDE)
    parts, own_rows = lax.optimization_barrier((parts, own_rows))
    pieces = added_pieces(lax.div(node, SIDE), parts)
    parts = sent_round(pieces, "node", lambda i, s: (i + s * SIDE) % (SIDE * SIDE))
    parts, _ = lax.optimization_barrier((parts, spread))
    total = parts[0]
    for part in parts[1:]:
        total = total + part.astype(F32)
    total = total.reshape(groups, EXTRA // 2, -1)
    high = total.astype(BF16)
    low = (total - high.astype(F32)).astype(BF16)
    rows = jnp.concatenate([high, low], axis=1)
    return lax.dynamic_update_slice(own_rows, rows, (0, own_rows.shape[1] - EXTRA, 0))


def paired(tiles):
    blocks, tile, _ = tiles.shape
    tiles = tiles.reshape(blocks // 2, 2, tile, tile)
    empty = jnp.zeros_like(tiles[:, 0])
    upper = jnp.concatenate([tiles[:, 0], empty], axis=2)
    lower = jnp.concatenate([empty, tiles[:, 1]], axis=2)
    return jnp.concatenate([upper, lower], axis=1)


def local(features, tile_values, tile_cols, tile_count, w_self, w_neigh, cotangent):
    feat_dev, node_dev = features.shape
    tile = tile_values.shape[-1]
    block_count = node_dev // tile
    groups = lax.axis_size("feat")
    size = w_self.shape[0]
    part, feat = lax.axis_index("node"), lax.axis_index("feat")
    col = tile_cols[:, 1] - (part - 1) * block_count
    mine = block_count // groups
    live = lax.dynamic_slice_in_dim(tile_count, feat * mine, mine) > 1
    tiles = lax.dynamic_slice_in_dim(tile_values, feat * mine, mine)
    other = jnp.where(live[:, None, None], tiles[:, 1], jnp.zeros_like(tiles[:, 1]))
    straight = jnp.stack([paired(tiles[:, 0]), paired(other)])
    turned = straight.swapaxes(2, 3)

    before = shifted(features, "node", 1)
    behind = shifted(features, "node", -1)
    x_rows = exchange(split_columns(features, groups), "feat").reshape(size, -1)
    picked = exchange(gather(col, before, features, behind, groups), "feat").reshape(size, -1)
    x_rows, self_back, neigh_back, straight, turned = lax.optimization_barrier(
        (x_rows, w_self.T, w_neigh.T, straight, turned)
    )
    pre_self = self_product(w_self, x_rows)
    core = lax.rem(feat, CORES)
    hidden, dpre, dagg, second, sent, kept = dense(
        core[None], straight, turned, x_rows, picked, w_neigh, pre_self, cotangent, neigh_back
    )
    second_cols = exchange(second.reshape(groups, feat_dev, -1), "feat")
    own_rows = own_part(self_back, dpre, dagg, turned, groups)
    to_before, spread, to_after = scatter(col, second_cols)
    own_cols = exchange(weight_rows(sent, kept, groups, own_rows, spread), "feat")
    from_after = shifted(to_before, "node", -1)
    from_before = shifted(to_after, "node", 1)
    base, grad_w_neigh = based(spread, own_cols)
    grad_features = finish(base, from_before, from_after)
    return (hidden, grad_features, grad_w_neigh)


def solution(mesh):
    placed = (
        P("feat", "node"),
        P("node", None, None, None),
        P("node", None),
        P("node"),
        P(),
        P(),
        P(None, ("node", "feat")),
    )
    return jax.shard_map(
        local,
        mesh=mesh,
        in_specs=placed,
        out_specs=(P(None, ("node", "feat")), P("feat", "node"), P(("node", "feat"), None)),
        check_vma=False,
    )
```
